128 devices in a mesh: dp: 8 (over y, core), mp: 16 (over z, x).
Axes of the slice: x: 4, y: 4, z: 4, core: 2. Of those that a mesh axis runs over, the one named last changes fastest.
Arguments:
- hidden_acts: bfloat16 [4096, 16384], P('dp', 'mp'), may hold values from -25 to 25
- out_grad: bfloat16 [4096, 8192], P('dp'), may hold values from -25 to 25
- owners: int32 [8, 16, 8], P('dp', 'mp'), may hold values from 0 to 15, as said below
Outputs:
- preconds: bfloat16 [8, 16, 12, 512, 512], P('dp', 'mp')
The draws below stay inside these ranges and needn't reach their ends.
Inputs may be any that keep to these rules, and one draw needn't show every extreme that they name: owners[r, c, j] names the mp index that owns statistic j of device (r, c). One device sends at most 2 statistics to one owner, and one owner receives at most 12 statistics of its dp index; both bounds are reached in every dp index.
All inputs are finite; a program needn't handle non-finite values.
Results may differ from the reference program's by a relative error of at most 0.013.
Values may be sent and summed in bfloat16 or wider, within the bound.
A program may use at most 128 MiB of HBM per device.

```python
import jax
import jax.numpy as jnp
from jax import lax

BLK = 512
TOK_DEV = 512
ITERS = 2
STATS = 8
MOST = 12
TOKENS = 4096
DW = 8192
FFW = 16384
N_DP = 8
N_MP = 16


def scaled_field(noise_field, key, spread):
    width = noise_field.shape[1]
    key_scale = jax.random.fold_in(key, 0)
    column_scale = jnp.exp(jax.random.uniform(key_scale, (width,), jnp.float32, -0.5, 0.5) * jnp.log(spread))
    values = column_scale[None, :] * noise_field
    return values.astype(jnp.bfloat16)


def draw_hidden_acts(key, part):
    key = jax.random.fold_in(key, 3)
    key_noise, key_field = jax.random.split(key)
    noise_field = jnp.clip(jax.random.normal(key_noise, (TOKENS, FFW), jnp.float32), -5.0, 5.0)
    return scaled_field(noise_field, key_field, 16.0)


def draw_out_grad(key, part):
    key = jax.random.fold_in(key, 5)
    key_noise, key_field = jax.random.split(key)
    noise_field = jnp.clip(jax.random.normal(key_noise, (TOKENS, DW), jnp.float32), -5.0, 5.0)
    return scaled_field(noise_field, key_field, 16.0)


def draw_owners(key, part):
    key = jax.random.fold_in(key, 11)
    sender = jnp.arange(N_MP, dtype=jnp.int32)[:, None]
    target = jnp.arange(N_MP, dtype=jnp.int32)[None, :]
    base = ((target - sender) % N_MP < STATS).astype(jnp.int32)
    paired = target < 2 * (N_MP // 4)
    heavy = paired & (target % 2 == 0) & ((target - sender) % N_MP < 4)
    light = paired & (target % 2 == 1) & ((target - 1 - sender) % N_MP < 4)
    counts = base + heavy.astype(jnp.int32) - light.astype(jnp.int32)
    running = jnp.cumsum(counts, axis=1)
    slots = jnp.arange(STATS, dtype=jnp.int32)
    owner_base = jnp.sum((running[:, None, :] <= slots[None, :, None]).astype(jnp.int32), axis=2)

    def one_row(row_key):
        key_a, key_b, key_c = jax.random.split(row_key, 3)
        relabel = jax.random.permutation(key_a, N_MP).astype(jnp.int32)
        placing = jax.random.permutation(key_b, N_MP).astype(jnp.int32)
        lists = relabel[owner_base]
        shuffles = jax.vmap(lambda each: jax.random.permutation(each, STATS))(jax.random.split(key_c, N_MP))
        lists = jnp.take_along_axis(lists, shuffles.astype(jnp.int32), axis=1)
        return lists[jnp.argsort(placing)]
    return jax.vmap(one_row)(jax.random.split(key, N_DP)).astype(jnp.int32)


def setup_inputs(seed: int = 0) -> dict:
    keys = jax.random.split(jax.random.key(seed), 4)
    hidden_acts = draw_hidden_acts(jax.random.fold_in(keys[3], 71), 0)
    out_grad = draw_out_grad(jax.random.fold_in(keys[3], 71), 0)
    owners = draw_owners(jax.random.fold_in(keys[3], 71), 0)
    return {"hidden_acts": hidden_acts, "out_grad": out_grad, "owners": owners}


stretch = 4.0

def rounded(value):
    return lax.optimization_barrier(value.astype(jnp.bfloat16)).astype(jnp.float32)

def batch_product(left, right):
    return jnp.einsum('nij,njk->nik', left, right)

def newton_root(stats):
    order = stats.shape[-1]
    symmetric = lax.optimization_barrier(stats).astype(jnp.float32)
    unit_diag = jnp.eye(order, dtype=jnp.float32)
    mean_diag = lax.optimization_barrier(jnp.sum(symmetric * unit_diag, axis=(1, 2))) / order
    damped = symmetric + 0.1 * mean_diag[:, None, None] * unit_diag
    frobenius = jnp.sqrt(lax.optimization_barrier(jnp.sum(damped * damped, axis=(1, 2))) + 1e-06)
    coupled = stretch * damped / frobenius[:, None, None]
    inv_root = jnp.sqrt(jnp.sqrt(stretch / frobenius))
    precond = coupled
    for step_num in range(ITERS):
        factor = (5.0 * unit_diag - coupled) * 0.25
        if step_num == 0:
            precond = inv_root[:, None, None] * factor
        else:
            precond = batch_product(rounded(precond), rounded(factor))
        if step_num + 1 < ITERS:
            factor_b = rounded(factor)
            square = batch_product(factor_b, factor_b)
            fourth = batch_product(rounded(square), rounded(square))
            coupled = batch_product(rounded(fourth), rounded(coupled))
    restore = jnp.sqrt(jnp.sqrt(1.1 * mean_diag))
    return (precond * restore[:, None, None]).astype(jnp.bfloat16)

def reference(hidden_acts, out_grad, owners):
    acts = hidden_acts.reshape(N_DP, TOK_DEV, FFW)
    cots = out_grad.reshape(N_DP, TOK_DEV, DW)

    def add_part(total, pair):
        part = jnp.dot(pair[0].T, pair[1], preferred_element_type=jnp.float32)
        return (total + part.astype(jnp.bfloat16).astype(jnp.float32), None)
    grad, _ = lax.scan(add_part, jnp.zeros((FFW, DW), jnp.float32), (acts, cots))
    blocks = grad.astype(jnp.bfloat16).reshape(N_MP, 2, BLK, N_DP, 2, BLK)
    flat_count = N_MP * STATS
    positions = jnp.arange(flat_count, dtype=jnp.int32)
    outs = []
    for row in range(N_DP):
        local = blocks[:, :, :, row].astype(jnp.float32)
        left = jnp.einsum('bpfqd,bpgqd->bpqfg', local, local).astype(jnp.bfloat16)
        right = jnp.einsum('bpfqd,bpfqe->bpqde', local, local).astype(jnp.bfloat16)
        stats = jnp.stack([left, right], axis=3).reshape(flat_count, BLK, BLK)
        results = lax.map(lambda one: newton_root(one[None])[0], stats)
        flat = owners[row].reshape(-1)
        match = (flat[None, :] == jnp.arange(N_MP, dtype=jnp.int32)[:, None]).astype(jnp.int32)
        rank = jnp.cumsum(match, axis=1) - match
        select = (match[:, None, :] > 0) & (rank[:, None, :] == jnp.arange(MOST, dtype=jnp.int32)[None, :, None])
        index = lax.optimization_barrier(jnp.sum(select.astype(jnp.int32) * positions, axis=2))
        filled = jnp.any(select, axis=2)
        picked = results[index]
        outs.append(jnp.where(filled[:, :, None, None], picked, jnp.zeros_like(picked)))
    return jnp.stack(outs, axis=0)
```

```python
import functools

import jax
import jax.numpy as jnp
import numpy as np
from jax import lax
from jax.experimental import pallas as pl
from jax.experimental.pallas import tpu as pltpu
from jax.sharding import PartitionSpec as P

MESH = pl.DeviceIdType.MESH
BLK = 512
STATS = 8
CAP = 2
MOST = 12
ROWS = 1280
STEPS_MAX = 10
STEPS_FEW = 8
TABLE = 4 * STEPS_MAX + MOST + 4
LIMIT = 56 * 1024 * 1024


def gather_kernel(hid, og, hid_all, og_all, ss, rs, ls, rs1):
    r, c = lax.axis_index("dp"), lax.axis_index("mp")
    y, k = r // 2, r % 2
    z, x = c // 4, c % 4
    sib = (2 * y + 1 - k, c)

    def yn(dy, core):
        return (2 * ((y + dy) % 4) + core, c)

    a = z * (1 - k) + x * k
    b = x * (1 - k) + z * k

    def plane(aa, bb):
        zz = aa * (1 - k) + bb * k
        xx = bb * (1 - k) + aa * k
        return (r, zz * 4 + xx)

    bp, bm = plane(a, (b + 1) % 4), plane(a, (b + 3) % 4)
    ap, am = plane((a + 1) % 4, b), plane((a + 3) % 4, b)

    barrier = pltpu.get_barrier_semaphore()
    partners = [sib] + [yn(dy, core) for dy in (1, 2, 3) for core in (0, 1)] + [bp, bm, ap, am]
    for dev in partners:
        pl.semaphore_signal(barrier, inc=1, device_id=dev, device_id_type=MESH)
    pl.semaphore_wait(barrier, len(partners))

    sent = []

    def send(src, dst, dev, landed=None):
        i = len(sent)
        landed = rs.at[i] if landed is None else landed
        copy = pltpu.make_async_remote_copy(
            src_ref=src, dst_ref=dst, send_sem=ss.at[i], recv_sem=landed, device_id=dev, device_id_type=MESH
        )
        copy.start()
        sent.append(copy)
        return copy

    for dy in (1, 3, 2):
        for core in (0, 1):
            aa = z * (1 - core) + x * core
            bb = x * (1 - core) + z * core
            rr = 2 * ((y + dy) % 4) + core
            cols = pl.ds(pl.multiple_of(rr * 1024, 1024), 1024)
            send(og.at[aa, bb, :, cols], og_all.at[4 - dy, k, aa, bb], yn(dy, core), rs1.at[4 - dy, k])
    hp, hm = {}, {}
    for h in (0, 1):
        hp[h] = send(hid.at[h], hid_all.at[3, k, h], yn(1, k))
        hm[1 - h] = send(hid.at[1 - h], hid_all.at[1, k, 1 - h], yn(3, k))
    rr = 2 * y + 1 - k
    sib_og = send(og.at[:, :, :, pl.ds(pl.multiple_of(rr * 1024, 1024), 1024)], og_all.at[0, k], sib)
    sib_hid = send(hid, hid_all.at[0, k], sib)
    l0 = pltpu.make_async_copy(og.at[:, :, :, pl.ds(pl.multiple_of(r * 1024, 1024), 1024)], og_all.at[0, k], ls.at[0])
    l1 = pltpu.make_async_copy(hid, hid_all.at[0, k], ls.at[1])
    l0.start()
    l1.start()

    order = (1, 3, 2)
    sa, sb, ra, rb = {}, {}, {}, {}
    for d in order:
        for core in (0, 1):
            here = og_all.at[d, core, a, b]
            pltpu.make_async_copy(here, here, rs1.at[d, core]).wait()
        sa[d, 0] = send(og_all.at[d, :, a, b], og_all.at[d, :, a, b], bp)
        sa[d, 1] = send(og_all.at[d, :, a, b], og_all.at[d, :, a, b], bm)
    for d in order:
        sa[d, 0].wait_recv()
        ra[d, 0] = send(og_all.at[d, 0, a, (b + 3) % 4], og_all.at[d, 0, a, (b + 3) % 4], bp)
        sa[d, 1].wait_recv()
        ra[d, 1] = send(og_all.at[d, 1, a, (b + 1) % 4], og_all.at[d, 1, a, (b + 1) % 4], bm)
    for d in order:
        ra[d, 0].wait_recv()
        ra[d, 1].wait_recv()
        sb[d, 0] = send(og_all.at[d, :, a], og_all.at[d, :, a], ap)
        sb[d, 1] = send(og_all.at[d, :, a], og_all.at[d, :, a], am)

    forwards = []

    def forward(d, h):
        forwards.append(send(hid_all.at[d, k, h], hid_all.at[d, k, h], sib))

    def relay_b(d):
        sb[d, 0].wait_recv()
        rb[d, 0] = send(og_all.at[d, 0, (a + 3) % 4], og_all.at[d, 0, (a + 3) % 4], ap)
        sb[d, 1].wait_recv()
        rb[d, 1] = send(og_all.at[d, 1, (a + 1) % 4], og_all.at[d, 1, (a + 1) % 4], am)

    hp[0].wait_recv()
    relay_p = send(hid_all.at[3, k, 0], hid_all.at[2, k, 0], yn(1, k))
    forward(3, 0)
    hm[1].wait_recv()
    relay_m = send(hid_all.at[1, k, 1], hid_all.at[2, k, 1], yn(3, k))
    forward(1, 1)
    relay_b(order[0])
    relay_b(order[1])
    hp[1].wait_recv()
    forward(3, 1)
    hm[0].wait_recv()
    forward(1, 0)
    relay_b(order[2])
    relay_p.wait_recv()
    forward(2, 0)
    relay_m.wait_recv()
    forward(2, 1)
    for d in order:
        rb[d, 0].wait_recv()
        rb[d, 1].wait_recv()
    sib_og.wait_recv()
    sib_hid.wait_recv()
    for copy in forwards:
        copy.wait_recv()
    l0.wait()
    l1.wait()
    for copy in sent:
        copy.wait_send()


SENDS = 6 + 4 + 2 + 3 * 4 + 3 * 4 + 2 + 6


def gather(hid, og):
    return pl.pallas_call(
        gather_kernel,
        out_shape=(
            jax.ShapeDtypeStruct((4, 2, 2, 256, 1024), jnp.bfloat16),
            jax.ShapeDtypeStruct((4, 2, 4, 4, 32, 1024), jnp.bfloat16),
        ),
        in_specs=[pl.BlockSpec(memory_space=pl.ANY)] * 2,
        out_specs=(pl.BlockSpec(memory_space=pl.ANY),) * 2,
        scratch_shapes=[
            pltpu.SemaphoreType.DMA((SENDS,)),
            pltpu.SemaphoreType.DMA((SENDS,)),
            pltpu.SemaphoreType.DMA((2,)),
            pltpu.SemaphoreType.DMA((4, 2)),
        ],
        compiler_params=pltpu.CompilerParams(collective_id=0, has_side_effects=True),
        name="gather",
    )(hid.reshape(2, 256, 1024), og.reshape(4, 4, 32, 8192))


def dot(left, right, dims):
    return lax.dot_general(left, right, (dims, ((), ())), preferred_element_type=jnp.float32)


def root_of(stat):
    rows = lax.broadcasted_iota(jnp.int32, (BLK, BLK), 0)
    cols = lax.broadcasted_iota(jnp.int32, (BLK, BLK), 1)
    diag = rows == cols
    sym = stat.astype(jnp.bfloat16).astype(jnp.float32)
    mean = jnp.sum(jnp.where(diag, sym, 0.0), keepdims=True) / BLK
    square = jnp.sum(sym * sym, keepdims=True)
    norm = jnp.sqrt(square + (0.21 * BLK) * mean * mean + 1e-06)
    scaled = (sym + jnp.where(diag, 0.1 * mean, 0.0)) * (1.0 / norm)
    coupled = (4.0 * scaled).astype(jnp.bfloat16)
    first = (jnp.where(diag, 1.25, 0.0) - scaled).astype(jnp.bfloat16)
    plain = ((1,), (0,))
    two = dot(first, first, plain).astype(jnp.bfloat16)
    four = dot(two, two, plain).astype(jnp.bfloat16)
    after = dot(four, coupled, plain)
    second = (jnp.where(diag, 1.25, 0.0) - 0.25 * after).astype(jnp.bfloat16)
    scale = jnp.sqrt(jnp.sqrt(4.0 / norm)) * jnp.sqrt(jnp.sqrt(1.1 * mean))
    top = (dot(first[:256], second, plain) * scale).astype(jnp.bfloat16)
    low = (dot(first[256:], second[:, 256:], plain) * scale).astype(jnp.bfloat16)
    return top, low


def roots_kernel(g_ref, out_ref):
    g = g_ref[...]
    for kind in (0, 1):
        axis = ((1,), (1,)) if kind == 0 else ((0,), (0,))
        top, low = root_of(dot(g, g, axis))
        n = 0
        for i in range(4):
            for j in range(i, 4):
                if i < 2:
                    block = top[128 * i : 128 * i + 128, 128 * j : 128 * j + 128]
                else:
                    block = low[128 * (i - 2) : 128 * (i - 1), 128 * (j - 2) : 128 * (j - 1)]
                out_ref[kind, 128 * n : 128 * n + 128, :] = block
                n += 1


def roots(grad):
    return pl.pallas_call(
        roots_kernel,
        grid=(4,),
        out_shape=jax.ShapeDtypeStruct((STATS, ROWS, 128), jnp.bfloat16),
        in_specs=[pl.BlockSpec((BLK, BLK), lambda i: (i // 2, i % 2))],
        out_specs=pl.BlockSpec((2, ROWS, 128), lambda i: (i, 0, 0)),
        compiler_params=pltpu.CompilerParams(vmem_limit_bytes=LIMIT),
        name="roots",
    )(grad)


def hop_matrix():
    out = np.zeros((4, 128, 256), np.float32)
    for lane in range(128):
        g, n = lane // 16, lane % 16
        z, x = n // 4, n % 4
        targets = (z * 4 + (x + 1) % 4, z * 4 + (x + 3) % 4, (z + 1) % 4 * 4 + x, (z + 3) % 4 * 4 + x)
        for link, to in enumerate(targets):
            out[link, lane, g * 16 + to] = 1.0
            out[link, lane, 128 + g * 16 + to] = link
    return out.reshape(512, 256)


def plan_kernel(dest_ref, hop_ref, out_ref):
    dest = dest_ref[...]
    lane = lax.broadcasted_iota(jnp.int32, (128, 128), 1)
    item = lax.broadcasted_iota(jnp.int32, (128, 128), 0)
    node = lane & 15
    home = dest == node
    dx = (dest - node) & 3
    dz = ((dest >> 2) - (node >> 2)) & 3
    wants = ((dx == 1) | (dx == 2), dx >= 2, (dz == 1) | (dz == 2), dz >= 2)
    ways = sum(w.astype(jnp.int32) for w in wants)
    far = jnp.where(dx == 3, 1, dx) + jnp.where(dz == 3, 1, dz)
    key = ((4 - ways) * 8192 + far * 1024 + (128 - item)).astype(jnp.float32)
    keys = [jnp.where(w, key, 0.0) for w in wants]
    here = ((item >> 3) == node).astype(jnp.float32)
    slot = (item & 7).astype(jnp.float32)
    homef = home.astype(jnp.float32)
    hop = hop_ref[...]
    out_ref[...] = jnp.zeros_like(out_ref)
    for t in range(STEPS_MAX):
        moves = []
        for link in range(4):
            v = keys[link] * here
            best = jnp.max(v, axis=0, keepdims=True)
            win = jnp.where((v == best) & (v > 0.0), 1.0, 0.0)
            here = here - win
            pick = jnp.sum(win * slot, axis=0, keepdims=True)
            out_ref[4 * t + link : 4 * t + link + 1, :] = pick.astype(jnp.int32)
            moves.append(win.astype(jnp.bfloat16))
        landed = dot(jnp.concatenate(moves, axis=1), hop, ((1,), (0,)))
        new = landed[:, :128]
        here = here + new
        slot = jnp.where(new > 0.5, landed[:, 128:] + (STATS + 4.0 * t), slot)
        if t + 1 in (STEPS_FEW, STEPS_MAX):
            row = 4 * STEPS_MAX + MOST + (0 if t + 1 == STEPS_FEW else 1)
            done = jnp.sum(here * homef, keepdims=True)
            out_ref[row : row + 1, :] = jnp.broadcast_to(done, (1, 128)).astype(jnp.int32)
    below = (lane < item).astype(jnp.bfloat16)
    rank = dot(below, home.astype(jnp.bfloat16), ((1,), (0,)))
    for n in range(MOST):
        mine = jnp.where(home & (rank == float(n)), slot + 1.0, 0.0)
        row = 4 * STEPS_MAX + n
        out_ref[row : row + 1, :] = jnp.sum(mine, axis=0, keepdims=True).astype(jnp.int32) - 1


def plan(all_owners):
    dest = jnp.repeat(all_owners.reshape(8, 128).T, 16, axis=1)
    return pl.pallas_call(
        plan_kernel,
        out_shape=jax.ShapeDtypeStruct((TABLE, 128), jnp.int32),
        compiler_params=pltpu.CompilerParams(vmem_limit_bytes=LIMIT),
        name="plan",
    )(dest, jnp.asarray(hop_matrix(), jnp.bfloat16))


def deliver_kernel(steps, table, packed, out, pool, recv, stage, ss, rs):
    r, c = lax.axis_index("dp"), lax.axis_index("mp")
    z, x = c // 4, c % 4
    me = r * 16 + c
    peers = (
        (r, z * 4 + (x + 1) % 4),
        (r, z * 4 + (x + 3) % 4),
        (r, (z + 1) % 4 * 4 + x),
        (r, (z + 3) % 4 * 4 + x),
    )
    barrier = pltpu.get_barrier_semaphore()
    for dev in peers:
        pl.semaphore_signal(barrier, inc=1, device_id=dev, device_id_type=MESH)
    pl.semaphore_wait(barrier, 4)

    pool[:STATS] = packed[...]

    def copy(t, link):
        return pltpu.make_async_remote_copy(
            src_ref=stage.at[t % 2, link],
            dst_ref=recv.at[t, link],
            send_sem=ss.at[t % 2, link],
            recv_sem=rs.at[t, link],
            device_id=peers[link],
            device_id_type=MESH,
        )

    def land(t):
        for link in range(4):
            copy(t, link).wait_recv()
            pool[STATS + 4 * t + link] = recv[t, link]

    def push(t):
        for link in range(4):
            stage[t % 2, link] = pool[table[4 * t + link, me]]
            copy(t, link).start()

    push(0)
    land(0)
    push(1)

    def step(t, carry):
        land(t - 1)
        for link in range(4):
            copy(t - 2, link).wait_send()
        push(t)
        return carry

    lax.fori_loop(2, steps, step, 0)
    land(steps - 1)
    for t in (steps - 2, steps - 1):
        for link in range(4):
            copy(t, link).wait_send()
    for n in range(MOST):
        at = table[4 * STEPS_MAX + n, me]
        block = pool[jnp.maximum(at, 0)]
        keep = (at >= 0).astype(jnp.bfloat16)
        out[n] = block * keep


def deliver(steps, table, packed):
    return pl.pallas_call(
        functools.partial(deliver_kernel, steps),
        out_shape=jax.ShapeDtypeStruct((MOST, ROWS, 128), jnp.bfloat16),
        in_specs=[pl.BlockSpec(memory_space=pltpu.SMEM), pl.BlockSpec(memory_space=pltpu.VMEM)],
        out_specs=pl.BlockSpec(memory_space=pltpu.VMEM),
        scratch_shapes=[
            pltpu.VMEM((STATS + 4 * steps, ROWS, 128), jnp.bfloat16),
            pltpu.VMEM((steps, 4, ROWS, 128), jnp.bfloat16),
            pltpu.VMEM((2, 4, ROWS, 128), jnp.bfloat16),
            pltpu.SemaphoreType.DMA((2, 4)),
            pltpu.SemaphoreType.DMA((steps, 4)),
        ],
        compiler_params=pltpu.CompilerParams(
            collective_id=steps, has_side_effects=True, vmem_limit_bytes=LIMIT
        ),
        name="deliver",
    )(table, packed)


def deliver_any(all_owners, packed):
    myself = lax.axis_index("mp")
    row = lax.axis_index("dp")
    lists = all_owners[row]
    mine = lists[myself]
    count = lists.shape[0]
    match = (mine[None, :] == jnp.arange(count, dtype=jnp.int32)[:, None]).astype(jnp.int32)
    rank = jnp.cumsum(match, axis=1) - match
    select = (match[:, None, :] > 0) & (rank[:, None, :] == jnp.arange(CAP, dtype=jnp.int32)[None, :, None])
    index = jnp.sum(select.astype(jnp.int32) * jnp.arange(STATS, dtype=jnp.int32), axis=2)
    outgoing = packed[index.reshape(-1)].reshape(count, CAP, ROWS, 128)
    received = lax.all_to_all(outgoing, "mp", split_axis=0, concat_axis=0, tiled=True)
    counts = jnp.sum((lists == myself).astype(jnp.int32), axis=1)
    valid = (jnp.arange(CAP, dtype=jnp.int32)[None, :] < counts[:, None]).reshape(-1).astype(jnp.int32)
    before = jnp.cumsum(valid) - valid
    chosen = (valid[None, :] > 0) & (before[None, :] == jnp.arange(MOST, dtype=jnp.int32)[:, None])
    index = jnp.sum(chosen.astype(jnp.int32) * jnp.arange(count * CAP, dtype=jnp.int32), axis=1)
    picked = received.reshape(count * CAP, ROWS, 128)[index]
    return jnp.where(jnp.any(chosen, axis=1)[:, None, None], picked, jnp.zeros_like(picked))


def unpack_kernel(in_ref, out_ref):
    n = 0
    for i in range(4):
        for j in range(i, 4):
            block = in_ref[0, 128 * n : 128 * n + 128, :]
            out_ref[0, 128 * i : 128 * i + 128, 128 * j : 128 * j + 128] = block
            if i != j:
                out_ref[0, 128 * j : 128 * j + 128, 128 * i : 128 * i + 128] = block.T
            n += 1


def unpack(packed):
    return pl.pallas_call(
        unpack_kernel,
        grid=(MOST,),
        out_shape=jax.ShapeDtypeStruct((MOST, BLK, BLK), jnp.bfloat16),
        in_specs=[pl.BlockSpec((1, ROWS, 128), lambda i: (i, 0, 0))],
        out_specs=pl.BlockSpec((1, BLK, BLK), lambda i: (i, 0, 0)),
        compiler_params=pltpu.CompilerParams(vmem_limit_bytes=LIMIT),
        name="unpack",
    )(packed)


def body(hidden_acts, out_grad, owners):
    all_owners = lax.all_gather(owners, "mp", axis=1, tiled=True)
    all_owners = lax.all_gather(all_owners, "dp", axis=0, tiled=True)
    hid_all, og_all = gather(hidden_acts, out_grad)
    table = plan(all_owners)
    grad = lax.dot_general(
        hid_all.reshape(4096, 1024),
        og_all.reshape(4096, 1024),
        (((0,), (0,)), ((), ())),
        preferred_element_type=jnp.float32,
    ).astype(jnp.bfloat16)
    packed = roots(grad)
    total = 8 * 128
    few = table[4 * STEPS_MAX + MOST, 0] == total
    most = table[4 * STEPS_MAX + MOST + 1, 0] == total
    which = jnp.where(few, 0, jnp.where(most, 1, 2))
    arrived = lax.switch(
        which,
        [
            lambda: deliver(STEPS_FEW, table, packed),
            lambda: deliver(STEPS_MAX, table, packed),
            lambda: deliver_any(all_owners, packed),
        ],
    )
    return unpack(arrived)[None, None]


def solution(mesh):
    placed = (P("dp", "mp"), P("dp", None), P("dp", "mp", None))
    return jax.shard_map(
        body, mesh=mesh, in_specs=placed, out_specs=P("dp", "mp", None, None, None), check_vma=False
    )
```

```python
import functools

import jax
import jax.numpy as jnp
import numpy as np
from jax import lax
from jax.experimental import pallas as pl
from jax.experimental.pallas import tpu as pltpu
from jax.sharding import PartitionSpec as P

MESH = pl.DeviceIdType.MESH
BLK = 512
STATS = 8
CAP = 2
MOST = 12
ROWS = 1040
STEPS_MAX = 10
STEPS_FEW = 8
TABLE = 4 * STEPS_MAX + MOST + 4
OFF = ((0, 1), (0, 2), (0, 3), (1, 2), (1, 3), (2, 3))
LIMIT = 56 * 1024 * 1024


def gather_kernel(hid, og, own, hop_ref, grad_ref, table_ref, hid_all, og_all, own_all, acc, ss, rs, ls, rs1, rso):
    r, c = lax.axis_index("dp"), lax.axis_index("mp")
    y, k = r // 2, r % 2
    z, x = c // 4, c % 4
    sib = (2 * y + 1 - k, c)

    def yn(dy, core):
        return (2 * ((y + dy) % 4) + core, c)

    a = z * (1 - k) + x * k
    b = x * (1 - k) + z * k

    def plane(aa, bb):
        zz = aa * (1 - k) + bb * k
        xx = bb * (1 - k) + aa * k
        return (r, zz * 4 + xx)

    bp, bm = plane(a, (b + 1) % 4), plane(a, (b + 3) % 4)
    ap, am = plane((a + 1) % 4, b), plane((a + 3) % 4, b)
    rows = [sib] + [yn(dy, core) for dy in (1, 2, 3) for core in (0, 1)]
    along_x = [(r, z * 4 + (x + n) % 4) for n in (1, 2, 3)]
    along_z = [(r, (z + n) % 4 * 4 + x) for n in (1, 2, 3)]

    barrier = pltpu.get_barrier_semaphore()
    partners = rows + along_x + along_z
    for dev in partners:
        pl.semaphore_signal(barrier, inc=1, device_id=dev, device_id_type=MESH)
    pl.semaphore_wait(barrier, len(partners))

    sent = []

    def send(src, dst, dev, landed=None):
        i = len(sent)
        landed = rs.at[i] if landed is None else landed
        copy = pltpu.make_async_remote_copy(
            src_ref=src, dst_ref=dst, send_sem=ss.at[i], recv_sem=landed, device_id=dev, device_id_type=MESH
        )
        copy.start()
        sent.append(copy)
        return copy

    def await_copy(ref, sem):
        pltpu.make_async_copy(ref, ref, sem).wait()

    def columns(row):
        return pl.ds(pl.multiple_of(row * 1024, 1024), 1024)

    l2 = pltpu.make_async_copy(own, own_all.at[z, x, r], ls.at[2])
    l2.start()
    for n, dev in enumerate(rows):
        send(own, own_all.at[z, x, r], dev, rso.at[r])
    for dy in (1, 3, 2):
        for core in (0, 1):
            aa = z * (1 - core) + x * core
            bb = x * (1 - core) + z * core
            row = 2 * ((y + dy) % 4) + core
            send(og.at[aa, bb, :, columns(row)], og_all.at[4 - dy, k, aa, bb], yn(dy, core), rs1.at[4 - dy, k])
    l0 = pltpu.make_async_copy(og.at[:, :, :, columns(r)], og_all.at[0, k], ls.at[0])
    l1 = pltpu.make_async_copy(hid, hid_all.at[0, k], ls.at[1])
    l0.start()
    l1.start()
    sib_og = send(og.at[:, :, :, columns(2 * y + 1 - k)], og_all.at[0, k], sib)
    sib_hid = send(hid, hid_all.at[0, k], sib)

    sa, sb, ra, rb, hp, hm, fw = {}, {}, {}, {}, {}, {}, {}

    def stage_a(d):
        for core in (0, 1):
            await_copy(og_all.at[d, core, a, b], rs1.at[d, core])
        sa[d, 0] = send(og_all.at[d, :, a, b], og_all.at[d, :, a, b], bp)
        sa[d, 1] = send(og_all.at[d, :, a, b], og_all.at[d, :, a, b], bm)

    def relay_a(d):
        sa[d, 0].wait_recv()
        ra[d, 0] = send(og_all.at[d, 0, a, (b + 3) % 4], og_all.at[d, 0, a, (b + 3) % 4], bp)
        sa[d, 1].wait_recv()
        ra[d, 1] = send(og_all.at[d, 1, a, (b + 1) % 4], og_all.at[d, 1, a, (b + 1) % 4], bm)

    def stage_b(d):
        ra[d, 0].wait_recv()
        ra[d, 1].wait_recv()
        sb[d, 0] = send(og_all.at[d, :, a], og_all.at[d, :, a], ap)
        sb[d, 1] = send(og_all.at[d, :, a], og_all.at[d, :, a], am)

    def relay_b(d):
        sb[d, 0].wait_recv()
        rb[d, 0] = send(og_all.at[d, 0, (a + 3) % 4], og_all.at[d, 0, (a + 3) % 4], ap)
        sb[d, 1].wait_recv()
        rb[d, 1] = send(og_all.at[d, 1, (a + 1) % 4], og_all.at[d, 1, (a + 1) % 4], am)

    def forward(d, h):
        fw[d, h] = send(hid_all.at[d, k, h], hid_all.at[d, k, h], sib)

    def add_products(d):
        def tile(i, carry):
            at = pl.ds(pl.multiple_of(i * 256, 256), 256)
            left = hid_all[d, :, :, :, at].reshape(1024, 256)
            right = og_all[d].reshape(1024, 1024)
            part = dot(left, right, ((0,), (0,)))
            if d == 0:
                acc[at, :] = part
            elif d == 2:
                grad_ref[at, :] = (acc[at, :] + part).astype(jnp.bfloat16)
            else:
                acc[at, :] += part
            return carry

        lax.fori_loop(0, 4, tile, 0)

    stage_a(1)
    stage_a(3)
    for h in (0, 1):
        hp[h] = send(hid.at[h], hid_all.at[3, k, h], yn(1, k))
        hm[1 - h] = send(hid.at[1 - h], hid_all.at[1, k, 1 - h], yn(3, k))
    stage_a(2)
    l2.wait()
    for dy in range(8):
        pl.when(dy != r)(lambda dy=dy: await_copy(own_all.at[z, x, dy], rso.at[dy]))
    own_x = [send(own_all.at[z, x], own_all.at[z, x], dev) for dev in along_x]
    relay_a(1)
    relay_a(3)
    stage_b(1)
    relay_a(2)
    stage_b(3)
    for copy in own_x:
        copy.wait_recv()
    own_z = [send(own_all.at[z], own_all.at[z], dev) for dev in along_z]
    stage_b(2)
    l0.wait()
    l1.wait()
    sib_og.wait_recv()
    sib_hid.wait_recv()
    add_products(0)
    relay_b(1)
    hp[0].wait_recv()
    relay_p = send(hid_all.at[3, k, 0], hid_all.at[2, k, 0], yn(1, k))
    forward(3, 0)
    hm[1].wait_recv()
    relay_m = send(hid_all.at[1, k, 1], hid_all.at[2, k, 1], yn(3, k))
    forward(1, 1)
    for copy in own_z:
        copy.wait_recv()
    make_plan(own_all, hop_ref, table_ref)
    relay_b(3)
    hm[0].wait_recv()
    forward(1, 0)
    hp[1].wait_recv()
    forward(3, 1)
    relay_b(2)
    rb[1, 0].wait_recv()
    rb[1, 1].wait_recv()
    fw[1, 0].wait_recv()
    fw[1, 1].wait_recv()
    add_products(1)
    rb[3, 0].wait_recv()
    rb[3, 1].wait_recv()
    fw[3, 0].wait_recv()
    fw[3, 1].wait_recv()
    add_products(3)
    relay_p.wait_recv()
    forward(2, 0)
    relay_m.wait_recv()
    forward(2, 1)
    rb[2, 0].wait_recv()
    rb[2, 1].wait_recv()
    fw[2, 0].wait_recv()
    fw[2, 1].wait_recv()
    add_products(2)
    for copy in sent:
        copy.wait_send()


SENDS = 7 + 6 + 2 + 4 + 6 + 6 + 6 + 6 + 2 + 6 + 3 + 3


def gather(hid, og, own):
    tile = jnp.broadcast_to(own.reshape(8, 1), (8, 128))
    return pl.pallas_call(
        gather_kernel,
        out_shape=(
            jax.ShapeDtypeStruct((1024, 1024), jnp.bfloat16),
            jax.ShapeDtypeStruct((TABLE, 128), jnp.int32),
        ),
        in_specs=[pl.BlockSpec(memory_space=pl.ANY)] * 3 + [pl.BlockSpec(memory_space=pltpu.VMEM)],
        out_specs=(pl.BlockSpec(memory_space=pltpu.VMEM),) * 2,
        scratch_shapes=[
            pltpu.VMEM((4, 2, 2, 256, 1024), jnp.bfloat16),
            pltpu.VMEM((4, 2, 4, 4, 32, 1024), jnp.bfloat16),
            pltpu.VMEM((4, 4, 8, 8, 128), jnp.int32),
            pltpu.VMEM((1024, 1024), jnp.float32),
            pltpu.SemaphoreType.DMA((SENDS,)),
            pltpu.SemaphoreType.DMA((SENDS,)),
            pltpu.SemaphoreType.DMA((3,)),
            pltpu.SemaphoreType.DMA((4, 2)),
            pltpu.SemaphoreType.DMA((8,)),
        ],
        compiler_params=pltpu.CompilerParams(collective_id=0, has_side_effects=True, vmem_limit_bytes=LIMIT),
        name="gather",
    )(hid.reshape(2, 256, 1024), og.reshape(4, 4, 32, 8192), tile, jnp.asarray(hop_matrix(), jnp.bfloat16))


def dot(left, right, dims):
    return lax.dot_general(left, right, (dims, ((), ())), preferred_element_type=jnp.float32)


def root_of(stat):
    rows = lax.broadcasted_iota(jnp.int32, (BLK, BLK), 0)
    cols = lax.broadcasted_iota(jnp.int32, (BLK, BLK), 1)
    diag = rows == cols
    sym = stat.astype(jnp.bfloat16).astype(jnp.float32)
    mean = jnp.sum(jnp.where(diag, sym, 0.0), keepdims=True) / BLK
    square = jnp.sum(sym * sym, keepdims=True)
    norm = jnp.sqrt(square + (0.21 * BLK) * mean * mean + 1e-06)
    scaled = (sym + jnp.where(diag, 0.1 * mean, 0.0)) * (1.0 / norm)
    coupled = (4.0 * scaled).astype(jnp.bfloat16)
    first = (jnp.where(diag, 1.25, 0.0) - scaled).astype(jnp.bfloat16)
    plain = ((1,), (0,))
    two = dot(first, first, plain).astype(jnp.bfloat16)
    four = dot(two, two, plain).astype(jnp.bfloat16)
    after = dot(four, coupled, plain)
    second = (jnp.where(diag, 1.25, 0.0) - 0.25 * after).astype(jnp.bfloat16)
    scale = jnp.sqrt(jnp.sqrt(4.0 / norm)) * jnp.sqrt(jnp.sqrt(1.1 * mean))
    top = dot(first[:256], second, plain) * scale
    low = dot(first[256:], second[:, 256:], plain) * scale
    return top, low


def roots_kernel(g_ref, out_ref):
    g = g_ref[...]
    rows = lax.broadcasted_iota(jnp.int32, (128, 128), 0)
    cols = lax.broadcasted_iota(jnp.int32, (128, 128), 1)
    for kind in (0, 1):
        axis = ((1,), (1,)) if kind == 0 else ((0,), (0,))
        top, low = root_of(dot(g, g, axis))

        def block(i, j):
            if i < 2:
                return top[128 * i : 128 * i + 128, 128 * j : 128 * j + 128]
            return low[128 * (i - 2) : 128 * (i - 1), 128 * (j - 2) : 128 * (j - 1)]

        for n, (i, j) in enumerate(OFF):
            out_ref[kind, 128 * n : 128 * n + 128, :] = block(i, j).astype(jnp.bfloat16)
        spare = jnp.zeros((16, 128), jnp.float32)
        for n in (0, 1):
            first, second = block(2 * n, 2 * n), block(2 * n + 1, 2 * n + 1)
            at = 128 * (6 + n)
            out_ref[kind, at : at + 128, :] = jnp.where(rows <= cols, first, second).astype(jnp.bfloat16)
            line = jnp.sum(jnp.where(rows == cols, second, 0.0), axis=0, keepdims=True)
            spare = jnp.where(rows[:16] == n, line, spare)
        out_ref[kind, 1024:, :] = spare.astype(jnp.bfloat16)


def roots(grad):
    return pl.pallas_call(
        roots_kernel,
        grid=(4,),
        out_shape=jax.ShapeDtypeStruct((STATS, ROWS, 128), jnp.bfloat16),
        in_specs=[pl.BlockSpec((BLK, BLK), lambda i: (i // 2, i % 2))],
        out_specs=pl.BlockSpec((2, ROWS, 128), lambda i: (i, 0, 0)),
        compiler_params=pltpu.CompilerParams(vmem_limit_bytes=LIMIT),
        name="roots",
    )(grad)


def hop_matrix():
    out = np.zeros((4, 128, 256), np.float32)
    for lane in range(128):
        g, n = lane // 16, lane % 16
        z, x = n // 4, n % 4
        targets = (z * 4 + (x + 1) % 4, z * 4 + (x + 3) % 4, (z + 1) % 4 * 4 + x, (z + 3) % 4 * 4 + x)
        for link, to in enumerate(targets):
            out[link, lane, g * 16 + to] = 1.0
            out[link, lane, 128 + g * 16 + to] = link
    return out.reshape(512, 256)


def make_plan(own_ref, hop_ref, out_ref):
    lane = lax.broadcasted_iota(jnp.int32, (128, 128), 1)
    item = lax.broadcasted_iota(jnp.int32, (128, 128), 0)
    node = lane & 15
    group = lax.broadcasted_iota(jnp.int32, (8, 128), 1) // 16
    parts = []
    for c in range(16):
        part = jnp.zeros((8, 128), jnp.int32)
        for row in range(8):
            part = jnp.where(group == row, own_ref[c // 4, c % 4, row], part)
        parts.append(part)
    dest = jnp.concatenate(parts, axis=0)
    home = dest == node
    dx = (dest - node) & 3
    dz = ((dest >> 2) - (node >> 2)) & 3
    wants = ((dx == 1) | (dx == 2), dx >= 2, (dz == 1) | (dz == 2), dz >= 2)
    ways = sum(w.astype(jnp.int32) for w in wants)
    far = jnp.where(dx == 3, 1, dx) + jnp.where(dz == 3, 1, dz)
    key = ((4 - ways) * 8192 + far * 1024 + (128 - item)).astype(jnp.float32)
    keys = [jnp.where(w, key, 0.0) for w in wants]
    here = ((item >> 3) == node).astype(jnp.float32)
    slot = (item & 7).astype(jnp.float32)
    homef = home.astype(jnp.float32)
    hop = hop_ref[...]
    out_ref[...] = jnp.zeros_like(out_ref)
    for t in range(STEPS_MAX):
        moves = []
        for link in range(4):
            v = keys[link] * here
            best = jnp.max(v, axis=0, keepdims=True)
            win = jnp.where((v == best) & (v > 0.0), 1.0, 0.0)
            here = here - win
            pick = jnp.sum(win * slot, axis=0, keepdims=True)
            out_ref[4 * t + link : 4 * t + link + 1, :] = pick.astype(jnp.int32)
            moves.append(win.astype(jnp.bfloat16))
        landed = dot(jnp.concatenate(moves, axis=1), hop, ((1,), (0,)))
        new = landed[:, :128]
        here = here + new
        slot = jnp.where(new > 0.5, landed[:, 128:] + (STATS + 4.0 * t), slot)
        if t + 1 in (STEPS_FEW, STEPS_MAX):
            row = 4 * STEPS_MAX + MOST + (0 if t + 1 == STEPS_FEW else 1)
            done = jnp.sum(here * homef, keepdims=True)
            out_ref[row : row + 1, :] = jnp.broadcast_to(done, (1, 128)).astype(jnp.int32)
    below = (lane < item).astype(jnp.bfloat16)
    rank = dot(below, home.astype(jnp.bfloat16), ((1,), (0,)))
    for n in range(MOST):
        mine = jnp.where(home & (rank == float(n)), slot + 1.0, 0.0)
        row = 4 * STEPS_MAX + n
        out_ref[row : row + 1, :] = jnp.sum(mine, axis=0, keepdims=True).astype(jnp.int32) - 1


def deliver_kernel(steps, table, packed, out, pool, recv, stage, ss, rs):
    r, c = lax.axis_index("dp"), lax.axis_index("mp")
    z, x = c // 4, c % 4
    me = r * 16 + c
    peers = (
        (r, z * 4 + (x + 1) % 4),
        (r, z * 4 + (x + 3) % 4),
        (r, (z + 1) % 4 * 4 + x),
        (r, (z + 3) % 4 * 4 + x),
    )
    barrier = pltpu.get_barrier_semaphore()
    for dev in peers:
        pl.semaphore_signal(barrier, inc=1, device_id=dev, device_id_type=MESH)
    pl.semaphore_wait(barrier, 4)

    pool[:STATS] = packed[...]

    def copy(t, link):
        return pltpu.make_async_remote_copy(
            src_ref=stage.at[t % 2, link],
            dst_ref=recv.at[t, link],
            send_sem=ss.at[t % 2, link],
            recv_sem=rs.at[t, link],
            device_id=peers[link],
            device_id_type=MESH,
        )

    def land(t):
        for link in range(4):
            copy(t, link).wait_recv()
            pool[STATS + 4 * t + link] = recv[t, link]

    def push(t):
        for link in range(4):
            stage[t % 2, link] = pool[table[4 * t + link, me]]
            copy(t, link).start()

    push(0)
    land(0)
    push(1)

    def step(t, carry):
        land(t - 1)
        for link in range(4):
            copy(t - 2, link).wait_send()
        push(t)
        return carry

    lax.fori_loop(2, steps, step, 0)
    land(steps - 1)
    for t in (steps - 2, steps - 1):
        for link in range(4):
            copy(t, link).wait_send()
    for n in range(MOST):
        at = table[4 * STEPS_MAX + n, me]
        block = pool[jnp.maximum(at, 0)]
        keep = (at >= 0).astype(jnp.bfloat16)
        out[n] = block * keep


def deliver(steps, table, packed):
    return pl.pallas_call(
        functools.partial(deliver_kernel, steps),
        out_shape=jax.ShapeDtypeStruct((MOST, ROWS, 128), jnp.bfloat16),
        in_specs=[pl.BlockSpec(memory_space=pltpu.SMEM), pl.BlockSpec(memory_space=pltpu.VMEM)],
        out_specs=pl.BlockSpec(memory_space=pltpu.VMEM),
        scratch_shapes=[
            pltpu.VMEM((STATS + 4 * steps, ROWS, 128), jnp.bfloat16),
            pltpu.VMEM((steps, 4, ROWS, 128), jnp.bfloat16),
            pltpu.VMEM((2, 4, ROWS, 128), jnp.bfloat16),
            pltpu.SemaphoreType.DMA((2, 4)),
            pltpu.SemaphoreType.DMA((steps, 4)),
        ],
        compiler_params=pltpu.CompilerParams(
            collective_id=steps, has_side_effects=True, vmem_limit_bytes=LIMIT
        ),
        name="deliver",
    )(table, packed)


def deliver_any(owners, packed):
    myself = lax.axis_index("mp")
    lists = lax.all_gather(owners, "mp", axis=1, tiled=True)[0]
    mine = lists[myself]
    count = lists.shape[0]
    match = (mine[None, :] == jnp.arange(count, dtype=jnp.int32)[:, None]).astype(jnp.int32)
    rank = jnp.cumsum(match, axis=1) - match
    select = (match[:, None, :] > 0) & (rank[:, None, :] == jnp.arange(CAP, dtype=jnp.int32)[None, :, None])
    index = jnp.sum(select.astype(jnp.int32) * jnp.arange(STATS, dtype=jnp.int32), axis=2)
    outgoing = packed[index.reshape(-1)].reshape(count, CAP, ROWS, 128)
    received = lax.all_to_all(outgoing, "mp", split_axis=0, concat_axis=0, tiled=True)
    counts = jnp.sum((lists == myself).astype(jnp.int32), axis=1)
    valid = (jnp.arange(CAP, dtype=jnp.int32)[None, :] < counts[:, None]).reshape(-1).astype(jnp.int32)
    before = jnp.cumsum(valid) - valid
    chosen = (valid[None, :] > 0) & (before[None, :] == jnp.arange(MOST, dtype=jnp.int32)[:, None])
    index = jnp.sum(chosen.astype(jnp.int32) * jnp.arange(count * CAP, dtype=jnp.int32), axis=1)
    picked = received.reshape(count * CAP, ROWS, 128)[index]
    return jnp.where(jnp.any(chosen, axis=1)[:, None, None], picked, jnp.zeros_like(picked))


def unpack_kernel(in_ref, out_ref):
    rows = lax.broadcasted_iota(jnp.int32, (128, 128), 0)
    cols = lax.broadcasted_iota(jnp.int32, (128, 128), 1)
    unit = (rows == cols).astype(jnp.bfloat16)
    for m in range(PAIR):
        flipped = dot(unit, in_ref[m, :1024, :], ((1,), (1,)))
        for n, (i, j) in enumerate(OFF):
            out_ref[m, 128 * i : 128 * i + 128, 128 * j : 128 * j + 128] = in_ref[m, 128 * n : 128 * n + 128, :]
            turned = flipped[:, 128 * n : 128 * n + 128].astype(jnp.bfloat16)
            out_ref[m, 128 * j : 128 * j + 128, 128 * i : 128 * i + 128] = turned
        spare = in_ref[m, 1024:, :].astype(jnp.float32)
        for n in (0, 1):
            both = in_ref[m, 128 * (6 + n) : 128 * (7 + n), :].astype(jnp.float32)
            other = flipped[:, 128 * (6 + n) : 128 * (7 + n)]
            first = jnp.where(rows <= cols, both, other)
            second = jnp.where(rows > cols, both, other)
            second = jnp.where(rows == cols, spare[n : n + 1, :], second)
            for half, value in ((0, first), (1, second)):
                at = 128 * (2 * n + half)
                out_ref[m, at : at + 128, at : at + 128] = value.astype(jnp.bfloat16)


PAIR = 2


def unpack(packed):
    return pl.pallas_call(
        unpack_kernel,
        grid=(MOST // PAIR,),
        out_shape=jax.ShapeDtypeStruct((MOST, BLK, BLK), jnp.bfloat16),
        in_specs=[pl.BlockSpec((PAIR, ROWS, 128), lambda i: (i, 0, 0))],
        out_specs=pl.BlockSpec((PAIR, BLK, BLK), lambda i: (i, 0, 0)),
        compiler_params=pltpu.CompilerParams(vmem_limit_bytes=LIMIT),
        name="unpack",
    )(packed)


def body(hidden_acts, out_grad, owners):
    grad, table = gather(hidden_acts, out_grad, owners)
    packed = roots(grad)
    total = 8 * 128
    few = table[4 * STEPS_MAX + MOST, 0] == total
    most = table[4 * STEPS_MAX + MOST + 1, 0] == total
    which = jnp.where(few, 0, jnp.where(most, 1, 2))
    arrived = lax.switch(
        which,
        [
            lambda: deliver(STEPS_FEW, table, packed),
            lambda: deliver(STEPS_MAX, table, packed),
            lambda: deliver_any(owners, packed),
        ],
    )
    return unpack(arrived)[None, None]


def solution(mesh):
    placed = (P("dp", "mp"), P("dp", None), P("dp", "mp", None))
    return jax.shard_map(
        body, mesh=mesh, in_specs=placed, out_specs=P("dp", "mp", None, None, None), check_vma=False
    )
```

```python
import functools

import jax
import jax.numpy as jnp
import numpy as np
from jax import lax
from jax.experimental import pallas as pl
from jax.experimental.pallas import tpu as pltpu
from jax.sharding import PartitionSpec as P

MESH = pl.DeviceIdType.MESH
BLK = 512
STATS = 8
CAP = 2
MOST = 12
ROWS = 1040
STEPS = (8, 9, 10)
STEPS_MAX = STEPS[-1]
TABLE = 4 * STEPS_MAX + MOST + 4
OFF = ((0, 1), (0, 2), (0, 3), (1, 2), (1, 3), (2, 3))
LIMIT = 56 * 1024 * 1024


def gather_kernel(hid, og, own, hop_ref, grad_ref, table_ref, hid_all, og_all, own_all, acc, ss, rs, ls, rs1, rso):
    r, c = lax.axis_index("dp"), lax.axis_index("mp")
    y, k = r // 2, r % 2
    z, x = c // 4, c % 4
    sib = (2 * y + 1 - k, c)

    def yn(dy, core):
        return (2 * ((y + dy) % 4) + core, c)

    a = z * (1 - k) + x * k
    b = x * (1 - k) + z * k

    def plane(aa, bb):
        zz = aa * (1 - k) + bb * k
        xx = bb * (1 - k) + aa * k
        return (r, zz * 4 + xx)

    bp, bm = plane(a, (b + 1) % 4), plane(a, (b + 3) % 4)
    ap, am = plane((a + 1) % 4, b), plane((a + 3) % 4, b)
    rows = [sib] + [yn(dy, core) for dy in (1, 2, 3) for core in (0, 1)]
    along_x = [(r, z * 4 + (x + n) % 4) for n in (1, 2, 3)]
    along_z = [(r, (z + n) % 4 * 4 + x) for n in (1, 2, 3)]

    barrier = pltpu.get_barrier_semaphore()
    partners = rows + along_x + along_z
    for dev in partners:
        pl.semaphore_signal(barrier, inc=1, device_id=dev, device_id_type=MESH)
    pl.semaphore_wait(barrier, len(partners))

    sent = []

    def send(src, dst, dev, landed=None):
        i = len(sent)
        landed = rs.at[i] if landed is None else landed
        copy = pltpu.make_async_remote_copy(
            src_ref=src, dst_ref=dst, send_sem=ss.at[i], recv_sem=landed, device_id=dev, device_id_type=MESH
        )
        copy.start()
        sent.append(copy)
        return copy

    def await_copy(ref, sem):
        pltpu.make_async_copy(ref, ref, sem).wait()

    def columns(row):
        return pl.ds(pl.multiple_of(row * 1024, 1024), 1024)

    l2 = pltpu.make_async_copy(own, own_all.at[z, x, r], ls.at[2])
    l2.start()
    for n, dev in enumerate(rows):
        send(own, own_all.at[z, x, r], dev, rso.at[r])
    for dy in (1, 3, 2):
        for core in (0, 1):
            aa = z * (1 - core) + x * core
            bb = x * (1 - core) + z * core
            row = 2 * ((y + dy) % 4) + core
            send(og.at[aa, bb, :, columns(row)], og_all.at[4 - dy, k, aa, bb], yn(dy, core), rs1.at[4 - dy, k])
    l0 = pltpu.make_async_copy(og.at[:, :, :, columns(r)], og_all.at[0, k], ls.at[0])
    l1 = pltpu.make_async_copy(hid, hid_all.at[0, k], ls.at[1])
    l0.start()
    l1.start()
    sib_og = send(og.at[:, :, :, columns(2 * y + 1 - k)], og_all.at[0, k], sib)
    sib_hid = send(hid, hid_all.at[0, k], sib)

    sa, sb, ra, rb, hp, hm, fw = {}, {}, {}, {}, {}, {}, {}

    def stage_a(d):
        for core in (0, 1):
            await_copy(og_all.at[d, core, a, b], rs1.at[d, core])
        sa[d, 0] = send(og_all.at[d, :, a, b], og_all.at[d, :, a, b], bp)
        sa[d, 1] = send(og_all.at[d, :, a, b], og_all.at[d, :, a, b], bm)

    def relay_a(d):
        sa[d, 0].wait_recv()
        ra[d, 0] = send(og_all.at[d, 0, a, (b + 3) % 4], og_all.at[d, 0, a, (b + 3) % 4], bp)
        sa[d, 1].wait_recv()
        ra[d, 1] = send(og_all.at[d, 1, a, (b + 1) % 4], og_all.at[d, 1, a, (b + 1) % 4], bm)

    def stage_b(d):
        ra[d, 0].wait_recv()
        ra[d, 1].wait_recv()
        sb[d, 0] = send(og_all.at[d, :, a], og_all.at[d, :, a], ap)
        sb[d, 1] = send(og_all.at[d, :, a], og_all.at[d, :, a], am)

    def relay_b(d):
        sb[d, 0].wait_recv()
        rb[d, 0] = send(og_all.at[d, 0, (a + 3) % 4], og_all.at[d, 0, (a + 3) % 4], ap)
        sb[d, 1].wait_recv()
        rb[d, 1] = send(og_all.at[d, 1, (a + 1) % 4], og_all.at[d, 1, (a + 1) % 4], am)

    def forward(d, h):
        fw[d, h] = send(hid_all.at[d, k, h], hid_all.at[d, k, h], sib)

    def add_products(d):
        def tile(i, carry):
            at = pl.ds(pl.multiple_of(i * 256, 256), 256)
            left = hid_all[d, :, :, :, at].reshape(1024, 256)
            right = og_all[d].reshape(1024, 1024)
            part = dot(left, right, ((0,), (0,)))
            if d == 0:
                acc[at, :] = part
            elif d == 2:
                grad_ref[at, :] = (acc[at, :] + part).astype(jnp.bfloat16)
            else:
                acc[at, :] += part
            return carry

        lax.fori_loop(0, 4, tile, 0)

    stage_a(1)
    stage_a(3)
    for h in (0, 1):
        hp[h] = send(hid.at[h], hid_all.at[3, k, h], yn(1, k))
        hm[1 - h] = send(hid.at[1 - h], hid_all.at[1, k, 1 - h], yn(3, k))
    stage_a(2)
    l2.wait()
    for dy in range(8):
        pl.when(dy != r)(lambda dy=dy: await_copy(own_all.at[z, x, dy], rso.at[dy]))
    own_x = [send(own_all.at[z, x], own_all.at[z, x], dev) for dev in along_x]
    relay_a(1)
    relay_a(3)
    stage_b(1)
    relay_a(2)
    stage_b(3)
    for copy in own_x:
        copy.wait_recv()
    own_z = [send(own_all.at[z], own_all.at[z], dev) for dev in along_z]
    stage_b(2)
    l0.wait()
    l1.wait()
    sib_og.wait_recv()
    sib_hid.wait_recv()
    add_products(0)
    relay_b(1)
    hp[0].wait_recv()
    relay_p = send(hid_all.at[3, k, 0], hid_all.at[2, k, 0], yn(1, k))
    forward(3, 0)
    hm[1].wait_recv()
    relay_m = send(hid_all.at[1, k, 1], hid_all.at[2, k, 1], yn(3, k))
    forward(1, 1)
    for copy in own_z:
        copy.wait_recv()
    make_plan(own_all, hop_ref, table_ref)
    relay_b(3)
    hm[0].wait_recv()
    forward(1, 0)
    hp[1].wait_recv()
    forward(3, 1)
    relay_b(2)
    rb[1, 0].wait_recv()
    rb[1, 1].wait_recv()
    fw[1, 0].wait_recv()
    fw[1, 1].wait_recv()
    add_products(1)
    rb[3, 0].wait_recv()
    rb[3, 1].wait_recv()
    fw[3, 0].wait_recv()
    fw[3, 1].wait_recv()
    add_products(3)
    relay_p.wait_recv()
    forward(2, 0)
    relay_m.wait_recv()
    forward(2, 1)
    rb[2, 0].wait_recv()
    rb[2, 1].wait_recv()
    fw[2, 0].wait_recv()
    fw[2, 1].wait_recv()
    add_products(2)
    for copy in sent:
        copy.wait_send()


SENDS = 7 + 6 + 2 + 4 + 6 + 6 + 6 + 6 + 2 + 6 + 3 + 3


def gather(hid, og, own):
    tile = jnp.broadcast_to(own.reshape(8, 1), (8, 128))
    return pl.pallas_call(
        gather_kernel,
        out_shape=(
            jax.ShapeDtypeStruct((1024, 1024), jnp.bfloat16),
            jax.ShapeDtypeStruct((TABLE, 128), jnp.int32),
        ),
        in_specs=[pl.BlockSpec(memory_space=pl.ANY)] * 3 + [pl.BlockSpec(memory_space=pltpu.VMEM)],
        out_specs=(pl.BlockSpec(memory_space=pltpu.VMEM),) * 2,
        scratch_shapes=[
            pltpu.VMEM((4, 2, 2, 256, 1024), jnp.bfloat16),
            pltpu.VMEM((4, 2, 4, 4, 32, 1024), jnp.bfloat16),
            pltpu.VMEM((4, 4, 8, 8, 128), jnp.int32),
            pltpu.VMEM((1024, 1024), jnp.float32),
            pltpu.SemaphoreType.DMA((SENDS,)),
            pltpu.SemaphoreType.DMA((SENDS,)),
            pltpu.SemaphoreType.DMA((3,)),
            pltpu.SemaphoreType.DMA((4, 2)),
            pltpu.SemaphoreType.DMA((8,)),
        ],
        compiler_params=pltpu.CompilerParams(collective_id=0, has_side_effects=True, vmem_limit_bytes=LIMIT),
        name="gather",
    )(hid.reshape(2, 256, 1024), og.reshape(4, 4, 32, 8192), tile, jnp.asarray(hop_matrix(), jnp.bfloat16))


def dot(left, right, dims):
    return lax.dot_general(left, right, (dims, ((), ())), preferred_element_type=jnp.float32)


def patched(matrix, blocks):
    lines = []
    for i in range(4):
        cells = [matrix[128 * i : 128 * i + 128, 128 * j : 128 * j + 128] for j in range(4)]
        cells[i] = blocks[i]
        lines.append(jnp.concatenate(cells, axis=1))
    return jnp.concatenate(lines, axis=0)


def diagonals(matrix):
    return [matrix[128 * i : 128 * i + 128, 128 * i : 128 * i + 128] for i in range(4)]


def make_pair(g, store):
    rows = lax.broadcasted_iota(jnp.int32, (128, 128), 0)
    cols = lax.broadcasted_iota(jnp.int32, (128, 128), 1)
    diag = rows == cols
    unit = diag.astype(jnp.float32)
    plain = ((1,), (0,))
    both = (0, 1)
    quarter = jnp.asarray(-0.25, jnp.bfloat16)

    def narrow(value):
        return value.astype(jnp.bfloat16)

    stats = [narrow(dot(g, g, ((1 - kind,), (1 - kind,)))) for kind in both]
    coupled, first, scale = [None] * 2, [None] * 2, [None] * 2
    for kind in both:
        sym = stats[kind].astype(jnp.float32)
        trace = sum(jnp.where(diag, block, 0.0) for block in diagonals(sym))
        mean = jnp.sum(trace, keepdims=True) / BLK
        norm = jnp.sqrt(jnp.sum(sym * sym, keepdims=True) + (0.21 * BLK) * mean * mean + 1e-06)
        grow = 4.0 / norm
        spread = sym * grow
        ends = [block + unit * (0.1 * mean * grow) for block in diagonals(spread)]
        body_b = narrow(spread)
        coupled[kind] = patched(body_b, [narrow(block) for block in ends])
        first[kind] = patched(body_b * quarter, [narrow(1.25 * unit - 0.25 * block) for block in ends])
        scale[kind] = jnp.sqrt(jnp.sqrt(grow)) * jnp.sqrt(jnp.sqrt(1.1 * mean))
    two = [narrow(dot(first[kind], first[kind], plain)) for kind in both]
    four = [narrow(dot(two[kind], two[kind], plain)) for kind in both]
    second = []
    for kind in both:
        after = dot(four[kind], coupled[kind], plain) * -0.25
        second.append(patched(narrow(after), [narrow(1.25 * unit + block) for block in diagonals(after)]))
    for kind in both:
        top = dot(first[kind][:256], second[kind], plain) * scale[kind]
        low = dot(first[kind][256:], second[kind][:, 256:], plain) * scale[kind]

        def block(i, j):
            if i < 2:
                return top[128 * i : 128 * i + 128, 128 * j : 128 * j + 128]
            return low[128 * (i - 2) : 128 * (i - 1), 128 * (j - 2) : 128 * (j - 1)]

        for n, (i, j) in enumerate(OFF):
            store(kind, 128 * n, narrow(block(i, j)))
        spare = jnp.zeros((16, 128), jnp.float32)
        for n in (0, 1):
            lead, tail = block(2 * n, 2 * n), block(2 * n + 1, 2 * n + 1)
            store(kind, 128 * (6 + n), narrow(jnp.where(rows <= cols, lead, tail)))
            line = jnp.sum(jnp.where(diag, tail, 0.0), axis=0, keepdims=True)
            spare = jnp.where(rows[:16] == n, line, spare)
        store(kind, 1024, narrow(spare))


def roots_kernel(g_ref, out_ref):
    def store(kind, at, value):
        out_ref[kind, at : at + value.shape[0], :] = value

    make_pair(g_ref[...], store)


def roots(grad):
    return pl.pallas_call(
        roots_kernel,
        grid=(4,),
        out_shape=jax.ShapeDtypeStruct((STATS, ROWS, 128), jnp.bfloat16),
        in_specs=[pl.BlockSpec((BLK, BLK), lambda i: (i // 2, i % 2))],
        out_specs=pl.BlockSpec((2, ROWS, 128), lambda i: (i, 0, 0)),
        compiler_params=pltpu.CompilerParams(vmem_limit_bytes=LIMIT),
        name="roots",
    )(grad)


def hop_matrix():
    out = np.zeros((4, 128, 256), np.float32)
    for lane in range(128):
        g, n = lane // 16, lane % 16
        z, x = n // 4, n % 4
        targets = (z * 4 + (x + 1) % 4, z * 4 + (x + 3) % 4, (z + 1) % 4 * 4 + x, (z + 3) % 4 * 4 + x)
        for link, to in enumerate(targets):
            out[link, lane, g * 16 + to] = 1.0
            out[link, lane, 128 + g * 16 + to] = link
    return out.reshape(512, 256)


def make_plan(own_ref, hop_ref, out_ref):
    lane = lax.broadcasted_iota(jnp.int32, (128, 128), 1)
    item = lax.broadcasted_iota(jnp.int32, (128, 128), 0)
    node = lane & 15
    group = lax.broadcasted_iota(jnp.int32, (8, 128), 1) // 16
    parts = []
    for c in range(16):
        part = jnp.zeros((8, 128), jnp.int32)
        for row in range(8):
            part = jnp.where(group == row, own_ref[c // 4, c % 4, row], part)
        parts.append(part)
    dest = jnp.concatenate(parts, axis=0)
    home = dest == node
    dx = (dest - node) & 3
    dz = ((dest >> 2) - (node >> 2)) & 3
    wants = ((dx == 1) | (dx == 2), dx >= 2, (dz == 1) | (dz == 2), dz >= 2)
    ways = sum(w.astype(jnp.int32) for w in wants)
    far = jnp.where(dx == 3, 1, dx) + jnp.where(dz == 3, 1, dz)
    key = ((4 - ways + far) * 1024 + (128 - item)).astype(jnp.float32)
    keys = [jnp.where(w, key, 0.0) for w in wants]
    origin = ((item >> 3) == node).astype(jnp.float32)
    late = (item & 7) >= 4
    here = jnp.where(late, 0.0, origin)
    slot = (item & 7).astype(jnp.float32)
    homef = home.astype(jnp.float32)
    hop = hop_ref[...]
    out_ref[...] = jnp.zeros_like(out_ref)
    for t in range(STEPS_MAX):
        moves = [None] * 4
        if t == 1:
            here = here + jnp.where(late, origin, 0.0)
        for link in (0, 2, 1, 3):
            v = keys[link] * here
            best = jnp.max(v, axis=0, keepdims=True)
            win = jnp.where((v == best) & (v > 0.0), 1.0, 0.0)
            here = here - win
            pick = jnp.sum(win * slot, axis=0, keepdims=True)
            out_ref[4 * t + link : 4 * t + link + 1, :] = pick.astype(jnp.int32)
            moves[link] = win.astype(jnp.bfloat16)
        landed = dot(jnp.concatenate(moves, axis=1), hop, ((1,), (0,)))
        new = landed[:, :128]
        here = here + new
        slot = jnp.where(new > 0.5, landed[:, 128:] + (STATS + 4.0 * t), slot)
        if t + 1 in STEPS:
            row = 4 * STEPS_MAX + MOST + STEPS.index(t + 1)
            done = jnp.sum(here * homef, keepdims=True)
            out_ref[row : row + 1, :] = jnp.broadcast_to(done, (1, 128)).astype(jnp.int32)
    below = (lane < item).astype(jnp.bfloat16)
    rank = dot(below, home.astype(jnp.bfloat16), ((1,), (0,)))
    for n in range(MOST):
        mine = jnp.where(home & (rank == float(n)), slot + 1.0, 0.0)
        row = 4 * STEPS_MAX + n
        out_ref[row : row + 1, :] = jnp.sum(mine, axis=0, keepdims=True).astype(jnp.int32) - 1


def deliver_kernel(steps, table, grad, out, pool, recv, stage, ss, rs):
    r, c = lax.axis_index("dp"), lax.axis_index("mp")
    z, x = c // 4, c % 4
    me = r * 16 + c
    peers = (
        (r, z * 4 + (x + 1) % 4),
        (r, z * 4 + (x + 3) % 4),
        (r, (z + 1) % 4 * 4 + x),
        (r, (z + 3) % 4 * 4 + x),
    )

    def work(p):
        def pair(q, carry):
            def store(kind, at, value):
                pool[4 * p + 2 * q + kind, at : at + value.shape[0], :] = value

            cols = pl.ds(pl.multiple_of(q * BLK, BLK), BLK)
            make_pair(grad[BLK * p : BLK * p + BLK, cols], store)
            return carry

        lax.fori_loop(0, 2, pair, 0)

    def copy(t, link, half):
        return pltpu.make_async_remote_copy(
            src_ref=stage.at[t % 2, link, HALVES[half]],
            dst_ref=recv.at[t, link, HALVES[half]],
            send_sem=ss.at[t % 2, link, half],
            recv_sem=rs.at[t, link, half],
            device_id=peers[link],
            device_id_type=MESH,
        )

    def land(t, half):
        for link in range(4):
            copy(t, link, half).wait_recv()
            pool[STATS + 4 * t + link, HALVES[half], :] = recv[t, link, HALVES[half], :]

    def push(t, half):
        for link in range(4):
            stage[t % 2, link, HALVES[half], :] = pool[table[4 * t + link, me], HALVES[half], :]
            copy(t, link, half).start()

    def settle(t, half):
        for link in range(4):
            copy(t, link, half).wait_send()

    barrier = pltpu.get_barrier_semaphore()
    for dev in peers:
        pl.semaphore_signal(barrier, inc=1, device_id=dev, device_id_type=MESH)
    work(0)
    pl.semaphore_wait(barrier, 4)
    push(0, 0)
    push(0, 1)
    work(1)
    for half in (0, 1):
        land(0, half)
        push(1, half)

    def step(t, carry):
        for half in (0, 1):
            land(t - 1, half)
            settle(t - 2, half)
            push(t, half)
        return carry

    lax.fori_loop(2, steps, step, 0)
    for half in (0, 1):
        land(steps - 1, half)
    for t in (steps - 2, steps - 1):
        for half in (0, 1):
            settle(t, half)
    for n in range(MOST):
        at = table[4 * STEPS_MAX + n, me]
        block = pool[jnp.maximum(at, 0)]
        keep = (at >= 0).astype(jnp.bfloat16)
        out[n] = block * keep


HALVES = (pl.ds(0, 528), pl.ds(528, 512))


def deliver(steps, table, grad):
    return pl.pallas_call(
        functools.partial(deliver_kernel, steps),
        out_shape=jax.ShapeDtypeStruct((MOST, ROWS, 128), jnp.bfloat16),
        in_specs=[pl.BlockSpec(memory_space=pltpu.SMEM), pl.BlockSpec(memory_space=pltpu.VMEM)],
        out_specs=pl.BlockSpec(memory_space=pltpu.VMEM),
        scratch_shapes=[
            pltpu.VMEM((STATS + 4 * steps, ROWS, 128), jnp.bfloat16),
            pltpu.VMEM((steps, 4, ROWS, 128), jnp.bfloat16),
            pltpu.VMEM((2, 4, ROWS, 128), jnp.bfloat16),
            pltpu.SemaphoreType.DMA((2, 4, 2)),
            pltpu.SemaphoreType.DMA((steps, 4, 2)),
        ],
        compiler_params=pltpu.CompilerParams(
            collective_id=steps, has_side_effects=True, vmem_limit_bytes=LIMIT
        ),
        name="deliver",
    )(table, grad)


def deliver_any(owners, packed):
    myself = lax.axis_index("mp")
    lists = lax.all_gather(owners, "mp", axis=1, tiled=True)[0]
    mine = lists[myself]
    count = lists.shape[0]
    match = (mine[None, :] == jnp.arange(count, dtype=jnp.int32)[:, None]).astype(jnp.int32)
    rank = jnp.cumsum(match, axis=1) - match
    select = (match[:, None, :] > 0) & (rank[:, None, :] == jnp.arange(CAP, dtype=jnp.int32)[None, :, None])
    index = jnp.sum(select.astype(jnp.int32) * jnp.arange(STATS, dtype=jnp.int32), axis=2)
    outgoing = packed[index.reshape(-1)].reshape(count, CAP, ROWS, 128)
    received = lax.all_to_all(outgoing, "mp", split_axis=0, concat_axis=0, tiled=True)
    counts = jnp.sum((lists == myself).astype(jnp.int32), axis=1)
    valid = (jnp.arange(CAP, dtype=jnp.int32)[None, :] < counts[:, None]).reshape(-1).astype(jnp.int32)
    before = jnp.cumsum(valid) - valid
    chosen = (valid[None, :] > 0) & (before[None, :] == jnp.arange(MOST, dtype=jnp.int32)[:, None])
    index = jnp.sum(chosen.astype(jnp.int32) * jnp.arange(count * CAP, dtype=jnp.int32), axis=1)
    picked = received.reshape(count * CAP, ROWS, 128)[index]
    return jnp.where(jnp.any(chosen, axis=1)[:, None, None], picked, jnp.zeros_like(picked))


def unpack_kernel(in_ref, out_ref):
    rows = lax.broadcasted_iota(jnp.int32, (128, 128), 0)
    cols = lax.broadcasted_iota(jnp.int32, (128, 128), 1)
    unit = (rows == cols).astype(jnp.bfloat16)
    for m in range(PAIR):
        flipped = dot(unit, in_ref[m, :1024, :], ((1,), (1,)))
        for n, (i, j) in enumerate(OFF):
            out_ref[m, 128 * i : 128 * i + 128, 128 * j : 128 * j + 128] = in_ref[m, 128 * n : 128 * n + 128, :]
            turned = flipped[:, 128 * n : 128 * n + 128].astype(jnp.bfloat16)
            out_ref[m, 128 * j : 128 * j + 128, 128 * i : 128 * i + 128] = turned
        spare = in_ref[m, 1024:, :].astype(jnp.float32)
        for n in (0, 1):
            both = in_ref[m, 128 * (6 + n) : 128 * (7 + n), :].astype(jnp.float32)
            other = flipped[:, 128 * (6 + n) : 128 * (7 + n)]
            first = jnp.where(rows <= cols, both, other)
            second = jnp.where(rows > cols, both, other)
            second = jnp.where(rows == cols, spare[n : n + 1, :], second)
            for half, value in ((0, first), (1, second)):
                at = 128 * (2 * n + half)
                out_ref[m, at : at + 128, at : at + 128] = value.astype(jnp.bfloat16)


PAIR = 2


def unpack(packed):
    return pl.pallas_call(
        unpack_kernel,
        grid=(MOST // PAIR,),
        out_shape=jax.ShapeDtypeStruct((MOST, BLK, BLK), jnp.bfloat16),
        in_specs=[pl.BlockSpec((PAIR, ROWS, 128), lambda i: (i, 0, 0))],
        out_specs=pl.BlockSpec((PAIR, BLK, BLK), lambda i: (i, 0, 0)),
        compiler_params=pltpu.CompilerParams(vmem_limit_bytes=LIMIT),
        name="unpack",
    )(packed)


def body(hidden_acts, out_grad, owners):
    grad, table = gather(hidden_acts, out_grad, owners)
    total = 8 * 128
    done = [table[4 * STEPS_MAX + MOST + n, 0] == total for n in range(len(STEPS))]
    which = jnp.asarray(len(STEPS), jnp.int32)
    for n in reversed(range(len(STEPS))):
        which = jnp.where(done[n], n, which)
    ways = [functools.partial(deliver, steps, table, grad) for steps in STEPS]
    arrived = lax.switch(which, ways + [lambda: deliver_any(owners, roots(grad))])
    return unpack(arrived)[None, None]


def solution(mesh):
    placed = (P("dp", "mp"), P("dp", None), P("dp", "mp", None))
    return jax.shard_map(
        body, mesh=mesh, in_specs=placed, out_specs=P("dp", "mp", None, None, None), check_vma=False
    )
```

```python
import functools

import jax
import jax.numpy as jnp
import numpy as np
from jax import lax
from jax.experimental import pallas as pl
from jax.experimental.pallas import tpu as pltpu
from jax.sharding import PartitionSpec as P

MESH = pl.DeviceIdType.MESH
BLK = 512
STATS = 8
CAP = 2
MOST = 12
ROWS = 1040
STEPS = (8, 9, 10)
STEPS_MAX = STEPS[-1]
TABLE = 4 * STEPS_MAX + MOST + 4
OFF = ((0, 1), (0, 2), (0, 3), (1, 2), (1, 3), (2, 3))
LIMIT = 56 * 1024 * 1024


def gather_kernel(own, hid, og, hop_ref, packed_ref, grad_ref, table_ref, hid_all, og_all, own_rows, own_all, tile_ref, raw, acc, lead, ss, rs, ls, rs1, rso):
    r, c = lax.axis_index("dp"), lax.axis_index("mp")
    y, k = r // 2, r % 2
    z, x = c // 4, c % 4
    sib = (2 * y + 1 - k, c)

    def yn(dy, core):
        return (2 * ((y + dy) % 4) + core, c)

    a = z * (1 - k) + x * k
    b = x * (1 - k) + z * k

    def plane(aa, bb):
        zz = aa * (1 - k) + bb * k
        xx = bb * (1 - k) + aa * k
        return (r, zz * 4 + xx)

    bp, bm = plane(a, (b + 1) % 4), plane(a, (b + 3) % 4)
    ap, am = plane((a + 1) % 4, b), plane((a + 3) % 4, b)
    rows = [sib] + [yn(dy, core) for dy in (1, 2, 3) for core in (0, 1)]
    along_x = [(r, z * 4 + (x + n) % 4) for n in (1, 2, 3)]
    along_z = [(r, (z + n) % 4 * 4 + x) for n in (1, 2, 3)]

    def columns(row):
        return pl.ds(pl.multiple_of(row * 1024, 1024), 1024)

    l0 = pltpu.make_async_copy(og.at[:, :, :, columns(r)], og_all.at[0, k], ls.at[0])
    l1 = pltpu.make_async_copy(hid, raw, ls.at[1])
    l1.start()
    l0.start()

    barrier = pltpu.get_barrier_semaphore()
    partners = rows + along_x + along_z
    for dev in partners:
        pl.semaphore_signal(barrier, inc=1, device_id=dev, device_id_type=MESH)
    pl.semaphore_wait(barrier, len(partners))

    sent = []

    def send(src, dst, dev, landed=None):
        i = len(sent)
        landed = rs.at[i] if landed is None else landed
        copy = pltpu.make_async_remote_copy(
            src_ref=src, dst_ref=dst, send_sem=ss.at[i], recv_sem=landed, device_id=dev, device_id_type=MESH
        )
        copy.start()
        sent.append(copy)
        return copy

    def await_copy(ref, sem):
        pltpu.make_async_copy(ref, ref, sem).wait()

    line = lax.broadcasted_iota(jnp.int32, (8, 128), 0)
    lists = jnp.zeros((8, 128), jnp.int32)
    for j in range(STATS):
        lists = jnp.where(line == j, own[0, 0, j], lists)
    tile_ref[...] = lists
    own_rows[r] = lists
    for n, dev in enumerate(rows):
        send(tile_ref, own_rows.at[r], dev, rso.at[r])
    for dy in (1, 3, 2):
        for core in (0, 1):
            aa = z * (1 - core) + x * core
            bb = x * (1 - core) + z * core
            row = 2 * ((y + dy) % 4) + core
            send(og.at[aa, bb, :, columns(row)], og_all.at[4 - dy, k, aa, bb], yn(dy, core), rs1.at[4 - dy, k])
    sib_og = send(og.at[:, :, :, columns(2 * y + 1 - k)], og_all.at[0, k], sib)
    l1.wait()
    for p in (0, 1):
        hid_all[0, k, p] = raw[:, 512 * p : 512 * p + 512].T
    sib_hid = send(hid_all.at[0, k], hid_all.at[0, k], sib)

    sa, sb, ra, rb, hp, hm, fw = ({} for _ in range(7))

    def stage_a(d):
        for core in (0, 1):
            await_copy(og_all.at[d, core, a, b], rs1.at[d, core])
        sa[d, 0] = send(og_all.at[d, :, a, b], og_all.at[d, :, a, b], bp)
        sa[d, 1] = send(og_all.at[d, :, a, b], og_all.at[d, :, a, b], bm)

    def relay_a(d):
        sa[d, 0].wait_recv()
        ra[d, 0] = send(og_all.at[d, 0, a, (b + 3) % 4], og_all.at[d, 0, a, (b + 3) % 4], bp)
        sa[d, 1].wait_recv()
        ra[d, 1] = send(og_all.at[d, 1, a, (b + 1) % 4], og_all.at[d, 1, a, (b + 1) % 4], bm)

    def stage_b(d):
        ra[d, 0].wait_recv()
        ra[d, 1].wait_recv()
        sb[d, 0] = send(og_all.at[d, :, a], og_all.at[d, :, a], ap)
        sb[d, 1] = send(og_all.at[d, :, a], og_all.at[d, :, a], am)

    def relay_b(d):
        sb[d, 0].wait_recv()
        rb[d, 0] = send(og_all.at[d, 0, (a + 3) % 4], og_all.at[d, 0, (a + 3) % 4], ap)
        sb[d, 1].wait_recv()
        rb[d, 1] = send(og_all.at[d, 1, (a + 1) % 4], og_all.at[d, 1, (a + 1) % 4], am)

    def part(ref, h, p):
        return ref.at[p, :, pl.ds(256 * h, 256)]

    def send_own(way, h, p):
        if way == 0:
            hp[h, p] = send(part(hid_all.at[0, k], h, p), part(hid_all.at[3, k], h, p), yn(1, k))
        else:
            hm[h, p] = send(part(hid_all.at[0, k], h, p), part(hid_all.at[1, k], h, p), yn(3, k))

    def forward(d, h, p):
        ref = part(hid_all.at[d, k], h, p)
        fw[d, h, p] = send(ref, ref, sib)

    def arrive(way, h, p):
        d = 3 if way == 0 else 1
        (hp if way == 0 else hm)[h, p].wait_recv()
        if h == way:
            relay[way, p] = send(part(hid_all.at[d, k], h, p), part(hid_all.at[2, k], h, p), yn(1 if way == 0 else 3, k))
        forward(d, h, p)

    def relayed(way, p):
        relay[way, p].wait_recv()
        forward(2, way, p)

    def whole(d, p):
        fw[d, 0, p].wait_recv()
        fw[d, 1, p].wait_recv()

    def whole_og(d):
        rb[d, 0].wait_recv()
        rb[d, 1].wait_recv()

    def add_products(d, p):
        def tile(i, carry):
            at = pl.ds(pl.multiple_of(512 * p + i * 256, 256), 256)
            here = pl.ds(pl.multiple_of(i * 256, 256), 256)
            left = jnp.concatenate([hid_all[d, core, p, here, :] for core in (0, 1)], axis=1)
            prod = dot(left, og_all[d].reshape(1024, 1024), ((1,), (0,)))
            if d == 0:
                acc[at, :] = prod
            elif d == 2:
                ref = lead if p == 0 else grad_ref
                ref[here, :] = (acc[at, :] + prod).astype(jnp.bfloat16)
            else:
                acc[at, :] += prod
            return carry

        lax.fori_loop(0, 2, tile, 0)

    relay = {}
    stage_a(1)
    stage_a(3)
    send_own(0, 0, 0)
    send_own(1, 1, 0)
    send_own(0, 1, 0)
    send_own(1, 0, 0)
    stage_a(2)
    relay_a(1)
    relay_a(3)
    stage_b(1)
    group = lax.broadcasted_iota(jnp.int32, (8, 128), 1) // 16
    for dy in range(8):
        pl.when(dy != r)(lambda dy=dy: await_copy(own_rows.at[dy], rso.at[dy]))
    for dy in range(8):
        lists = jnp.where(group == dy, own_rows[dy], lists)
    own_all[z, x] = lists
    own_x = [send(own_all.at[z, x], own_all.at[z, x], dev) for dev in along_x]
    relay_a(2)
    stage_b(3)
    for copy in own_x:
        copy.wait_recv()
    own_z = [send(own_all.at[z], own_all.at[z], dev) for dev in along_z]
    stage_b(2)
    l0.wait()
    sib_og.wait_recv()
    sib_hid.wait_recv()
    arrive(0, 0, 0)
    send_own(0, 0, 1)
    arrive(1, 1, 0)
    send_own(1, 1, 1)
    add_products(0, 0)
    add_products(0, 1)
    relay_b(1)
    arrive(0, 1, 0)
    send_own(0, 1, 1)
    arrive(1, 0, 0)
    send_own(1, 0, 1)
    for copy in own_z:
        copy.wait_recv()
    relay_b(3)
    relayed(0, 0)
    relayed(1, 0)
    make_plan(own_all, hop_ref, table_ref)
    arrive(0, 0, 1)
    arrive(1, 1, 1)
    relay_b(2)
    whole_og(1)
    whole(1, 0)
    add_products(1, 0)
    arrive(0, 1, 1)
    arrive(1, 0, 1)
    whole_og(3)
    whole(3, 0)
    add_products(3, 0)
    whole(1, 1)
    add_products(1, 1)
    whole_og(2)
    whole(2, 0)
    add_products(2, 0)
    relayed(0, 1)
    relayed(1, 1)
    whole(3, 1)
    add_products(3, 1)

    def pair(q, carry):
        def store(kind, at, value):
            packed_ref[2 * q + kind, at : at + value.shape[0], :] = value

        make_pair(lead[:, pl.ds(pl.multiple_of(q * BLK, BLK), BLK)], store)
        return carry

    lax.fori_loop(0, 2, pair, 0)
    whole(2, 1)
    add_products(2, 1)
    for copy in sent:
        copy.wait_send()


SENDS = 7 + 6 + 2 + 8 + 6 + 6 + 6 + 6 + 4 + 12 + 3 + 3


def gather(hid, og, own):
    return pl.pallas_call(
        gather_kernel,
        out_shape=(
            jax.ShapeDtypeStruct((4, ROWS, 128), jnp.bfloat16),
            jax.ShapeDtypeStruct((512, 1024), jnp.bfloat16),
            jax.ShapeDtypeStruct((TABLE, 128), jnp.int32),
        ),
        in_specs=[
            pl.BlockSpec(memory_space=pltpu.SMEM),
            pl.BlockSpec(memory_space=pl.ANY),
            pl.BlockSpec(memory_space=pl.ANY),
            pl.BlockSpec(memory_space=pltpu.VMEM),
        ],
        out_specs=(pl.BlockSpec(memory_space=pltpu.VMEM),) * 3,
        scratch_shapes=[
            pltpu.VMEM((4, 2, 2, 512, 512), jnp.bfloat16),
            pltpu.VMEM((4, 2, 4, 4, 32, 1024), jnp.bfloat16),
            pltpu.VMEM((8, 8, 128), jnp.int32),
            pltpu.VMEM((4, 4, 8, 128), jnp.int32),
            pltpu.VMEM((8, 128), jnp.int32),
            pltpu.VMEM((512, 1024), jnp.bfloat16),
            pltpu.VMEM((1024, 1024), jnp.float32),
            pltpu.VMEM((512, 1024), jnp.bfloat16),
            pltpu.SemaphoreType.DMA((SENDS,)),
            pltpu.SemaphoreType.DMA((SENDS,)),
            pltpu.SemaphoreType.DMA((2,)),
            pltpu.SemaphoreType.DMA((4, 2)),
            pltpu.SemaphoreType.DMA((8,)),
        ],
        compiler_params=pltpu.CompilerParams(collective_id=0, has_side_effects=True, vmem_limit_bytes=LIMIT),
        name="gather",
    )(own, hid, og.reshape(4, 4, 32, 8192), jnp.asarray(hop_matrix(), jnp.bfloat16))


def dot(left, right, dims):
    return lax.dot_general(left, right, (dims, ((), ())), preferred_element_type=jnp.float32)


def patched(matrix, blocks):
    lines = []
    for i in range(4):
        cells = [matrix[128 * i : 128 * i + 128, 128 * j : 128 * j + 128] for j in range(4)]
        cells[i] = blocks[i]
        lines.append(jnp.concatenate(cells, axis=1))
    return jnp.concatenate(lines, axis=0)


def diagonals(matrix):
    return [matrix[128 * i : 128 * i + 128, 128 * i : 128 * i + 128] for i in range(4)]


def make_pair(g, store):
    rows = lax.broadcasted_iota(jnp.int32, (128, 128), 0)
    cols = lax.broadcasted_iota(jnp.int32, (128, 128), 1)
    diag = rows == cols
    unit = diag.astype(jnp.float32)
    plain = ((1,), (0,))
    both = (0, 1)
    quarter = jnp.asarray(-0.25, jnp.bfloat16)

    def narrow(value):
        return value.astype(jnp.bfloat16)

    stats = [narrow(dot(g, g, ((1 - kind,), (1 - kind,)))) for kind in both]
    coupled, first, scale = [None] * 2, [None] * 2, [None] * 2
    for kind in both:
        sym = stats[kind].astype(jnp.float32)
        trace = sum(jnp.where(diag, block, 0.0) for block in diagonals(sym))
        mean = jnp.sum(trace, keepdims=True) / BLK
        norm = jnp.sqrt(jnp.sum(sym * sym, keepdims=True) + (0.21 * BLK) * mean * mean + 1e-06)
        grow = 4.0 / norm
        spread = sym * grow
        ends = [block + unit * (0.1 * mean * grow) for block in diagonals(spread)]
        body_b = narrow(spread)
        coupled[kind] = patched(body_b, [narrow(block) for block in ends])
        first[kind] = patched(body_b * quarter, [narrow(1.25 * unit - 0.25 * block) for block in ends])
        scale[kind] = jnp.sqrt(jnp.sqrt(grow)) * jnp.sqrt(jnp.sqrt(1.1 * mean))
    two = [narrow(dot(first[kind], first[kind], plain)) for kind in both]
    four = [narrow(dot(two[kind], two[kind], plain)) for kind in both]
    second = []
    for kind in both:
        after = dot(four[kind], coupled[kind], plain) * -0.25
        second.append(patched(narrow(after), [narrow(1.25 * unit + block) for block in diagonals(after)]))
    for kind in both:
        top = dot(first[kind][:256], second[kind], plain) * scale[kind]
        low = dot(first[kind][256:], second[kind][:, 256:], plain) * scale[kind]

        def block(i, j):
            if i < 2:
                return top[128 * i : 128 * i + 128, 128 * j : 128 * j + 128]
            return low[128 * (i - 2) : 128 * (i - 1), 128 * (j - 2) : 128 * (j - 1)]

        for n, (i, j) in enumerate(OFF):
            store(kind, 128 * n, narrow(block(i, j)))
        spare = jnp.zeros((16, 128), jnp.float32)
        for n in (0, 1):
            lead, tail = block(2 * n, 2 * n), block(2 * n + 1, 2 * n + 1)
            store(kind, 128 * (6 + n), narrow(jnp.where(rows <= cols, lead, tail)))
            line = jnp.sum(jnp.where(diag, tail, 0.0), axis=0, keepdims=True)
            spare = jnp.where(rows[:16] == n, line, spare)
        store(kind, 1024, narrow(spare))


def roots_kernel(g_ref, out_ref):
    def store(kind, at, value):
        out_ref[kind, at : at + value.shape[0], :] = value

    make_pair(g_ref[...], store)


def roots(grad):
    return pl.pallas_call(
        roots_kernel,
        grid=(2,),
        out_shape=jax.ShapeDtypeStruct((4, ROWS, 128), jnp.bfloat16),
        in_specs=[pl.BlockSpec((BLK, BLK), lambda i: (0, i))],
        out_specs=pl.BlockSpec((2, ROWS, 128), lambda i: (i, 0, 0)),
        compiler_params=pltpu.CompilerParams(vmem_limit_bytes=LIMIT),
        name="roots",
    )(grad)


def hop_matrix():
    out = np.zeros((4, 128, 256), np.float32)
    for lane in range(128):
        g, n = lane // 16, lane % 16
        z, x = n // 4, n % 4
        targets = (z * 4 + (x + 1) % 4, z * 4 + (x + 3) % 4, (z + 1) % 4 * 4 + x, (z + 3) % 4 * 4 + x)
        for link, to in enumerate(targets):
            out[link, lane, g * 16 + to] = 1.0
            out[link, lane, 128 + g * 16 + to] = link
    return out.reshape(512, 256)


def make_plan(own_ref, hop_ref, out_ref):
    lane = lax.broadcasted_iota(jnp.int32, (128, 128), 1)
    item = lax.broadcasted_iota(jnp.int32, (128, 128), 0)
    node = lane & 15
    dest = jnp.concatenate([own_ref[c // 4, c % 4] for c in range(16)], axis=0)
    home = dest == node
    dx = (dest - node) & 3
    dz = ((dest >> 2) - (node >> 2)) & 3
    wants = ((dx == 1) | (dx == 2), dx >= 2, (dz == 1) | (dz == 2), dz >= 2)
    ways = sum(w.astype(jnp.int32) for w in wants)
    far = jnp.where(dx == 3, 1, dx) + jnp.where(dz == 3, 1, dz)
    key = ((4 - ways + far) * 1024 + (128 - item)).astype(jnp.float32)
    keys = [jnp.where(w, key, 0.0) for w in wants]
    origin = ((item >> 3) == node).astype(jnp.float32)
    late = (item & 7) >= 4
    here = jnp.where(late, 0.0, origin)
    slot = (item & 7).astype(jnp.float32)
    homef = home.astype(jnp.float32)
    hop = hop_ref[...]
    out_ref[...] = jnp.zeros_like(out_ref)
    for t in range(STEPS_MAX):
        moves = [None] * 4
        if t == 1:
            here = here + jnp.where(late, origin, 0.0)
        for link in (0, 2, 1, 3):
            v = keys[link] * here
            best = jnp.max(v, axis=0, keepdims=True)
            win = jnp.where((v == best) & (v > 0.0), 1.0, 0.0)
            here = here - win
            pick = jnp.sum(win * slot, axis=0, keepdims=True)
            out_ref[4 * t + link : 4 * t + link + 1, :] = pick.astype(jnp.int32)
            moves[link] = win.astype(jnp.bfloat16)
        landed = dot(jnp.concatenate(moves, axis=1), hop, ((1,), (0,)))
        new = landed[:, :128]
        here = here + new
        slot = jnp.where(new > 0.5, landed[:, 128:] + (STATS + 4.0 * t), slot)
        if t + 1 in STEPS:
            row = 4 * STEPS_MAX + MOST + STEPS.index(t + 1)
            done = jnp.sum(here * homef, keepdims=True)
            out_ref[row : row + 1, :] = jnp.broadcast_to(done, (1, 128)).astype(jnp.int32)
    below = (lane < item).astype(jnp.bfloat16)
    rank = dot(below, home.astype(jnp.bfloat16), ((1,), (0,)))
    for n in range(MOST):
        mine = jnp.where(home & (rank == float(n)), slot + 1.0, 0.0)
        row = 4 * STEPS_MAX + n
        out_ref[row : row + 1, :] = jnp.sum(mine, axis=0, keepdims=True).astype(jnp.int32) - 1


def deliver_kernel(steps, table, packed, grad, out, pool, recv, stage, ss, rs):
    r, c = lax.axis_index("dp"), lax.axis_index("mp")
    z, x = c // 4, c % 4
    me = r * 16 + c
    peers = (
        (r, z * 4 + (x + 1) % 4),
        (r, z * 4 + (x + 3) % 4),
        (r, (z + 1) % 4 * 4 + x),
        (r, (z + 3) % 4 * 4 + x),
    )

    def pair(q, carry):
        def store(kind, at, value):
            pool[4 + 2 * q + kind, at : at + value.shape[0], :] = value

        make_pair(grad[:, pl.ds(pl.multiple_of(q * BLK, BLK), BLK)], store)
        return carry

    def copy(t, link, half):
        return pltpu.make_async_remote_copy(
            src_ref=stage.at[t % 2, link, HALVES[half]],
            dst_ref=recv.at[t, link, HALVES[half]],
            send_sem=ss.at[t % 2, link, half],
            recv_sem=rs.at[t, link, half],
            device_id=peers[link],
            device_id_type=MESH,
        )

    def land(t, half):
        for link in range(4):
            copy(t, link, half).wait_recv()
            pool[STATS + 4 * t + link, HALVES[half], :] = recv[t, link, HALVES[half], :]

    def push(t, half):
        for link in range(4):
            stage[t % 2, link, HALVES[half], :] = pool[table[4 * t + link, me], HALVES[half], :]
            copy(t, link, half).start()

    def settle(t, half):
        for link in range(4):
            copy(t, link, half).wait_send()

    barrier = pltpu.get_barrier_semaphore()
    for dev in peers:
        pl.semaphore_signal(barrier, inc=1, device_id=dev, device_id_type=MESH)
    pool[:4] = packed[...]
    pl.semaphore_wait(barrier, 4)
    push(0, 0)
    push(0, 1)
    lax.fori_loop(0, 2, pair, 0)
    for half in (0, 1):
        land(0, half)
        push(1, half)

    def step(t, carry):
        for half in (0, 1):
            land(t - 1, half)
            settle(t - 2, half)
            push(t, half)
        return carry

    lax.fori_loop(2, steps, step, 0)
    for half in (0, 1):
        land(steps - 1, half)
    for t in (steps - 2, steps - 1):
        for half in (0, 1):
            settle(t, half)
    for n in range(MOST):
        at = table[4 * STEPS_MAX + n, me]
        block = pool[jnp.maximum(at, 0)]
        keep = (at >= 0).astype(jnp.bfloat16)
        out[n] = block * keep


HALVES = (pl.ds(0, 528), pl.ds(528, 512))


def deliver(steps, table, packed, grad):
    return pl.pallas_call(
        functools.partial(deliver_kernel, steps),
        out_shape=jax.ShapeDtypeStruct((MOST, ROWS, 128), jnp.bfloat16),
        in_specs=[pl.BlockSpec(memory_space=pltpu.SMEM)] + [pl.BlockSpec(memory_space=pltpu.VMEM)] * 2,
        out_specs=pl.BlockSpec(memory_space=pltpu.VMEM),
        scratch_shapes=[
            pltpu.VMEM((STATS + 4 * steps, ROWS, 128), jnp.bfloat16),
            pltpu.VMEM((steps, 4, ROWS, 128), jnp.bfloat16),
            pltpu.VMEM((2, 4, ROWS, 128), jnp.bfloat16),
            pltpu.SemaphoreType.DMA((2, 4, 2)),
            pltpu.SemaphoreType.DMA((steps, 4, 2)),
        ],
        compiler_params=pltpu.CompilerParams(
            collective_id=steps, has_side_effects=True, vmem_limit_bytes=LIMIT
        ),
        name="deliver",
    )(table, packed, grad)


def deliver_any(owners, packed):
    myself = lax.axis_index("mp")
    lists = lax.all_gather(owners, "mp", axis=1, tiled=True)[0]
    mine = lists[myself]
    count = lists.shape[0]
    match = (mine[None, :] == jnp.arange(count, dtype=jnp.int32)[:, None]).astype(jnp.int32)
    rank = jnp.cumsum(match, axis=1) - match
    select = (match[:, None, :] > 0) & (rank[:, None, :] == jnp.arange(CAP, dtype=jnp.int32)[None, :, None])
    index = jnp.sum(select.astype(jnp.int32) * jnp.arange(STATS, dtype=jnp.int32), axis=2)
    outgoing = packed[index.reshape(-1)].reshape(count, CAP, ROWS, 128)
    received = lax.all_to_all(outgoing, "mp", split_axis=0, concat_axis=0, tiled=True)
    counts = jnp.sum((lists == myself).astype(jnp.int32), axis=1)
    valid = (jnp.arange(CAP, dtype=jnp.int32)[None, :] < counts[:, None]).reshape(-1).astype(jnp.int32)
    before = jnp.cumsum(valid) - valid
    chosen = (valid[None, :] > 0) & (before[None, :] == jnp.arange(MOST, dtype=jnp.int32)[:, None])
    index = jnp.sum(chosen.astype(jnp.int32) * jnp.arange(count * CAP, dtype=jnp.int32), axis=1)
    picked = received.reshape(count * CAP, ROWS, 128)[index]
    return jnp.where(jnp.any(chosen, axis=1)[:, None, None], picked, jnp.zeros_like(picked))


def unpack_kernel(in_ref, out_ref):
    rows = lax.broadcasted_iota(jnp.int32, (128, 128), 0)
    cols = lax.broadcasted_iota(jnp.int32, (128, 128), 1)
    unit = (rows == cols).astype(jnp.bfloat16)
    for m in range(PAIR):
        flipped = dot(unit, in_ref[m, :1024, :], ((1,), (1,)))
        for n, (i, j) in enumerate(OFF):
            out_ref[m, 128 * i : 128 * i + 128, 128 * j : 128 * j + 128] = in_ref[m, 128 * n : 128 * n + 128, :]
            turned = flipped[:, 128 * n : 128 * n + 128].astype(jnp.bfloat16)
            out_ref[m, 128 * j : 128 * j + 128, 128 * i : 128 * i + 128] = turned
        spare = in_ref[m, 1024:, :].astype(jnp.float32)
        for n in (0, 1):
            both = in_ref[m, 128 * (6 + n) : 128 * (7 + n), :].astype(jnp.float32)
            other = flipped[:, 128 * (6 + n) : 128 * (7 + n)]
            first = jnp.where(rows <= cols, both, other)
            second = jnp.where(rows > cols, both, other)
            second = jnp.where(rows == cols, spare[n : n + 1, :], second)
            for half, value in ((0, first), (1, second)):
                at = 128 * (2 * n + half)
                out_ref[m, at : at + 128, at : at + 128] = value.astype(jnp.bfloat16)


PAIR = 2


def unpack(packed):
    return pl.pallas_call(
        unpack_kernel,
        grid=(MOST // PAIR,),
        out_shape=jax.ShapeDtypeStruct((MOST, BLK, BLK), jnp.bfloat16),
        in_specs=[pl.BlockSpec((PAIR, ROWS, 128), lambda i: (i, 0, 0))],
        out_specs=pl.BlockSpec((PAIR, BLK, BLK), lambda i: (i, 0, 0)),
        compiler_params=pltpu.CompilerParams(vmem_limit_bytes=LIMIT),
        name="unpack",
    )(packed)


def body(hidden_acts, out_grad, owners):
    packed, grad, table = gather(hidden_acts, out_grad, owners)
    total = 8 * 128
    done = [table[4 * STEPS_MAX + MOST + n, 0] == total for n in range(len(STEPS))]
    which = jnp.asarray(len(STEPS), jnp.int32)
    for n in reversed(range(len(STEPS))):
        which = jnp.where(done[n], n, which)
    ways = [functools.partial(deliver, steps, table, packed, grad) for steps in STEPS]
    arrived = lax.switch(which, ways + [lambda: deliver_any(owners, jnp.concatenate([packed, roots(grad)]))])
    return unpack(arrived)[None, None]


def solution(mesh):
    placed = (P("dp", "mp"), P("dp", None), P("dp", "mp", None))
    return jax.shard_map(
        body, mesh=mesh, in_specs=placed, out_specs=P("dp", "mp", None, None, None), check_vma=False
    )
```

```python
import functools

import jax
import jax.numpy as jnp
import numpy as np
from jax import lax
from jax.experimental import pallas as pl
from jax.experimental.pallas import tpu as pltpu
from jax.sharding import PartitionSpec as P

MESH = pl.DeviceIdType.MESH
BLK = 512
STATS = 8
CAP = 2
MOST = 12
ROWS = 1040
STEPS = (7, 8, 9)
STEPS_MAX = STEPS[-1]
WHICH = 4 * STEPS_MAX + MOST
TABLE = WHICH + 8
RULES = (((0, 2, 1, 3), 0), ((0, 2, 1, 3), 1), ((0, 2, 1, 3), 2), ((1, 3, 0, 2), 2))
OFF = ((0, 1), (0, 2), (0, 3), (1, 2), (1, 3), (2, 3))
LIMIT = 56 * 1024 * 1024


def gather_kernel(own, hid, og, hop_ref, packed_ref, grad_ref, table_ref, hid_all, og_all, own_rows, own_all, tile_ref, trials, counts, raw, acc, lead, ss, rs, ls, rs1, rso):
    r, c = lax.axis_index("dp"), lax.axis_index("mp")
    y, k = r // 2, r % 2
    z, x = c // 4, c % 4
    sib = (2 * y + 1 - k, c)

    def yn(dy, core):
        return (2 * ((y + dy) % 4) + core, c)

    a = z * (1 - k) + x * k
    b = x * (1 - k) + z * k

    def plane(aa, bb):
        zz = aa * (1 - k) + bb * k
        xx = bb * (1 - k) + aa * k
        return (r, zz * 4 + xx)

    bp, bm = plane(a, (b + 1) % 4), plane(a, (b + 3) % 4)
    ap, am = plane((a + 1) % 4, b), plane((a + 3) % 4, b)
    rows = [sib] + [yn(dy, core) for dy in (1, 2, 3) for core in (0, 1)]
    along_x = [(r, z * 4 + (x + n) % 4) for n in (1, 2, 3)]
    along_z = [(r, (z + n) % 4 * 4 + x) for n in (1, 2, 3)]

    def columns(row):
        return pl.ds(pl.multiple_of(row * 1024, 1024), 1024)

    l0 = pltpu.make_async_copy(og.at[:, :, :, columns(r)], og_all.at[0, k], ls.at[0])
    l1 = pltpu.make_async_copy(hid, raw, ls.at[1])
    l1.start()
    l0.start()

    barrier = pltpu.get_barrier_semaphore()
    partners = rows + along_x + along_z
    for dev in partners:
        pl.semaphore_signal(barrier, inc=1, device_id=dev, device_id_type=MESH)
    pl.semaphore_wait(barrier, len(partners))

    sent = []

    def send(src, dst, dev, landed=None):
        i = len(sent)
        landed = rs.at[i] if landed is None else landed
        copy = pltpu.make_async_remote_copy(
            src_ref=src, dst_ref=dst, send_sem=ss.at[i], recv_sem=landed, device_id=dev, device_id_type=MESH
        )
        copy.start()
        sent.append(copy)
        return copy

    def await_copy(ref, sem):
        pltpu.make_async_copy(ref, ref, sem).wait()

    line = lax.broadcasted_iota(jnp.int32, (8, 128), 0)
    lists = jnp.zeros((8, 128), jnp.int32)
    for j in range(STATS):
        lists = jnp.where(line == j, own[0, 0, j], lists)
    tile_ref[...] = lists
    own_rows[r] = lists
    for n, dev in enumerate(rows):
        send(tile_ref, own_rows.at[r], dev, rso.at[r])
    for dy in (1, 3, 2):
        for core in (0, 1):
            aa = z * (1 - core) + x * core
            bb = x * (1 - core) + z * core
            row = 2 * ((y + dy) % 4) + core
            send(og.at[aa, bb, :, columns(row)], og_all.at[4 - dy, k, aa, bb], yn(dy, core), rs1.at[4 - dy, k])
    sib_og = send(og.at[:, :, :, columns(2 * y + 1 - k)], og_all.at[0, k], sib)
    l1.wait()
    for p in (0, 1):
        hid_all[0, k, p] = raw[:, 512 * p : 512 * p + 512].T
    sib_hid = send(hid_all.at[0, k], hid_all.at[0, k], sib)

    sa, sb, ra, rb, hp, hm, fw = ({} for _ in range(7))

    def stage_a(d):
        for core in (0, 1):
            await_copy(og_all.at[d, core, a, b], rs1.at[d, core])
        sa[d, 0] = send(og_all.at[d, :, a, b], og_all.at[d, :, a, b], bp)
        sa[d, 1] = send(og_all.at[d, :, a, b], og_all.at[d, :, a, b], bm)

    def relay_a(d):
        sa[d, 0].wait_recv()
        ra[d, 0] = send(og_all.at[d, 0, a, (b + 3) % 4], og_all.at[d, 0, a, (b + 3) % 4], bp)
        sa[d, 1].wait_recv()
        ra[d, 1] = send(og_all.at[d, 1, a, (b + 1) % 4], og_all.at[d, 1, a, (b + 1) % 4], bm)

    def stage_b(d):
        ra[d, 0].wait_recv()
        ra[d, 1].wait_recv()
        sb[d, 0] = send(og_all.at[d, :, a], og_all.at[d, :, a], ap)
        sb[d, 1] = send(og_all.at[d, :, a], og_all.at[d, :, a], am)

    def relay_b(d):
        sb[d, 0].wait_recv()
        rb[d, 0] = send(og_all.at[d, 0, (a + 3) % 4], og_all.at[d, 0, (a + 3) % 4], ap)
        sb[d, 1].wait_recv()
        rb[d, 1] = send(og_all.at[d, 1, (a + 1) % 4], og_all.at[d, 1, (a + 1) % 4], am)

    def part(ref, h, p):
        return ref.at[p, :, pl.ds(256 * h, 256)]

    def send_own(way, h, p):
        if way == 0:
            hp[h, p] = send(part(hid_all.at[0, k], h, p), part(hid_all.at[3, k], h, p), yn(1, k))
        else:
            hm[h, p] = send(part(hid_all.at[0, k], h, p), part(hid_all.at[1, k], h, p), yn(3, k))

    def forward(d, h, p):
        ref = part(hid_all.at[d, k], h, p)
        fw[d, h, p] = send(ref, ref, sib)

    def arrive(way, h, p):
        d = 3 if way == 0 else 1
        (hp if way == 0 else hm)[h, p].wait_recv()
        if h == way:
            relay[way, p] = send(part(hid_all.at[d, k], h, p), part(hid_all.at[2, k], h, p), yn(1 if way == 0 else 3, k))
        forward(d, h, p)

    def relayed(way, p):
        relay[way, p].wait_recv()
        forward(2, way, p)

    def whole(d, p):
        fw[d, 0, p].wait_recv()
        fw[d, 1, p].wait_recv()

    def whole_og(d):
        rb[d, 0].wait_recv()
        rb[d, 1].wait_recv()

    def add_products(d, p):
        def tile(i, carry):
            at = pl.ds(pl.multiple_of(512 * p + i * 256, 256), 256)
            here = pl.ds(pl.multiple_of(i * 256, 256), 256)
            left = jnp.concatenate([hid_all[d, core, p, here, :] for core in (0, 1)], axis=1)
            prod = dot(left, og_all[d].reshape(1024, 1024), ((1,), (0,)))
            if d == 0:
                acc[at, :] = prod
            elif d == 2:
                ref = lead if p == 0 else grad_ref
                ref[here, :] = (acc[at, :] + prod).astype(jnp.bfloat16)
            else:
                acc[at, :] += prod
            return carry

        lax.fori_loop(0, 2, tile, 0)

    relay = {}
    stage_a(1)
    stage_a(3)
    send_own(0, 0, 0)
    send_own(1, 1, 0)
    send_own(0, 1, 0)
    send_own(1, 0, 0)
    stage_a(2)
    relay_a(1)
    relay_a(3)
    stage_b(1)
    group = lax.broadcasted_iota(jnp.int32, (8, 128), 1) // 16
    for dy in range(8):
        pl.when(dy != r)(lambda dy=dy: await_copy(own_rows.at[dy], rso.at[dy]))
    for dy in range(8):
        lists = jnp.where(group == dy, own_rows[dy], lists)
    own_all[z, x] = lists
    own_x = [send(own_all.at[z, x], own_all.at[z, x], dev) for dev in along_x]
    relay_a(2)
    stage_b(3)
    for copy in own_x:
        copy.wait_recv()
    own_z = [send(own_all.at[z], own_all.at[z], dev) for dev in along_z]
    stage_b(2)
    l0.wait()
    sib_og.wait_recv()
    sib_hid.wait_recv()
    arrive(0, 0, 0)
    send_own(0, 0, 1)
    arrive(1, 1, 0)
    send_own(1, 1, 1)
    add_products(0, 0)
    add_products(0, 1)
    relay_b(1)
    arrive(0, 1, 0)
    send_own(0, 1, 1)
    arrive(1, 0, 0)
    send_own(1, 0, 1)
    for copy in own_z:
        copy.wait_recv()
    counts[...] = jnp.zeros_like(counts)
    plan_rules(own_all, hop_ref, trials, counts, (0, 1))
    relay_b(3)
    relayed(0, 0)
    relayed(1, 0)
    plan_rules(own_all, hop_ref, trials, counts, (2, 3))
    plan_choice(trials, counts, table_ref)
    arrive(0, 0, 1)
    arrive(1, 1, 1)
    relay_b(2)
    whole_og(1)
    whole(1, 0)
    add_products(1, 0)
    arrive(0, 1, 1)
    arrive(1, 0, 1)
    whole_og(3)
    whole(3, 0)
    add_products(3, 0)
    whole(1, 1)
    add_products(1, 1)
    whole_og(2)
    whole(2, 0)
    add_products(2, 0)
    relayed(0, 1)
    relayed(1, 1)
    whole(3, 1)
    add_products(3, 1)

    def pair(q, carry):
        def store(kind, at, value):
            packed_ref[2 * q + kind, at : at + value.shape[0], :] = value

        make_pair(lead[:, pl.ds(pl.multiple_of(q * BLK, BLK), BLK)], store)
        return carry

    lax.fori_loop(0, 2, pair, 0)
    whole(2, 1)
    add_products(2, 1)
    for copy in sent:
        copy.wait_send()


SENDS = 7 + 6 + 2 + 8 + 6 + 6 + 6 + 6 + 4 + 12 + 3 + 3


def gather(hid, og, own):
    return pl.pallas_call(
        gather_kernel,
        out_shape=(
            jax.ShapeDtypeStruct((4, ROWS, 128), jnp.bfloat16),
            jax.ShapeDtypeStruct((512, 1024), jnp.bfloat16),
            jax.ShapeDtypeStruct((TABLE, 128), jnp.int32),
        ),
        in_specs=[
            pl.BlockSpec(memory_space=pltpu.SMEM),
            pl.BlockSpec(memory_space=pl.ANY),
            pl.BlockSpec(memory_space=pl.ANY),
            pl.BlockSpec(memory_space=pltpu.VMEM),
        ],
        out_specs=(pl.BlockSpec(memory_space=pltpu.VMEM),) * 3,
        scratch_shapes=[
            pltpu.VMEM((4, 2, 2, 512, 512), jnp.bfloat16),
            pltpu.VMEM((4, 2, 4, 4, 32, 1024), jnp.bfloat16),
            pltpu.VMEM((8, 8, 128), jnp.int32),
            pltpu.VMEM((4, 4, 8, 128), jnp.int32),
            pltpu.VMEM((8, 128), jnp.int32),
            pltpu.VMEM((len(RULES), WHICH, 128), jnp.int32),
            pltpu.VMEM((16, 128), jnp.float32),
            pltpu.VMEM((512, 1024), jnp.bfloat16),
            pltpu.VMEM((1024, 1024), jnp.float32),
            pltpu.VMEM((512, 1024), jnp.bfloat16),
            pltpu.SemaphoreType.DMA((SENDS,)),
            pltpu.SemaphoreType.DMA((SENDS,)),
            pltpu.SemaphoreType.DMA((2,)),
            pltpu.SemaphoreType.DMA((4, 2)),
            pltpu.SemaphoreType.DMA((8,)),
        ],
        compiler_params=pltpu.CompilerParams(collective_id=0, has_side_effects=True, vmem_limit_bytes=LIMIT),
        name="gather",
    )(own, hid, og.reshape(4, 4, 32, 8192), jnp.asarray(hop_matrix(), jnp.bfloat16))


def dot(left, right, dims):
    return lax.dot_general(left, right, (dims, ((), ())), preferred_element_type=jnp.float32)


def patched(matrix, blocks):
    lines = []
    for i in range(4):
        cells = [matrix[128 * i : 128 * i + 128, 128 * j : 128 * j + 128] for j in range(4)]
        cells[i] = blocks[i]
        lines.append(jnp.concatenate(cells, axis=1))
    return jnp.concatenate(lines, axis=0)


def diagonals(matrix):
    return [matrix[128 * i : 128 * i + 128, 128 * i : 128 * i + 128] for i in range(4)]


def make_pair(g, store):
    rows = lax.broadcasted_iota(jnp.int32, (128, 128), 0)
    cols = lax.broadcasted_iota(jnp.int32, (128, 128), 1)
    diag = rows == cols
    unit = diag.astype(jnp.float32)
    plain = ((1,), (0,))
    both = (0, 1)
    quarter = jnp.asarray(-0.25, jnp.bfloat16)

    def narrow(value):
        return value.astype(jnp.bfloat16)

    stats = [narrow(dot(g, g, ((1 - kind,), (1 - kind,)))) for kind in both]
    coupled, first, scale = [None] * 2, [None] * 2, [None] * 2
    for kind in both:
        sym = stats[kind].astype(jnp.float32)
        trace = sum(jnp.where(diag, block, 0.0) for block in diagonals(sym))
        mean = jnp.sum(trace, keepdims=True) / BLK
        norm = jnp.sqrt(jnp.sum(sym * sym, keepdims=True) + (0.21 * BLK) * mean * mean + 1e-06)
        grow = 4.0 / norm
        spread = sym * grow
        ends = [block + unit * (0.1 * mean * grow) for block in diagonals(spread)]
        body_b = narrow(spread)
        coupled[kind] = patched(body_b, [narrow(block) for block in ends])
        first[kind] = patched(body_b * quarter, [narrow(1.25 * unit - 0.25 * block) for block in ends])
        scale[kind] = jnp.sqrt(jnp.sqrt(grow)) * jnp.sqrt(jnp.sqrt(1.1 * mean))
    two = [narrow(dot(first[kind], first[kind], plain)) for kind in both]
    four = [narrow(dot(two[kind], two[kind], plain)) for kind in both]
    second = []
    for kind in both:
        after = dot(four[kind], coupled[kind], plain) * -0.25
        second.append(patched(narrow(after), [narrow(1.25 * unit + block) for block in diagonals(after)]))
    for kind in both:
        top = dot(first[kind][:256], second[kind], plain) * scale[kind]
        low = dot(first[kind][256:], second[kind][:, 256:], plain) * scale[kind]

        def block(i, j):
            if i < 2:
                return top[128 * i : 128 * i + 128, 128 * j : 128 * j + 128]
            return low[128 * (i - 2) : 128 * (i - 1), 128 * (j - 2) : 128 * (j - 1)]

        for n, (i, j) in enumerate(OFF):
            store(kind, 128 * n, narrow(block(i, j)))
        spare = jnp.zeros((16, 128), jnp.float32)
        for n in (0, 1):
            lead, tail = block(2 * n, 2 * n), block(2 * n + 1, 2 * n + 1)
            store(kind, 128 * (6 + n), narrow(jnp.where(rows <= cols, lead, tail)))
            line = jnp.sum(jnp.where(diag, tail, 0.0), axis=0, keepdims=True)
            spare = jnp.where(rows[:16] == n, line, spare)
        store(kind, 1024, narrow(spare))


def roots_kernel(g_ref, out_ref):
    def store(kind, at, value):
        out_ref[kind, at : at + value.shape[0], :] = value

    make_pair(g_ref[...], store)


def roots(grad):
    return pl.pallas_call(
        roots_kernel,
        grid=(2,),
        out_shape=jax.ShapeDtypeStruct((4, ROWS, 128), jnp.bfloat16),
        in_specs=[pl.BlockSpec((BLK, BLK), lambda i: (0, i))],
        out_specs=pl.BlockSpec((2, ROWS, 128), lambda i: (i, 0, 0)),
        compiler_params=pltpu.CompilerParams(vmem_limit_bytes=LIMIT),
        name="roots",
    )(grad)


def hop_matrix():
    out = np.zeros((4, 128, 256), np.float32)
    for lane in range(128):
        g, n = lane // 16, lane % 16
        z, x = n // 4, n % 4
        targets = (z * 4 + (x + 1) % 4, z * 4 + (x + 3) % 4, (z + 1) % 4 * 4 + x, (z + 3) % 4 * 4 + x)
        for link, to in enumerate(targets):
            out[link, lane, g * 16 + to] = 1.0
            out[link, lane, 128 + g * 16 + to] = link
    return out.reshape(512, 256)


def plan_state(own_ref):
    lane = lax.broadcasted_iota(jnp.int32, (128, 128), 1)
    item = lax.broadcasted_iota(jnp.int32, (128, 128), 0)
    dest = jnp.concatenate([own_ref[c // 4, c % 4] for c in range(16)], axis=0)
    return lane, item, dest, lane & 15


def plan_rules(own_ref, hop_ref, trial_ref, count_ref, rules):
    lane, item, dest, node = plan_state(own_ref)
    home = dest == node
    homef = home.astype(jnp.float32)
    dx = (dest - node) & 3
    dz = ((dest >> 2) - (node >> 2)) & 3
    wants = ((dx == 1) | (dx == 2), dx >= 2, (dz == 1) | (dz == 2), dz >= 2)
    ways = sum(w.astype(jnp.int32) for w in wants)
    far = jnp.where(dx == 3, 1, dx) + jnp.where(dz == 3, 1, dz)
    origin = ((item >> 3) == node).astype(jnp.float32)
    late = (item & 7) >= 4
    below = (lane < item).astype(jnp.bfloat16)
    rank = dot(below, home.astype(jnp.bfloat16), ((1,), (0,)))
    hop = hop_ref[...]
    keys, here, slot = {}, {}, {}
    for v in rules:
        tie = (128 - item, item + 1, ((item * 37) & 127) + 1)[RULES[v][1]]
        key = ((4 - ways + far) * 1024 + tie).astype(jnp.float32)
        keys[v] = [jnp.where(w, key, 0.0) for w in wants]
        here[v] = jnp.where(late, 0.0, origin)
        slot[v] = (item & 7).astype(jnp.float32)
    for t in range(STEPS_MAX):
        for v in rules:
            if t == 1:
                here[v] = here[v] + jnp.where(late, origin, 0.0)
            moves = [None] * 4
            for link in RULES[v][0]:
                value = keys[v][link] * here[v]
                best = jnp.max(value, axis=0, keepdims=True)
                win = jnp.where((value == best) & (value > 0.0), 1.0, 0.0)
                here[v] = here[v] - win
                pick = jnp.sum(win * slot[v], axis=0, keepdims=True)
                trial_ref[v, 4 * t + link : 4 * t + link + 1, :] = pick.astype(jnp.int32)
                moves[link] = win.astype(jnp.bfloat16)
            landed = dot(jnp.concatenate(moves, axis=1), hop, ((1,), (0,)))
            new = landed[:, :128]
            here[v] = here[v] + new
            slot[v] = jnp.where(new > 0.5, landed[:, 128:] + (STATS + 4.0 * t), slot[v])
            if t + 1 in STEPS:
                row = len(STEPS) * v + STEPS.index(t + 1)
                count_ref[row : row + 1, :] = jnp.sum(here[v] * homef, axis=0, keepdims=True)
    for v in rules:
        for n in range(MOST):
            mine = jnp.where(home & (rank == float(n)), slot[v] + 1.0, 0.0)
            row = 4 * STEPS_MAX + n
            trial_ref[v, row : row + 1, :] = jnp.sum(mine, axis=0, keepdims=True).astype(jnp.int32) - 1


def plan_choice(trial_ref, count_ref, out_ref):
    left = lax.broadcasted_iota(jnp.int32, (128, 128), 0) // 16
    right = lax.broadcasted_iota(jnp.int32, (128, 128), 1) // 16
    same = (left == right).astype(jnp.bfloat16)
    done = (dot(count_ref[...].astype(jnp.bfloat16), same, ((1,), (0,))) == 128.0).astype(jnp.float32)
    score = [sum(done[len(STEPS) * v + n : len(STEPS) * v + n + 1] for n in range(len(STEPS))) for v in range(len(RULES))]
    best, table = score[0], trial_ref[0]
    for v in range(1, len(RULES)):
        better = score[v] > best
        table = jnp.where(better, trial_ref[v], table)
        best = jnp.maximum(best, score[v])
    out_ref[:WHICH, :] = table
    which = len(STEPS) - jnp.min(best, keepdims=True)
    out_ref[WHICH:, :] = jnp.broadcast_to(which, (8, 128)).astype(jnp.int32)


def deliver_kernel(steps, table, packed, grad, out, pool, recv, stage, ss, rs):
    r, c = lax.axis_index("dp"), lax.axis_index("mp")
    z, x = c // 4, c % 4
    me = r * 16 + c
    peers = (
        (r, z * 4 + (x + 1) % 4),
        (r, z * 4 + (x + 3) % 4),
        (r, (z + 1) % 4 * 4 + x),
        (r, (z + 3) % 4 * 4 + x),
    )

    def pair(q, carry):
        def store(kind, at, value):
            pool[4 + 2 * q + kind, at : at + value.shape[0], :] = value

        make_pair(grad[:, pl.ds(pl.multiple_of(q * BLK, BLK), BLK)], store)
        return carry

    def copy(t, link, half):
        return pltpu.make_async_remote_copy(
            src_ref=stage.at[t % 2, link, HALVES[half]],
            dst_ref=recv.at[t, link, HALVES[half]],
            send_sem=ss.at[t % 2, link, half],
            recv_sem=rs.at[t, link, half],
            device_id=peers[link],
            device_id_type=MESH,
        )

    def land(t, half):
        for link in range(4):
            copy(t, link, half).wait_recv()
            pool[STATS + 4 * t + link, HALVES[half], :] = recv[t, link, HALVES[half], :]

    def push(t, half):
        for link in range(4):
            stage[t % 2, link, HALVES[half], :] = pool[table[4 * t + link, me], HALVES[half], :]
            copy(t, link, half).start()

    def settle(t, half):
        for link in range(4):
            copy(t, link, half).wait_send()

    barrier = pltpu.get_barrier_semaphore()
    for dev in peers:
        pl.semaphore_signal(barrier, inc=1, device_id=dev, device_id_type=MESH)
    pool[:4] = packed[...]
    pl.semaphore_wait(barrier, 4)
    push(0, 0)
    push(0, 1)
    lax.fori_loop(0, 2, pair, 0)
    for half in (0, 1):
        land(0, half)
        push(1, half)

    def step(t, carry):
        for half in (0, 1):
            land(t - 1, half)
            settle(t - 2, half)
            push(t, half)
        return carry

    lax.fori_loop(2, steps, step, 0)
    for half in (0, 1):
        land(steps - 1, half)
    for t in (steps - 2, steps - 1):
        for half in (0, 1):
            settle(t, half)
    for n in range(MOST):
        at = table[4 * STEPS_MAX + n, me]
        block = pool[jnp.maximum(at, 0)]
        keep = (at >= 0).astype(jnp.bfloat16)
        out[n] = block * keep


HALVES = (pl.ds(0, 528), pl.ds(528, 512))


def deliver(steps, table, packed, grad):
    return pl.pallas_call(
        functools.partial(deliver_kernel, steps),
        out_shape=jax.ShapeDtypeStruct((MOST, ROWS, 128), jnp.bfloat16),
        in_specs=[pl.BlockSpec(memory_space=pltpu.SMEM)] + [pl.BlockSpec(memory_space=pltpu.VMEM)] * 2,
        out_specs=pl.BlockSpec(memory_space=pltpu.VMEM),
        scratch_shapes=[
            pltpu.VMEM((STATS + 4 * steps, ROWS, 128), jnp.bfloat16),
            pltpu.VMEM((steps, 4, ROWS, 128), jnp.bfloat16),
            pltpu.VMEM((2, 4, ROWS, 128), jnp.bfloat16),
            pltpu.SemaphoreType.DMA((2, 4, 2)),
            pltpu.SemaphoreType.DMA((steps, 4, 2)),
        ],
        compiler_params=pltpu.CompilerParams(
            collective_id=steps, has_side_effects=True, vmem_limit_bytes=LIMIT
        ),
        name="deliver",
    )(table, packed, grad)


def deliver_any(owners, packed):
    myself = lax.axis_index("mp")
    lists = lax.all_gather(owners, "mp", axis=1, tiled=True)[0]
    mine = lists[myself]
    count = lists.shape[0]
    match = (mine[None, :] == jnp.arange(count, dtype=jnp.int32)[:, None]).astype(jnp.int32)
    rank = jnp.cumsum(match, axis=1) - match
    select = (match[:, None, :] > 0) & (rank[:, None, :] == jnp.arange(CAP, dtype=jnp.int32)[None, :, None])
    index = jnp.sum(select.astype(jnp.int32) * jnp.arange(STATS, dtype=jnp.int32), axis=2)
    outgoing = packed[index.reshape(-1)].reshape(count, CAP, ROWS, 128)
    received = lax.all_to_all(outgoing, "mp", split_axis=0, concat_axis=0, tiled=True)
    counts = jnp.sum((lists == myself).astype(jnp.int32), axis=1)
    valid = (jnp.arange(CAP, dtype=jnp.int32)[None, :] < counts[:, None]).reshape(-1).astype(jnp.int32)
    before = jnp.cumsum(valid) - valid
    chosen = (valid[None, :] > 0) & (before[None, :] == jnp.arange(MOST, dtype=jnp.int32)[:, None])
    index = jnp.sum(chosen.astype(jnp.int32) * jnp.arange(count * CAP, dtype=jnp.int32), axis=1)
    picked = received.reshape(count * CAP, ROWS, 128)[index]
    return jnp.where(jnp.any(chosen, axis=1)[:, None, None], picked, jnp.zeros_like(picked))


def unpack_kernel(in_ref, out_ref):
    rows = lax.broadcasted_iota(jnp.int32, (128, 128), 0)
    cols = lax.broadcasted_iota(jnp.int32, (128, 128), 1)
    unit = (rows == cols).astype(jnp.bfloat16)
    for m in range(PAIR):
        flipped = dot(unit, in_ref[m, :1024, :], ((1,), (1,)))
        for n, (i, j) in enumerate(OFF):
            out_ref[m, 128 * i : 128 * i + 128, 128 * j : 128 * j + 128] = in_ref[m, 128 * n : 128 * n + 128, :]
            turned = flipped[:, 128 * n : 128 * n + 128].astype(jnp.bfloat16)
            out_ref[m, 128 * j : 128 * j + 128, 128 * i : 128 * i + 128] = turned
        spare = in_ref[m, 1024:, :].astype(jnp.float32)
        for n in (0, 1):
            both = in_ref[m, 128 * (6 + n) : 128 * (7 + n), :].astype(jnp.float32)
            other = flipped[:, 128 * (6 + n) : 128 * (7 + n)]
            first = jnp.where(rows <= cols, both, other)
            second = jnp.where(rows > cols, both, other)
            second = jnp.where(rows == cols, spare[n : n + 1, :], second)
            for half, value in ((0, first), (1, second)):
                at = 128 * (2 * n + half)
                out_ref[m, at : at + 128, at : at + 128] = value.astype(jnp.bfloat16)


PAIR = 2


def unpack(packed):
    return pl.pallas_call(
        unpack_kernel,
        grid=(MOST // PAIR,),
        out_shape=jax.ShapeDtypeStruct((MOST, BLK, BLK), jnp.bfloat16),
        in_specs=[pl.BlockSpec((PAIR, ROWS, 128), lambda i: (i, 0, 0))],
        out_specs=pl.BlockSpec((PAIR, BLK, BLK), lambda i: (i, 0, 0)),
        compiler_params=pltpu.CompilerParams(vmem_limit_bytes=LIMIT),
        name="unpack",
    )(packed)


def body(hidden_acts, out_grad, owners):
    packed, grad, table = gather(hidden_acts, out_grad, owners)
    ways = [functools.partial(deliver, steps, table, packed, grad) for steps in STEPS]
    ways.append(lambda: deliver_any(owners, jnp.concatenate([packed, roots(grad)])))
    arrived = lax.switch(table[WHICH, 0], ways)
    return unpack(arrived)[None, None]


def solution(mesh):
    placed = (P("dp", "mp"), P("dp", None), P("dp", "mp", None))
    return jax.shard_map(
        body, mesh=mesh, in_specs=placed, out_specs=P("dp", "mp", None, None, None), check_vma=False
    )
```

```python
import functools

import jax
import jax.numpy as jnp
import numpy as np
from jax import lax
from jax.experimental import pallas as pl
from jax.experimental.pallas import tpu as pltpu
from jax.sharding import PartitionSpec as P

MESH = pl.DeviceIdType.MESH
BLK = 512
STATS = 8
CAP = 2
MOST = 12
ROWS = 1040
STEPS = (7, 8, 9)
STEPS_MAX = STEPS[-1]
WHICH = 4 * STEPS_MAX + MOST
TABLE = WHICH + 8
RULES = (((0, 2, 1, 3), 0), ((0, 2, 1, 3), 1), ((0, 2, 1, 3), 2), ((1, 3, 0, 2), 2))
OFF = ((0, 1), (0, 2), (0, 3), (1, 2), (1, 3), (2, 3))
LIMIT = 56 * 1024 * 1024


def gather_kernel(own, hid, og, hop_ref, packed_ref, grad_ref, table_ref, hid_all, og_all, own_rows, own_all, tile_ref, trials, counts, raw, acc, lead, ss, rs, ls, rs1, rso):
    r, c = lax.axis_index("dp"), lax.axis_index("mp")
    y, k = r // 2, r % 2
    z, x = c // 4, c % 4
    sib = (2 * y + 1 - k, c)

    def yn(dy, core):
        return (2 * ((y + dy) % 4) + core, c)

    a = z * (1 - k) + x * k
    b = x * (1 - k) + z * k

    def plane(aa, bb):
        zz = aa * (1 - k) + bb * k
        xx = bb * (1 - k) + aa * k
        return (r, zz * 4 + xx)

    bp, bm = plane(a, (b + 1) % 4), plane(a, (b + 3) % 4)
    ap, am = plane((a + 1) % 4, b), plane((a + 3) % 4, b)
    rows = [sib] + [yn(dy, core) for dy in (1, 2, 3) for core in (0, 1)]
    along_x = [(r, z * 4 + (x + n) % 4) for n in (1, 2, 3)]
    along_z = [(r, (z + n) % 4 * 4 + x) for n in (1, 2, 3)]

    def columns(row):
        return pl.ds(pl.multiple_of(row * 1024, 1024), 1024)

    l0 = pltpu.make_async_copy(og.at[:, :, :, columns(r)], og_all.at[0, k], ls.at[0])
    l1 = pltpu.make_async_copy(hid, raw, ls.at[1])
    l1.start()
    l0.start()

    barrier = pltpu.get_barrier_semaphore()
    partners = rows + along_x + along_z
    for dev in partners:
        pl.semaphore_signal(barrier, inc=1, device_id=dev, device_id_type=MESH)
    l1.wait()
    for p in (0, 1):
        hid_all[0, k, p] = raw[:, 512 * p : 512 * p + 512].T
    pl.semaphore_wait(barrier, len(partners))

    sent = []

    def send(src, dst, dev, landed=None):
        i = len(sent)
        landed = rs.at[i] if landed is None else landed
        copy = pltpu.make_async_remote_copy(
            src_ref=src, dst_ref=dst, send_sem=ss.at[i], recv_sem=landed, device_id=dev, device_id_type=MESH
        )
        copy.start()
        sent.append(copy)
        return copy

    def await_copy(ref, sem):
        pltpu.make_async_copy(ref, ref, sem).wait()

    line = lax.broadcasted_iota(jnp.int32, (8, 128), 0)
    lists = jnp.zeros((8, 128), jnp.int32)
    for j in range(STATS):
        lists = jnp.where(line == j, own[0, 0, j], lists)
    tile_ref[...] = lists
    own_rows[r] = lists
    for n, dev in enumerate(rows):
        send(tile_ref, own_rows.at[r], dev, rso.at[r])
    for dy in (1, 3, 2):
        for core in (0, 1):
            aa = z * (1 - core) + x * core
            bb = x * (1 - core) + z * core
            row = 2 * ((y + dy) % 4) + core
            send(og.at[aa, bb, :, columns(row)], og_all.at[4 - dy, k, aa, bb], yn(dy, core), rs1.at[4 - dy, k])
    sib_og = send(og.at[:, :, :, columns(2 * y + 1 - k)], og_all.at[0, k], sib)
    sib_hid = send(hid_all.at[0, k], hid_all.at[0, k], sib)

    sa, sb, ra, rb, hp, hm, fw = ({} for _ in range(7))

    def stage_a(d):
        for core in (0, 1):
            await_copy(og_all.at[d, core, a, b], rs1.at[d, core])
        sa[d, 0] = send(og_all.at[d, :, a, b], og_all.at[d, :, a, b], bp)
        sa[d, 1] = send(og_all.at[d, :, a, b], og_all.at[d, :, a, b], bm)

    def relay_a(d):
        sa[d, 0].wait_recv()
        ra[d, 0] = send(og_all.at[d, 0, a, (b + 3) % 4], og_all.at[d, 0, a, (b + 3) % 4], bp)
        sa[d, 1].wait_recv()
        ra[d, 1] = send(og_all.at[d, 1, a, (b + 1) % 4], og_all.at[d, 1, a, (b + 1) % 4], bm)

    def stage_b(d):
        ra[d, 0].wait_recv()
        ra[d, 1].wait_recv()
        sb[d, 0] = send(og_all.at[d, :, a], og_all.at[d, :, a], ap)
        sb[d, 1] = send(og_all.at[d, :, a], og_all.at[d, :, a], am)

    def relay_b(d):
        sb[d, 0].wait_recv()
        rb[d, 0] = send(og_all.at[d, 0, (a + 3) % 4], og_all.at[d, 0, (a + 3) % 4], ap)
        sb[d, 1].wait_recv()
        rb[d, 1] = send(og_all.at[d, 1, (a + 1) % 4], og_all.at[d, 1, (a + 1) % 4], am)

    def part(ref, h, p):
        return ref.at[p, :, pl.ds(256 * h, 256)]

    def send_own(way, h, p):
        if way == 0:
            hp[h, p] = send(part(hid_all.at[0, k], h, p), part(hid_all.at[3, k], h, p), yn(1, k))
        else:
            hm[h, p] = send(part(hid_all.at[0, k], h, p), part(hid_all.at[1, k], h, p), yn(3, k))

    def forward(d, h, p):
        ref = part(hid_all.at[d, k], h, p)
        fw[d, h, p] = send(ref, ref, sib)

    def arrive(way, h, p):
        d = 3 if way == 0 else 1
        (hp if way == 0 else hm)[h, p].wait_recv()
        if h == way:
            relay[way, p] = send(part(hid_all.at[d, k], h, p), part(hid_all.at[2, k], h, p), yn(1 if way == 0 else 3, k))
        forward(d, h, p)

    def relayed(way, p):
        relay[way, p].wait_recv()
        forward(2, way, p)

    def whole(d, p):
        fw[d, 0, p].wait_recv()
        fw[d, 1, p].wait_recv()

    def whole_og(d):
        rb[d, 0].wait_recv()
        rb[d, 1].wait_recv()

    def add_products(d, p):
        def tile(i, carry):
            at = pl.ds(pl.multiple_of(512 * p + i * 256, 256), 256)
            here = pl.ds(pl.multiple_of(i * 256, 256), 256)
            left = jnp.concatenate([hid_all[d, core, p, here, :] for core in (0, 1)], axis=1)
            prod = dot(left, og_all[d].reshape(1024, 1024), ((1,), (0,)))
            if d == 0:
                acc[at, :] = prod
            elif d == 2:
                ref = lead if p == 0 else grad_ref
                ref[here, :] = (acc[at, :] + prod).astype(jnp.bfloat16)
            else:
                acc[at, :] += prod
            return carry

        lax.fori_loop(0, 2, tile, 0)

    relay = {}
    stage_a(1)
    stage_a(3)
    send_own(0, 0, 0)
    send_own(1, 1, 0)
    send_own(0, 1, 0)
    send_own(1, 0, 0)
    stage_a(2)
    relay_a(1)
    relay_a(3)
    stage_b(1)
    group = lax.broadcasted_iota(jnp.int32, (8, 128), 1) // 16
    for dy in range(8):
        pl.when(dy != r)(lambda dy=dy: await_copy(own_rows.at[dy], rso.at[dy]))
    for dy in range(8):
        lists = jnp.where(group == dy, own_rows[dy], lists)
    own_all[z, x] = lists
    own_x = [send(own_all.at[z, x], own_all.at[z, x], dev) for dev in along_x]
    relay_a(2)
    stage_b(3)
    for copy in own_x:
        copy.wait_recv()
    own_z = [send(own_all.at[z], own_all.at[z], dev) for dev in along_z]
    stage_b(2)
    l0.wait()
    sib_og.wait_recv()
    sib_hid.wait_recv()
    arrive(0, 0, 0)
    send_own(0, 0, 1)
    arrive(1, 1, 0)
    send_own(1, 1, 1)
    add_products(0, 0)
    add_products(0, 1)
    relay_b(1)
    arrive(0, 1, 0)
    send_own(0, 1, 1)
    arrive(1, 0, 0)
    send_own(1, 0, 1)
    for copy in own_z:
        copy.wait_recv()
    counts[...] = jnp.zeros_like(counts)
    plan_rules(own_all, hop_ref, trials, counts, (0, 1))
    relay_b(3)
    relayed(0, 0)
    relayed(1, 0)
    plan_rules(own_all, hop_ref, trials, counts, (2, 3))
    plan_choice(trials, counts, table_ref)
    arrive(0, 0, 1)
    arrive(1, 1, 1)
    relay_b(2)
    whole_og(1)
    whole(1, 0)
    add_products(1, 0)
    arrive(0, 1, 1)
    arrive(1, 0, 1)
    whole_og(3)
    whole(3, 0)
    add_products(3, 0)
    whole(1, 1)
    add_products(1, 1)
    whole(3, 1)
    add_products(3, 1)
    whole_og(2)
    whole(2, 0)
    add_products(2, 0)

    def pair(q, carry):
        def store(kind, at, value):
            packed_ref[2 * q + kind, at : at + value.shape[0], :] = value

        make_pair(lead[:, pl.ds(pl.multiple_of(q * BLK, BLK), BLK)], store)
        return carry

    lax.fori_loop(0, 1, pair, 0)
    relayed(0, 1)
    relayed(1, 1)
    lax.fori_loop(1, 2, pair, 0)
    whole(2, 1)
    add_products(2, 1)
    for copy in sent:
        copy.wait_send()


SENDS = 7 + 6 + 2 + 8 + 6 + 6 + 6 + 6 + 4 + 12 + 3 + 3


def gather(hid, og, own):
    return pl.pallas_call(
        gather_kernel,
        out_shape=(
            jax.ShapeDtypeStruct((4, ROWS, 128), jnp.bfloat16),
            jax.ShapeDtypeStruct((512, 1024), jnp.bfloat16),
            jax.ShapeDtypeStruct((TABLE, 128), jnp.int32),
        ),
        in_specs=[
            pl.BlockSpec(memory_space=pltpu.SMEM),
            pl.BlockSpec(memory_space=pl.ANY),
            pl.BlockSpec(memory_space=pl.ANY),
            pl.BlockSpec(memory_space=pltpu.VMEM),
        ],
        out_specs=(pl.BlockSpec(memory_space=pltpu.VMEM),) * 3,
        scratch_shapes=[
            pltpu.VMEM((4, 2, 2, 512, 512), jnp.bfloat16),
            pltpu.VMEM((4, 2, 4, 4, 32, 1024), jnp.bfloat16),
            pltpu.VMEM((8, 8, 128), jnp.int32),
            pltpu.VMEM((4, 4, 8, 128), jnp.int32),
            pltpu.VMEM((8, 128), jnp.int32),
            pltpu.VMEM((len(RULES), WHICH, 128), jnp.int32),
            pltpu.VMEM((16, 128), jnp.float32),
            pltpu.VMEM((512, 1024), jnp.bfloat16),
            pltpu.VMEM((1024, 1024), jnp.float32),
            pltpu.VMEM((512, 1024), jnp.bfloat16),
            pltpu.SemaphoreType.DMA((SENDS,)),
            pltpu.SemaphoreType.DMA((SENDS,)),
            pltpu.SemaphoreType.DMA((2,)),
            pltpu.SemaphoreType.DMA((4, 2)),
            pltpu.SemaphoreType.DMA((8,)),
        ],
        compiler_params=pltpu.CompilerParams(collective_id=0, has_side_effects=True, vmem_limit_bytes=LIMIT),
        name="gather",
    )(own, hid, og.reshape(4, 4, 32, 8192), jnp.asarray(hop_matrix(), jnp.bfloat16))


def dot(left, right, dims):
    return lax.dot_general(left, right, (dims, ((), ())), preferred_element_type=jnp.float32)


def patched(matrix, blocks):
    lines = []
    for i in range(4):
        cells = [matrix[128 * i : 128 * i + 128, 128 * j : 128 * j + 128] for j in range(4)]
        cells[i] = blocks[i]
        lines.append(jnp.concatenate(cells, axis=1))
    return jnp.concatenate(lines, axis=0)


def diagonals(matrix):
    return [matrix[128 * i : 128 * i + 128, 128 * i : 128 * i + 128] for i in range(4)]


def make_pair(g, store):
    rows = lax.broadcasted_iota(jnp.int32, (128, 128), 0)
    cols = lax.broadcasted_iota(jnp.int32, (128, 128), 1)
    diag = rows == cols
    unit = diag.astype(jnp.float32)
    plain = ((1,), (0,))
    both = (0, 1)
    quarter = jnp.asarray(-0.25, jnp.bfloat16)

    def narrow(value):
        return value.astype(jnp.bfloat16)

    stats = [narrow(dot(g, g, ((1 - kind,), (1 - kind,)))) for kind in both]
    coupled, first, scale = [None] * 2, [None] * 2, [None] * 2
    for kind in both:
        sym = stats[kind].astype(jnp.float32)
        trace = sum(jnp.where(diag, block, 0.0) for block in diagonals(sym))
        mean = jnp.sum(trace, keepdims=True) / BLK
        norm = jnp.sqrt(jnp.sum(sym * sym, keepdims=True) + (0.21 * BLK) * mean * mean + 1e-06)
        grow = 4.0 / norm
        spread = sym * grow
        ends = [block + unit * (0.1 * mean * grow) for block in diagonals(spread)]
        body_b = narrow(spread)
        coupled[kind] = patched(body_b, [narrow(block) for block in ends])
        first[kind] = patched(body_b * quarter, [narrow(1.25 * unit - 0.25 * block) for block in ends])
        scale[kind] = jnp.sqrt(jnp.sqrt(grow)) * jnp.sqrt(jnp.sqrt(1.1 * mean))
    two = [narrow(dot(first[kind], first[kind], plain)) for kind in both]
    four = [narrow(dot(two[kind], two[kind], plain)) for kind in both]
    second = []
    for kind in both:
        after = dot(four[kind], coupled[kind], plain) * -0.25
        second.append(patched(narrow(after), [narrow(1.25 * unit + block) for block in diagonals(after)]))
    for kind in both:
        top = dot(first[kind][:256], second[kind], plain) * scale[kind]
        low = dot(first[kind][256:], second[kind][:, 256:], plain) * scale[kind]

        def block(i, j):
            if i < 2:
                return top[128 * i : 128 * i + 128, 128 * j : 128 * j + 128]
            return low[128 * (i - 2) : 128 * (i - 1), 128 * (j - 2) : 128 * (j - 1)]

        for n, (i, j) in enumerate(OFF):
            store(kind, 128 * n, narrow(block(i, j)))
        spare = jnp.zeros((16, 128), jnp.float32)
        for n in (0, 1):
            lead, tail = block(2 * n, 2 * n), block(2 * n + 1, 2 * n + 1)
            store(kind, 128 * (6 + n), narrow(jnp.where(rows <= cols, lead, tail)))
            line = jnp.sum(jnp.where(diag, tail, 0.0), axis=0, keepdims=True)
            spare = jnp.where(rows[:16] == n, line, spare)
        store(kind, 1024, narrow(spare))


def roots_kernel(g_ref, out_ref):
    def store(kind, at, value):
        out_ref[kind, at : at + value.shape[0], :] = value

    make_pair(g_ref[...], store)


def roots(grad):
    return pl.pallas_call(
        roots_kernel,
        grid=(2,),
        out_shape=jax.ShapeDtypeStruct((4, ROWS, 128), jnp.bfloat16),
        in_specs=[pl.BlockSpec((BLK, BLK), lambda i: (0, i))],
        out_specs=pl.BlockSpec((2, ROWS, 128), lambda i: (i, 0, 0)),
        compiler_params=pltpu.CompilerParams(vmem_limit_bytes=LIMIT),
        name="roots",
    )(grad)


def hop_matrix():
    out = np.zeros((4, 128, 256), np.float32)
    for lane in range(128):
        g, n = lane // 16, lane % 16
        z, x = n // 4, n % 4
        targets = (z * 4 + (x + 1) % 4, z * 4 + (x + 3) % 4, (z + 1) % 4 * 4 + x, (z + 3) % 4 * 4 + x)
        for link, to in enumerate(targets):
            out[link, lane, g * 16 + to] = 1.0
            out[link, lane, 128 + g * 16 + to] = link
    return out.reshape(512, 256)


def plan_state(own_ref):
    lane = lax.broadcasted_iota(jnp.int32, (128, 128), 1)
    item = lax.broadcasted_iota(jnp.int32, (128, 128), 0)
    dest = jnp.concatenate([own_ref[c // 4, c % 4] for c in range(16)], axis=0)
    return lane, item, dest, lane & 15


def plan_rules(own_ref, hop_ref, trial_ref, count_ref, rules):
    lane, item, dest, node = plan_state(own_ref)
    home = dest == node
    homef = home.astype(jnp.float32)
    dx = (dest - node) & 3
    dz = ((dest >> 2) - (node >> 2)) & 3
    wants = ((dx == 1) | (dx == 2), dx >= 2, (dz == 1) | (dz == 2), dz >= 2)
    ways = sum(w.astype(jnp.int32) for w in wants)
    far = jnp.where(dx == 3, 1, dx) + jnp.where(dz == 3, 1, dz)
    origin = ((item >> 3) == node).astype(jnp.float32)
    late = (item & 7) >= 4
    below = (lane < item).astype(jnp.bfloat16)
    rank = dot(below, home.astype(jnp.bfloat16), ((1,), (0,)))
    hop = hop_ref[...]
    keys, here, slot = {}, {}, {}
    for v in rules:
        tie = (128 - item, item + 1, ((item * 37) & 127) + 1)[RULES[v][1]]
        key = ((4 - ways + far) * 1024 + tie).astype(jnp.float32)
        keys[v] = [jnp.where(w, key, 0.0) for w in wants]
        here[v] = jnp.where(late, 0.0, origin)
        slot[v] = (item & 7).astype(jnp.float32)
    for t in range(STEPS_MAX):
        for v in rules:
            if t == 1:
                here[v] = here[v] + jnp.where(late, origin, 0.0)
            moves = [None] * 4
            for link in RULES[v][0]:
                value = keys[v][link] * here[v]
                best = jnp.max(value, axis=0, keepdims=True)
                win = jnp.where((value == best) & (value > 0.0), 1.0, 0.0)
                here[v] = here[v] - win
                pick = jnp.sum(win * slot[v], axis=0, keepdims=True)
                trial_ref[v, 4 * t + link : 4 * t + link + 1, :] = pick.astype(jnp.int32)
                moves[link] = win.astype(jnp.bfloat16)
            landed = dot(jnp.concatenate(moves, axis=1), hop, ((1,), (0,)))
            new = landed[:, :128]
            here[v] = here[v] + new
            slot[v] = jnp.where(new > 0.5, landed[:, 128:] + (STATS + 4.0 * t), slot[v])
            if t + 1 in STEPS:
                row = len(STEPS) * v + STEPS.index(t + 1)
                count_ref[row : row + 1, :] = jnp.sum(here[v] * homef, axis=0, keepdims=True)
    for v in rules:
        for n in range(MOST):
            mine = jnp.where(home & (rank == float(n)), slot[v] + 1.0, 0.0)
            row = 4 * STEPS_MAX + n
            trial_ref[v, row : row + 1, :] = jnp.sum(mine, axis=0, keepdims=True).astype(jnp.int32) - 1


def plan_choice(trial_ref, count_ref, out_ref):
    left = lax.broadcasted_iota(jnp.int32, (128, 128), 0) // 16
    right = lax.broadcasted_iota(jnp.int32, (128, 128), 1) // 16
    same = (left == right).astype(jnp.bfloat16)
    done = (dot(count_ref[...].astype(jnp.bfloat16), same, ((1,), (0,))) == 128.0).astype(jnp.float32)
    score = [sum(done[len(STEPS) * v + n : len(STEPS) * v + n + 1] for n in range(len(STEPS))) for v in range(len(RULES))]
    best, table = score[0], trial_ref[0]
    for v in range(1, len(RULES)):
        better = score[v] > best
        table = jnp.where(better, trial_ref[v], table)
        best = jnp.maximum(best, score[v])
    out_ref[:WHICH, :] = table
    which = len(STEPS) - jnp.min(best, keepdims=True)
    out_ref[WHICH:, :] = jnp.broadcast_to(which, (8, 128)).astype(jnp.int32)


def deliver_kernel(steps, table, packed, grad, out, pool, recv, stage, ss, rs):
    r, c = lax.axis_index("dp"), lax.axis_index("mp")
    z, x = c // 4, c % 4
    me = r * 16 + c
    peers = (
        (r, z * 4 + (x + 1) % 4),
        (r, z * 4 + (x + 3) % 4),
        (r, (z + 1) % 4 * 4 + x),
        (r, (z + 3) % 4 * 4 + x),
    )

    def pair(q, carry):
        def store(kind, at, value):
            pool[4 + 2 * q + kind, at : at + value.shape[0], :] = value

        make_pair(grad[:, pl.ds(pl.multiple_of(q * BLK, BLK), BLK)], store)
        return carry

    def copy(t, link, half):
        return pltpu.make_async_remote_copy(
            src_ref=stage.at[t % 2, link, HALVES[half]],
            dst_ref=recv.at[t, link, HALVES[half]],
            send_sem=ss.at[t % 2, link, half],
            recv_sem=rs.at[t, link, half],
            device_id=peers[link],
            device_id_type=MESH,
        )

    def land(t, half):
        for link in range(4):
            copy(t, link, half).wait_recv()
            pool[STATS + 4 * t + link, HALVES[half], :] = recv[t, link, HALVES[half], :]

    def push(t, half):
        for link in range(4):
            stage[t % 2, link, HALVES[half], :] = pool[table[4 * t + link, me], HALVES[half], :]
            copy(t, link, half).start()

    def settle(t, half):
        for link in range(4):
            copy(t, link, half).wait_send()

    barrier = pltpu.get_barrier_semaphore()
    for dev in peers:
        pl.semaphore_signal(barrier, inc=1, device_id=dev, device_id_type=MESH)
    pool[:4] = packed[...]
    pl.semaphore_wait(barrier, 4)
    push(0, 0)
    push(0, 1)
    lax.fori_loop(0, 2, pair, 0)
    for half in (0, 1):
        land(0, half)
        push(1, half)

    def step(t, carry):
        for half in (0, 1):
            land(t - 1, half)
            settle(t - 2, half)
            push(t, half)
        return carry

    lax.fori_loop(2, steps, step, 0)
    for half in (0, 1):
        land(steps - 1, half)
    for t in (steps - 2, steps - 1):
        for half in (0, 1):
            settle(t, half)
    for n in range(MOST):
        at = table[4 * STEPS_MAX + n, me]
        block = pool[jnp.maximum(at, 0)]
        keep = (at >= 0).astype(jnp.bfloat16)
        out[n] = block * keep


HALVES = (pl.ds(0, 528), pl.ds(528, 512))


def deliver(steps, table, packed, grad):
    return pl.pallas_call(
        functools.partial(deliver_kernel, steps),
        out_shape=jax.ShapeDtypeStruct((MOST, ROWS, 128), jnp.bfloat16),
        in_specs=[pl.BlockSpec(memory_space=pltpu.SMEM)] + [pl.BlockSpec(memory_space=pltpu.VMEM)] * 2,
        out_specs=pl.BlockSpec(memory_space=pltpu.VMEM),
        scratch_shapes=[
            pltpu.VMEM((STATS + 4 * steps, ROWS, 128), jnp.bfloat16),
            pltpu.VMEM((steps, 4, ROWS, 128), jnp.bfloat16),
            pltpu.VMEM((2, 4, ROWS, 128), jnp.bfloat16),
            pltpu.SemaphoreType.DMA((2, 4, 2)),
            pltpu.SemaphoreType.DMA((steps, 4, 2)),
        ],
        compiler_params=pltpu.CompilerParams(
            collective_id=steps, has_side_effects=True, vmem_limit_bytes=LIMIT
        ),
        name="deliver",
    )(table, packed, grad)


def deliver_any(owners, packed):
    myself = lax.axis_index("mp")
    lists = lax.all_gather(owners, "mp", axis=1, tiled=True)[0]
    mine = lists[myself]
    count = lists.shape[0]
    match = (mine[None, :] == jnp.arange(count, dtype=jnp.int32)[:, None]).astype(jnp.int32)
    rank = jnp.cumsum(match, axis=1) - match
    select = (match[:, None, :] > 0) & (rank[:, None, :] == jnp.arange(CAP, dtype=jnp.int32)[None, :, None])
    index = jnp.sum(select.astype(jnp.int32) * jnp.arange(STATS, dtype=jnp.int32), axis=2)
    outgoing = packed[index.reshape(-1)].reshape(count, CAP, ROWS, 128)
    received = lax.all_to_all(outgoing, "mp", split_axis=0, concat_axis=0, tiled=True)
    counts = jnp.sum((lists == myself).astype(jnp.int32), axis=1)
    valid = (jnp.arange(CAP, dtype=jnp.int32)[None, :] < counts[:, None]).reshape(-1).astype(jnp.int32)
    before = jnp.cumsum(valid) - valid
    chosen = (valid[None, :] > 0) & (before[None, :] == jnp.arange(MOST, dtype=jnp.int32)[:, None])
    index = jnp.sum(chosen.astype(jnp.int32) * jnp.arange(count * CAP, dtype=jnp.int32), axis=1)
    picked = received.reshape(count * CAP, ROWS, 128)[index]
    return jnp.where(jnp.any(chosen, axis=1)[:, None, None], picked, jnp.zeros_like(picked))


def unpack_kernel(in_ref, out_ref):
    rows = lax.broadcasted_iota(jnp.int32, (128, 128), 0)
    cols = lax.broadcasted_iota(jnp.int32, (128, 128), 1)
    for m in range(GROUP):
        flipped = in_ref[m, :1024, :].T
        for n, (i, j) in enumerate(OFF):
            out_ref[m, 128 * i : 128 * i + 128, 128 * j : 128 * j + 128] = in_ref[m, 128 * n : 128 * n + 128, :]
            out_ref[m, 128 * j : 128 * j + 128, 128 * i : 128 * i + 128] = flipped[:, 128 * n : 128 * n + 128]
        spare = in_ref[m, 1024:, :].astype(jnp.float32)
        for n in (0, 1):
            both = in_ref[m, 128 * (6 + n) : 128 * (7 + n), :].astype(jnp.float32)
            other = flipped[:, 128 * (6 + n) : 128 * (7 + n)].astype(jnp.float32)
            first = jnp.where(rows <= cols, both, other)
            second = jnp.where(rows > cols, both, other)
            second = jnp.where(rows == cols, spare[n : n + 1, :], second)
            for half, value in ((0, first), (1, second)):
                at = 128 * (2 * n + half)
                out_ref[m, at : at + 128, at : at + 128] = value.astype(jnp.bfloat16)


GROUP = 4


def unpack(packed):
    return pl.pallas_call(
        unpack_kernel,
        grid=(MOST // GROUP,),
        out_shape=jax.ShapeDtypeStruct((MOST, BLK, BLK), jnp.bfloat16),
        in_specs=[pl.BlockSpec((GROUP, ROWS, 128), lambda i: (i, 0, 0))],
        out_specs=pl.BlockSpec((GROUP, BLK, BLK), lambda i: (i, 0, 0)),
        compiler_params=pltpu.CompilerParams(vmem_limit_bytes=LIMIT),
        name="unpack",
    )(packed)


def body(hidden_acts, out_grad, owners):
    packed, grad, table = gather(hidden_acts, out_grad, owners)
    ways = [functools.partial(deliver, steps, table, packed, grad) for steps in STEPS]
    ways.append(lambda: deliver_any(owners, jnp.concatenate([packed, roots(grad)])))
    arrived = lax.switch(table[WHICH, 0], ways)
    return unpack(arrived)[None, None]


def solution(mesh):
    placed = (P("dp", "mp"), P("dp", None), P("dp", "mp", None))
    return jax.shard_map(
        body, mesh=mesh, in_specs=placed, out_specs=P("dp", "mp", None, None, None), check_vma=False
    )
```

```python
import functools

import jax
import jax.numpy as jnp
import numpy as np
from jax import lax
from jax.experimental import pallas as pl
from jax.experimental.pallas import tpu as pltpu
from jax.sharding import PartitionSpec as P

MESH = pl.DeviceIdType.MESH
BLK = 512
STATS = 8
CAP = 2
MOST = 12
ROWS = 1040
STEPS = (7, 8, 9)
STEPS_MAX = STEPS[-1]
WHICH = 4 * STEPS_MAX + MOST
TABLE = WHICH + 8
RULES = (((0, 2, 1, 3), 0), ((0, 2, 1, 3), 1), ((0, 2, 1, 3), 2), ((1, 3, 0, 2), 2))
OFF = ((0, 1), (0, 2), (0, 3), (1, 2), (1, 3), (2, 3))
LIMIT = 56 * 1024 * 1024


def gather_kernel(own, hid, og, hop_ref, packed_ref, grad_ref, table_ref, hid_all, og_all, own_rows, own_all, tile_ref, trials, counts, raw, acc, lead, ss, rs, ls, rs1, rso):
    r, c = lax.axis_index("dp"), lax.axis_index("mp")
    y, k = r // 2, r % 2
    z, x = c // 4, c % 4
    sib = (2 * y + 1 - k, c)

    def yn(dy, core):
        return (2 * ((y + dy) % 4) + core, c)

    a = z * (1 - k) + x * k
    b = x * (1 - k) + z * k

    def plane(aa, bb):
        zz = aa * (1 - k) + bb * k
        xx = bb * (1 - k) + aa * k
        return (r, zz * 4 + xx)

    bp, bm = plane(a, (b + 1) % 4), plane(a, (b + 3) % 4)
    ap, am = plane((a + 1) % 4, b), plane((a + 3) % 4, b)
    rows = [sib] + [yn(dy, core) for dy in (1, 2, 3) for core in (0, 1)]
    along_x = [(r, z * 4 + (x + n) % 4) for n in (1, 2, 3)]
    along_z = [(r, (z + n) % 4 * 4 + x) for n in (1, 2, 3)]

    def columns(row):
        return pl.ds(pl.multiple_of(row * 1024, 1024), 1024)

    l0 = pltpu.make_async_copy(og.at[:, :, :, columns(r)], og_all.at[0, k], ls.at[0])
    l1 = pltpu.make_async_copy(hid, raw, ls.at[1])
    l1.start()
    l0.start()

    barrier = pltpu.get_barrier_semaphore()
    partners = rows + along_x + along_z
    for dev in partners:
        pl.semaphore_signal(barrier, inc=1, device_id=dev, device_id_type=MESH)
    l1.wait()
    for p in (0, 1):
        hid_all[0, k, p] = raw[:, 512 * p : 512 * p + 512].T
    pl.semaphore_wait(barrier, len(partners))

    sent = []

    def send(src, dst, dev, landed=None):
        i = len(sent)
        landed = rs.at[i] if landed is None else landed
        copy = pltpu.make_async_remote_copy(
            src_ref=src, dst_ref=dst, send_sem=ss.at[i], recv_sem=landed, device_id=dev, device_id_type=MESH
        )
        copy.start()
        sent.append(copy)
        return copy

    def await_copy(ref, sem):
        pltpu.make_async_copy(ref, ref, sem).wait()

    line = lax.broadcasted_iota(jnp.int32, (8, 128), 0)
    lists = jnp.zeros((8, 128), jnp.int32)
    for j in range(STATS):
        lists = jnp.where(line == j, own[0, 0, j], lists)
    tile_ref[...] = lists
    own_rows[r] = lists
    for n, dev in enumerate(rows):
        send(tile_ref, own_rows.at[r], dev, rso.at[r])
    for dy in (1, 3, 2):
        for core in (0, 1):
            aa = z * (1 - core) + x * core
            bb = x * (1 - core) + z * core
            row = 2 * ((y + dy) % 4) + core
            send(og.at[aa, bb, :, columns(row)], og_all.at[4 - dy, k, aa, bb], yn(dy, core), rs1.at[4 - dy, k])
    sib_og = send(og.at[:, :, :, columns(2 * y + 1 - k)], og_all.at[0, k], sib)
    sib_hid = send(hid_all.at[0, k], hid_all.at[0, k], sib)

    sa, sb, ra, rb, hp, hm, fw = ({} for _ in range(7))

    def stage_a(d):
        for core in (0, 1):
            await_copy(og_all.at[d, core, a, b], rs1.at[d, core])
        sa[d, 0] = send(og_all.at[d, :, a, b], og_all.at[d, :, a, b], bp)
        sa[d, 1] = send(og_all.at[d, :, a, b], og_all.at[d, :, a, b], bm)

    def relay_a(d):
        sa[d, 0].wait_recv()
        ra[d, 0] = send(og_all.at[d, 0, a, (b + 3) % 4], og_all.at[d, 0, a, (b + 3) % 4], bp)
        sa[d, 1].wait_recv()
        ra[d, 1] = send(og_all.at[d, 1, a, (b + 1) % 4], og_all.at[d, 1, a, (b + 1) % 4], bm)

    def stage_b(d):
        ra[d, 0].wait_recv()
        ra[d, 1].wait_recv()
        sb[d, 0] = send(og_all.at[d, :, a], og_all.at[d, :, a], ap)
        sb[d, 1] = send(og_all.at[d, :, a], og_all.at[d, :, a], am)

    def relay_b(d):
        sb[d, 0].wait_recv()
        rb[d, 0] = send(og_all.at[d, 0, (a + 3) % 4], og_all.at[d, 0, (a + 3) % 4], ap)
        sb[d, 1].wait_recv()
        rb[d, 1] = send(og_all.at[d, 1, (a + 1) % 4], og_all.at[d, 1, (a + 1) % 4], am)

    def part(ref, h, p):
        return ref.at[p, :, pl.ds(256 * h, 256)]

    def send_own(way, h, p):
        if way == 0:
            hp[h, p] = send(part(hid_all.at[0, k], h, p), part(hid_all.at[3, k], h, p), yn(1, k))
        else:
            hm[h, p] = send(part(hid_all.at[0, k], h, p), part(hid_all.at[1, k], h, p), yn(3, k))

    def forward(d, h, p):
        ref = part(hid_all.at[d, k], h, p)
        fw[d, h, p] = send(ref, ref, sib)

    def arrive(way, h, p):
        d = 3 if way == 0 else 1
        (hp if way == 0 else hm)[h, p].wait_recv()
        if h == way:
            relay[way, p] = send(part(hid_all.at[d, k], h, p), part(hid_all.at[2, k], h, p), yn(1 if way == 0 else 3, k))
        forward(d, h, p)

    def relayed(way, p):
        relay[way, p].wait_recv()
        forward(2, way, p)

    def whole(d, p):
        fw[d, 0, p].wait_recv()
        fw[d, 1, p].wait_recv()

    def whole_og(d):
        rb[d, 0].wait_recv()
        rb[d, 1].wait_recv()

    def add_products(d, p):
        def tile(i, carry):
            at = pl.ds(pl.multiple_of(512 * p + i * 256, 256), 256)
            here = pl.ds(pl.multiple_of(i * 256, 256), 256)
            left = jnp.concatenate([hid_all[d, core, p, here, :] for core in (0, 1)], axis=1)
            prod = dot(left, og_all[d].reshape(1024, 1024), ((1,), (0,)))
            if d == 0:
                acc[at, :] = prod
            elif d == 2:
                ref = lead if p == 0 else grad_ref
                ref[here, :] = (acc[at, :] + prod).astype(jnp.bfloat16)
            else:
                acc[at, :] += prod
            return carry

        lax.fori_loop(0, 2, tile, 0)

    relay = {}
    stage_a(1)
    stage_a(3)
    send_own(0, 0, 0)
    send_own(1, 1, 0)
    send_own(0, 1, 0)
    send_own(1, 0, 0)
    stage_a(2)
    relay_a(1)
    relay_a(3)
    stage_b(1)
    group = lax.broadcasted_iota(jnp.int32, (8, 128), 1) // 16
    for dy in range(8):
        pl.when(dy != r)(lambda dy=dy: await_copy(own_rows.at[dy], rso.at[dy]))
    for dy in range(8):
        lists = jnp.where(group == dy, own_rows[dy], lists)
    own_all[z, x] = lists
    own_x = [send(own_all.at[z, x], own_all.at[z, x], dev) for dev in along_x]
    relay_a(2)
    stage_b(3)
    for copy in own_x:
        copy.wait_recv()
    own_z = [send(own_all.at[z], own_all.at[z], dev) for dev in along_z]
    stage_b(2)
    l0.wait()
    sib_og.wait_recv()
    sib_hid.wait_recv()
    arrive(0, 0, 0)
    send_own(0, 0, 1)
    arrive(1, 1, 0)
    send_own(1, 1, 1)
    add_products(0, 0)
    add_products(0, 1)
    relay_b(1)
    arrive(0, 1, 0)
    send_own(0, 1, 1)
    arrive(1, 0, 0)
    send_own(1, 0, 1)
    for copy in own_z:
        copy.wait_recv()
    counts[...] = jnp.zeros_like(counts)
    plan_rules(own_all, hop_ref, trials, counts, (0, 1))
    relay_b(3)
    relayed(0, 0)
    relayed(1, 0)
    plan_rules(own_all, hop_ref, trials, counts, (2, 3))
    plan_choice(trials, counts, table_ref)
    arrive(0, 0, 1)
    arrive(1, 1, 1)
    relay_b(2)
    whole_og(1)
    whole(1, 0)
    add_products(1, 0)
    arrive(0, 1, 1)
    arrive(1, 0, 1)
    whole_og(3)
    whole(3, 0)
    add_products(3, 0)
    whole(1, 1)
    add_products(1, 1)
    whole(3, 1)
    add_products(3, 1)
    whole_og(2)
    whole(2, 0)
    add_products(2, 0)

    def pair(q, carry):
        def store(kind, at, value):
            packed_ref[2 * q + kind, at : at + value.shape[0], :] = value

        make_pair(lead[:, pl.ds(pl.multiple_of(q * BLK, BLK), BLK)], store)
        return carry

    lax.fori_loop(0, 1, pair, 0)
    relayed(0, 1)
    relayed(1, 1)
    lax.fori_loop(1, 2, pair, 0)
    whole(2, 1)
    add_products(2, 1)
    for copy in sent:
        copy.wait_send()


SENDS = 7 + 6 + 2 + 8 + 6 + 6 + 6 + 6 + 4 + 12 + 3 + 3


def gather(hid, og, own):
    return pl.pallas_call(
        gather_kernel,
        out_shape=(
            jax.ShapeDtypeStruct((4, ROWS, 128), jnp.bfloat16),
            jax.ShapeDtypeStruct((512, 1024), jnp.bfloat16),
            jax.ShapeDtypeStruct((TABLE, 128), jnp.int32),
        ),
        in_specs=[
            pl.BlockSpec(memory_space=pltpu.SMEM),
            pl.BlockSpec(memory_space=pl.ANY),
            pl.BlockSpec(memory_space=pl.ANY),
            pl.BlockSpec(memory_space=pltpu.VMEM),
        ],
        out_specs=(pl.BlockSpec(memory_space=pltpu.VMEM),) * 3,
        scratch_shapes=[
            pltpu.VMEM((4, 2, 2, 512, 512), jnp.bfloat16),
            pltpu.VMEM((4, 2, 4, 4, 32, 1024), jnp.bfloat16),
            pltpu.VMEM((8, 8, 128), jnp.int32),
            pltpu.VMEM((4, 4, 8, 128), jnp.int32),
            pltpu.VMEM((8, 128), jnp.int32),
            pltpu.VMEM((len(RULES), WHICH, 128), jnp.int32),
            pltpu.VMEM((16, 128), jnp.float32),
            pltpu.VMEM((512, 1024), jnp.bfloat16),
            pltpu.VMEM((1024, 1024), jnp.float32),
            pltpu.VMEM((512, 1024), jnp.bfloat16),
            pltpu.SemaphoreType.DMA((SENDS,)),
            pltpu.SemaphoreType.DMA((SENDS,)),
            pltpu.SemaphoreType.DMA((2,)),
            pltpu.SemaphoreType.DMA((4, 2)),
            pltpu.SemaphoreType.DMA((8,)),
        ],
        compiler_params=pltpu.CompilerParams(collective_id=0, has_side_effects=True, vmem_limit_bytes=LIMIT),
        name="gather",
    )(own, hid, og.reshape(4, 4, 32, 8192), jnp.asarray(hop_matrix(), jnp.bfloat16))


def dot(left, right, dims):
    return lax.dot_general(left, right, (dims, ((), ())), preferred_element_type=jnp.float32)


def patched(matrix, blocks):
    lines = []
    for i in range(4):
        cells = [matrix[128 * i : 128 * i + 128, 128 * j : 128 * j + 128] for j in range(4)]
        cells[i] = blocks[i]
        lines.append(jnp.concatenate(cells, axis=1))
    return jnp.concatenate(lines, axis=0)


def diagonals(matrix):
    return [matrix[128 * i : 128 * i + 128, 128 * i : 128 * i + 128] for i in range(4)]


def make_pair(g, store):
    rows = lax.broadcasted_iota(jnp.int32, (128, 128), 0)
    cols = lax.broadcasted_iota(jnp.int32, (128, 128), 1)
    diag = rows == cols
    unit = diag.astype(jnp.float32)
    plain = ((1,), (0,))
    both = (0, 1)
    quarter = jnp.asarray(-0.25, jnp.bfloat16)

    def narrow(value):
        return value.astype(jnp.bfloat16)

    stats = [narrow(dot(g, g, ((1 - kind,), (1 - kind,)))) for kind in both]
    coupled, first, scale = [None] * 2, [None] * 2, [None] * 2
    for kind in both:
        sym = stats[kind].astype(jnp.float32)
        trace = sum(jnp.where(diag, block, 0.0) for block in diagonals(sym))
        mean = jnp.sum(trace, keepdims=True) / BLK
        norm = jnp.sqrt(jnp.sum(sym * sym, keepdims=True) + (0.21 * BLK) * mean * mean + 1e-06)
        grow = 4.0 / norm
        spread = sym * grow
        ends = [block + unit * (0.1 * mean * grow) for block in diagonals(spread)]
        body_b = narrow(spread)
        coupled[kind] = patched(body_b, [narrow(block) for block in ends])
        first[kind] = patched(body_b * quarter, [narrow(1.25 * unit - 0.25 * block) for block in ends])
        scale[kind] = jnp.sqrt(jnp.sqrt(grow)) * jnp.sqrt(jnp.sqrt(1.1 * mean))
    two = [narrow(dot(first[kind], first[kind], plain)) for kind in both]
    four = [narrow(dot(two[kind], two[kind], plain)) for kind in both]
    second = []
    for kind in both:
        after = dot(four[kind], coupled[kind], plain) * -0.25
        second.append(patched(narrow(after), [narrow(1.25 * unit + block) for block in diagonals(after)]))
    for kind in both:
        top = dot(first[kind][:256], second[kind], plain) * scale[kind]
        low = dot(first[kind][256:], second[kind][:, 256:], plain) * scale[kind]

        def block(i, j):
            if i < 2:
                return top[128 * i : 128 * i + 128, 128 * j : 128 * j + 128]
            return low[128 * (i - 2) : 128 * (i - 1), 128 * (j - 2) : 128 * (j - 1)]

        for n, (i, j) in enumerate(OFF):
            store(kind, 128 * n, narrow(block(i, j)))
        spare = jnp.zeros((16, 128), jnp.float32)
        for n in (0, 1):
            lead, tail = block(2 * n, 2 * n), block(2 * n + 1, 2 * n + 1)
            store(kind, 128 * (6 + n), narrow(jnp.where(rows <= cols, lead, tail)))
            line = jnp.sum(jnp.where(diag, tail, 0.0), axis=0, keepdims=True)
            spare = jnp.where(rows[:16] == n, line, spare)
        store(kind, 1024, narrow(spare))


def roots_kernel(g_ref, out_ref):
    def store(kind, at, value):
        out_ref[kind, at : at + value.shape[0], :] = value

    make_pair(g_ref[...], store)


def roots(grad):
    return pl.pallas_call(
        roots_kernel,
        grid=(2,),
        out_shape=jax.ShapeDtypeStruct((4, ROWS, 128), jnp.bfloat16),
        in_specs=[pl.BlockSpec((BLK, BLK), lambda i: (0, i))],
        out_specs=pl.BlockSpec((2, ROWS, 128), lambda i: (i, 0, 0)),
        compiler_params=pltpu.CompilerParams(vmem_limit_bytes=LIMIT),
        name="roots",
    )(grad)


def hop_matrix():
    out = np.zeros((4, 128, 256), np.float32)
    for lane in range(128):
        g, n = lane // 16, lane % 16
        z, x = n // 4, n % 4
        targets = (z * 4 + (x + 1) % 4, z * 4 + (x + 3) % 4, (z + 1) % 4 * 4 + x, (z + 3) % 4 * 4 + x)
        for link, to in enumerate(targets):
            out[link, lane, g * 16 + to] = 1.0
            out[link, lane, 128 + g * 16 + to] = link
    return out.reshape(512, 256)


def plan_state(own_ref):
    lane = lax.broadcasted_iota(jnp.int32, (128, 128), 1)
    item = lax.broadcasted_iota(jnp.int32, (128, 128), 0)
    dest = jnp.concatenate([own_ref[c // 4, c % 4] for c in range(16)], axis=0)
    return lane, item, dest, lane & 15


def plan_rules(own_ref, hop_ref, trial_ref, count_ref, rules):
    lane, item, dest, node = plan_state(own_ref)
    home = dest == node
    homef = home.astype(jnp.float32)
    dx = (dest - node) & 3
    dz = ((dest >> 2) - (node >> 2)) & 3
    wants = ((dx == 1) | (dx == 2), dx >= 2, (dz == 1) | (dz == 2), dz >= 2)
    ways = sum(w.astype(jnp.int32) for w in wants)
    far = jnp.where(dx == 3, 1, dx) + jnp.where(dz == 3, 1, dz)
    origin = ((item >> 3) == node).astype(jnp.float32)
    late = (item & 7) >= 4
    below = (lane < item).astype(jnp.bfloat16)
    rank = dot(below, home.astype(jnp.bfloat16), ((1,), (0,)))
    hop = hop_ref[...]
    keys, here, slot = {}, {}, {}
    for v in rules:
        tie = (128 - item, item + 1, ((item * 37) & 127) + 1)[RULES[v][1]]
        key = ((4 - ways + far) * 1024 + tie).astype(jnp.float32)
        keys[v] = [jnp.where(w, key, 0.0) for w in wants]
        here[v] = jnp.where(late, 0.0, origin)
        slot[v] = (item & 7).astype(jnp.float32)
    for t in range(STEPS_MAX):
        for v in rules:
            if t == 1:
                here[v] = here[v] + jnp.where(late, origin, 0.0)
            moves = [None] * 4
            for link in RULES[v][0]:
                value = keys[v][link] * here[v]
                best = jnp.max(value, axis=0, keepdims=True)
                win = jnp.where((value == best) & (value > 0.0), 1.0, 0.0)
                here[v] = here[v] - win
                pick = jnp.sum(win * slot[v], axis=0, keepdims=True)
                trial_ref[v, 4 * t + link : 4 * t + link + 1, :] = pick.astype(jnp.int32)
                moves[link] = win.astype(jnp.bfloat16)
            landed = dot(jnp.concatenate(moves, axis=1), hop, ((1,), (0,)))
            new = landed[:, :128]
            here[v] = here[v] + new
            slot[v] = jnp.where(new > 0.5, landed[:, 128:] + (STATS + 4.0 * t), slot[v])
            if t + 1 in STEPS:
                row = len(STEPS) * v + STEPS.index(t + 1)
                count_ref[row : row + 1, :] = jnp.sum(here[v] * homef, axis=0, keepdims=True)
    for v in rules:
        for n in range(MOST):
            mine = jnp.where(home & (rank == float(n)), slot[v] + 1.0, 0.0)
            row = 4 * STEPS_MAX + n
            trial_ref[v, row : row + 1, :] = jnp.sum(mine, axis=0, keepdims=True).astype(jnp.int32) - 1


def plan_choice(trial_ref, count_ref, out_ref):
    left = lax.broadcasted_iota(jnp.int32, (128, 128), 0) // 16
    right = lax.broadcasted_iota(jnp.int32, (128, 128), 1) // 16
    same = (left == right).astype(jnp.bfloat16)
    done = (dot(count_ref[...].astype(jnp.bfloat16), same, ((1,), (0,))) == 128.0).astype(jnp.float32)
    score = [sum(done[len(STEPS) * v + n : len(STEPS) * v + n + 1] for n in range(len(STEPS))) for v in range(len(RULES))]
    best, table = score[0], trial_ref[0]
    for v in range(1, len(RULES)):
        better = score[v] > best
        table = jnp.where(better, trial_ref[v], table)
        best = jnp.maximum(best, score[v])
    out_ref[:WHICH, :] = table
    which = len(STEPS) - jnp.min(best, keepdims=True)
    out_ref[WHICH:, :] = jnp.broadcast_to(which, (8, 128)).astype(jnp.int32)


def deliver_kernel(steps, table, packed, grad, out, pool, recv, stage, ss, rs):
    r, c = lax.axis_index("dp"), lax.axis_index("mp")
    z, x = c // 4, c % 4
    me = r * 16 + c
    peers = (
        (r, z * 4 + (x + 1) % 4),
        (r, z * 4 + (x + 3) % 4),
        (r, (z + 1) % 4 * 4 + x),
        (r, (z + 3) % 4 * 4 + x),
    )

    def pair(q, carry):
        def store(kind, at, value):
            pool[4 + 2 * q + kind, at : at + value.shape[0], :] = value

        make_pair(grad[:, pl.ds(pl.multiple_of(q * BLK, BLK), BLK)], store)
        return carry

    def copy(t, link, half):
        return pltpu.make_async_remote_copy(
            src_ref=stage.at[t % 2, link, HALVES[half]],
            dst_ref=recv.at[t, link, HALVES[half]],
            send_sem=ss.at[t % 2, link, half],
            recv_sem=rs.at[t, link, half],
            device_id=peers[link],
            device_id_type=MESH,
        )

    def land(t, half):
        for link in range(4):
            copy(t, link, half).wait_recv()
            pool[STATS + 4 * t + link, HALVES[half], :] = recv[t, link, HALVES[half], :]

    def push(t, half):
        for link in range(4):
            stage[t % 2, link, HALVES[half], :] = pool[table[4 * t + link, me], HALVES[half], :]
            copy(t, link, half).start()

    def settle(t, half):
        for link in range(4):
            copy(t, link, half).wait_send()

    barrier = pltpu.get_barrier_semaphore()
    for dev in peers:
        pl.semaphore_signal(barrier, inc=1, device_id=dev, device_id_type=MESH)
    pool[:4] = packed[...]
    pl.semaphore_wait(barrier, 4)
    push(0, 0)
    push(0, 1)
    lax.fori_loop(0, 2, pair, 0)
    for half in (0, 1):
        land(0, half)
        push(1, half)

    def step(t, carry):
        for half in (0, 1):
            land(t - 1, half)
            settle(t - 2, half)
            push(t, half)
        return carry

    lax.fori_loop(2, steps, step, 0)
    for half in (0, 1):
        land(steps - 1, half)
    for t in (steps - 2, steps - 1):
        for half in (0, 1):
            settle(t, half)
    for n in range(MOST):
        at = table[4 * STEPS_MAX + n, me]
        block = pool[jnp.maximum(at, 0)]
        keep = (at >= 0).astype(jnp.bfloat16)
        out[n] = block * keep


HALVES = (pl.ds(0, 528), pl.ds(528, 512))


def deliver(steps, table, packed, grad):
    return pl.pallas_call(
        functools.partial(deliver_kernel, steps),
        out_shape=jax.ShapeDtypeStruct((MOST, ROWS, 128), jnp.bfloat16),
        in_specs=[pl.BlockSpec(memory_space=pltpu.SMEM)] + [pl.BlockSpec(memory_space=pltpu.VMEM)] * 2,
        out_specs=pl.BlockSpec(memory_space=pltpu.VMEM),
        scratch_shapes=[
            pltpu.VMEM((STATS + 4 * steps, ROWS, 128), jnp.bfloat16),
            pltpu.VMEM((steps, 4, ROWS, 128), jnp.bfloat16),
            pltpu.VMEM((2, 4, ROWS, 128), jnp.bfloat16),
            pltpu.SemaphoreType.DMA((2, 4, 2)),
            pltpu.SemaphoreType.DMA((steps, 4, 2)),
        ],
        compiler_params=pltpu.CompilerParams(
            collective_id=steps, has_side_effects=True, vmem_limit_bytes=LIMIT
        ),
        name="deliver",
    )(table, packed, grad)


def deliver_any(owners, packed):
    myself = lax.axis_index("mp")
    lists = lax.all_gather(owners, "mp", axis=1, tiled=True)[0]
    mine = lists[myself]
    count = lists.shape[0]
    match = (mine[None, :] == jnp.arange(count, dtype=jnp.int32)[:, None]).astype(jnp.int32)
    rank = jnp.cumsum(match, axis=1) - match
    select = (match[:, None, :] > 0) & (rank[:, None, :] == jnp.arange(CAP, dtype=jnp.int32)[None, :, None])
    index = jnp.sum(select.astype(jnp.int32) * jnp.arange(STATS, dtype=jnp.int32), axis=2)
    outgoing = packed[index.reshape(-1)].reshape(count, CAP, ROWS, 128)
    received = lax.all_to_all(outgoing, "mp", split_axis=0, concat_axis=0, tiled=True)
    counts = jnp.sum((lists == myself).astype(jnp.int32), axis=1)
    valid = (jnp.arange(CAP, dtype=jnp.int32)[None, :] < counts[:, None]).reshape(-1).astype(jnp.int32)
    before = jnp.cumsum(valid) - valid
    chosen = (valid[None, :] > 0) & (before[None, :] == jnp.arange(MOST, dtype=jnp.int32)[:, None])
    index = jnp.sum(chosen.astype(jnp.int32) * jnp.arange(count * CAP, dtype=jnp.int32), axis=1)
    picked = received.reshape(count * CAP, ROWS, 128)[index]
    return jnp.where(jnp.any(chosen, axis=1)[:, None, None], picked, jnp.zeros_like(picked))


def unpack_kernel(src, dst, packed, whole, came, left):
    rows = lax.broadcasted_iota(jnp.int32, (128, 128), 0)
    cols = lax.broadcasted_iota(jnp.int32, (128, 128), 1)

    def fetch(m):
        return pltpu.make_async_copy(src.at[m], packed.at[m], came.at[m])

    def write(m):
        return pltpu.make_async_copy(whole.at[m], dst.at[m], left.at[m])

    def place(m, i, j, value):
        whole[m, 128 * i : 128 * i + 128, 128 * j : 128 * j + 128] = value

    for m in range(MOST):
        fetch(m).start()

    def one(m, carry):
        fetch(m).wait()
        flipped = packed[m, :1024, :].T
        for n, (i, j) in enumerate(OFF):
            place(m, i, j, packed[m, 128 * n : 128 * n + 128, :])
            place(m, j, i, flipped[:, 128 * n : 128 * n + 128])
        spare = packed[m, 1024:, :].astype(jnp.float32)
        for n in (0, 1):
            both = packed[m, 128 * (6 + n) : 128 * (7 + n), :].astype(jnp.float32)
            other = flipped[:, 128 * (6 + n) : 128 * (7 + n)].astype(jnp.float32)
            first = jnp.where(rows <= cols, both, other)
            second = jnp.where(rows > cols, both, other)
            second = jnp.where(rows == cols, spare[n : n + 1, :], second)
            place(m, 2 * n, 2 * n, first.astype(jnp.bfloat16))
            place(m, 2 * n + 1, 2 * n + 1, second.astype(jnp.bfloat16))
        write(m).start()
        return carry

    lax.fori_loop(0, MOST, one, 0)
    for m in range(MOST):
        write(m).wait()


def unpack(packed):
    return pl.pallas_call(
        unpack_kernel,
        out_shape=jax.ShapeDtypeStruct((MOST, BLK, BLK), jnp.bfloat16),
        in_specs=[pl.BlockSpec(memory_space=pl.ANY)],
        out_specs=pl.BlockSpec(memory_space=pl.ANY),
        scratch_shapes=[
            pltpu.VMEM((MOST, ROWS, 128), jnp.bfloat16),
            pltpu.VMEM((MOST, BLK, BLK), jnp.bfloat16),
            pltpu.SemaphoreType.DMA((MOST,)),
            pltpu.SemaphoreType.DMA((MOST,)),
        ],
        compiler_params=pltpu.CompilerParams(vmem_limit_bytes=LIMIT),
        name="unpack",
    )(packed)


def body(hidden_acts, out_grad, owners):
    packed, grad, table = gather(hidden_acts, out_grad, owners)
    ways = [functools.partial(deliver, steps, table, packed, grad) for steps in STEPS]
    ways.append(lambda: deliver_any(owners, jnp.concatenate([packed, roots(grad)])))
    arrived = lax.switch(table[WHICH, 0], ways)
    return unpack(arrived)[None, None]


def solution(mesh):
    placed = (P("dp", "mp"), P("dp", None), P("dp", "mp", None))
    return jax.shard_map(
        body, mesh=mesh, in_specs=placed, out_specs=P("dp", "mp", None, None, None), check_vma=False
    )
```

```python
import functools

import jax
import jax.numpy as jnp
import numpy as np
from jax import lax
from jax.experimental import pallas as pl
from jax.experimental.pallas import tpu as pltpu
from jax.sharding import PartitionSpec as P

MESH = pl.DeviceIdType.MESH
BLK = 512
STATS = 8
CAP = 2
MOST = 12
ROWS = 1040
STEPS = (7, 8, 9)
STEPS_MAX = STEPS[-1]
WHICH = 4 * STEPS_MAX + MOST
TABLE = WHICH + 8
RULES = (((0, 2, 1, 3), 0), ((0, 2, 1, 3), 1), ((0, 2, 1, 3), 2), ((1, 3, 0, 2), 2))
OFF = ((0, 1), (0, 2), (0, 3), (1, 2), (1, 3), (2, 3))
LIMIT = 56 * 1024 * 1024


def gather_kernel(own, hid, og, hop_ref, packed_ref, grad_ref, table_ref, hid_all, og_all, own_rows, own_all, tile_ref, trials, counts, raw, acc, lead, ss, rs, ls, rs1, rso):
    r, c = lax.axis_index("dp"), lax.axis_index("mp")
    y, k = r // 2, r % 2
    z, x = c // 4, c % 4
    sib = (2 * y + 1 - k, c)

    def yn(dy, core):
        return (2 * ((y + dy) % 4) + core, c)

    a = z * (1 - k) + x * k
    b = x * (1 - k) + z * k

    def plane(aa, bb):
        zz = aa * (1 - k) + bb * k
        xx = bb * (1 - k) + aa * k
        return (r, zz * 4 + xx)

    bp, bm = plane(a, (b + 1) % 4), plane(a, (b + 3) % 4)
    ap, am = plane((a + 1) % 4, b), plane((a + 3) % 4, b)
    rows = [sib] + [yn(dy, core) for dy in (1, 2, 3) for core in (0, 1)]
    along_x = [(r, z * 4 + (x + n) % 4) for n in (1, 2, 3)]
    along_z = [(r, (z + n) % 4 * 4 + x) for n in (1, 2, 3)]

    def columns(row):
        return pl.ds(pl.multiple_of(row * 1024, 1024), 1024)

    l0 = pltpu.make_async_copy(og.at[:, :, :, columns(r)], og_all.at[0, k], ls.at[0])
    l1 = pltpu.make_async_copy(hid, raw, ls.at[1])
    l1.start()
    l0.start()

    barrier = pltpu.get_barrier_semaphore()
    partners = rows + along_x + along_z
    for dev in partners:
        pl.semaphore_signal(barrier, inc=1, device_id=dev, device_id_type=MESH)
    l1.wait()
    for p in (0, 1):
        hid_all[0, k, p] = raw[:, 512 * p : 512 * p + 512].T
    pl.semaphore_wait(barrier, len(partners))

    sent = []

    def send(src, dst, dev, landed=None):
        i = len(sent)
        landed = rs.at[i] if landed is None else landed
        copy = pltpu.make_async_remote_copy(
            src_ref=src, dst_ref=dst, send_sem=ss.at[i], recv_sem=landed, device_id=dev, device_id_type=MESH
        )
        copy.start()
        sent.append(copy)
        return copy

    def await_copy(ref, sem):
        pltpu.make_async_copy(ref, ref, sem).wait()

    line = lax.broadcasted_iota(jnp.int32, (8, 128), 0)
    lists = jnp.zeros((8, 128), jnp.int32)
    for j in range(STATS):
        lists = jnp.where(line == j, own[0, 0, j], lists)
    tile_ref[...] = lists
    own_rows[r] = lists
    for n, dev in enumerate(rows):
        send(tile_ref, own_rows.at[r], dev, rso.at[r])
    for dy in (1, 3, 2):
        for core in (0, 1):
            aa = z * (1 - core) + x * core
            bb = x * (1 - core) + z * core
            row = 2 * ((y + dy) % 4) + core
            send(og.at[aa, bb, :, columns(row)], og_all.at[4 - dy, k, aa, bb], yn(dy, core), rs1.at[4 - dy, k])
    sib_og = send(og.at[:, :, :, columns(2 * y + 1 - k)], og_all.at[0, k], sib)
    sib_hid = send(hid_all.at[0, k], hid_all.at[0, k], sib)

    sa, sb, ra, rb, hp, hm, fw = ({} for _ in range(7))

    def stage_a(d):
        for core in (0, 1):
            await_copy(og_all.at[d, core, a, b], rs1.at[d, core])
        sa[d, 0] = send(og_all.at[d, :, a, b], og_all.at[d, :, a, b], bp)
        sa[d, 1] = send(og_all.at[d, :, a, b], og_all.at[d, :, a, b], bm)

    def relay_a(d):
        sa[d, 0].wait_recv()
        ra[d, 0] = send(og_all.at[d, 0, a, (b + 3) % 4], og_all.at[d, 0, a, (b + 3) % 4], bp)
        sa[d, 1].wait_recv()
        ra[d, 1] = send(og_all.at[d, 1, a, (b + 1) % 4], og_all.at[d, 1, a, (b + 1) % 4], bm)

    def stage_b(d):
        ra[d, 0].wait_recv()
        ra[d, 1].wait_recv()
        sb[d, 0] = send(og_all.at[d, :, a], og_all.at[d, :, a], ap)
        sb[d, 1] = send(og_all.at[d, :, a], og_all.at[d, :, a], am)

    def relay_b(d):
        sb[d, 0].wait_recv()
        rb[d, 0] = send(og_all.at[d, 0, (a + 3) % 4], og_all.at[d, 0, (a + 3) % 4], ap)
        sb[d, 1].wait_recv()
        rb[d, 1] = send(og_all.at[d, 1, (a + 1) % 4], og_all.at[d, 1, (a + 1) % 4], am)

    def part(ref, h, p):
        return ref.at[p, :, pl.ds(256 * h, 256)]

    def send_own(way, h, p):
        if way == 0:
            hp[h, p] = send(part(hid_all.at[0, k], h, p), part(hid_all.at[3, k], h, p), yn(1, k))
        else:
            hm[h, p] = send(part(hid_all.at[0, k], h, p), part(hid_all.at[1, k], h, p), yn(3, k))

    def forward(d, h, p):
        ref = part(hid_all.at[d, k], h, p)
        fw[d, h, p] = send(ref, ref, sib)

    def arrive(way, h, p):
        d = 3 if way == 0 else 1
        (hp if way == 0 else hm)[h, p].wait_recv()
        if h == way:
            relay[way, p] = send(part(hid_all.at[d, k], h, p), part(hid_all.at[2, k], h, p), yn(1 if way == 0 else 3, k))
        forward(d, h, p)

    def relayed(way, p):
        relay[way, p].wait_recv()
        forward(2, way, p)

    def whole(d, p):
        fw[d, 0, p].wait_recv()
        fw[d, 1, p].wait_recv()

    def whole_og(d):
        rb[d, 0].wait_recv()
        rb[d, 1].wait_recv()

    def add_products(d, p):
        def tile(i, carry):
            at = pl.ds(pl.multiple_of(512 * p + i * 256, 256), 256)
            here = pl.ds(pl.multiple_of(i * 256, 256), 256)
            left = jnp.concatenate([hid_all[d, core, p, here, :] for core in (0, 1)], axis=1)
            prod = dot(left, og_all[d].reshape(1024, 1024), ((1,), (0,)))
            if d == 0:
                acc[at, :] = prod
            elif d == 2:
                ref = lead if p == 0 else grad_ref
                ref[here, :] = (acc[at, :] + prod).astype(jnp.bfloat16)
            else:
                acc[at, :] += prod
            return carry

        lax.fori_loop(0, 2, tile, 0)

    relay = {}
    stage_a(1)
    stage_a(3)
    send_own(0, 0, 0)
    send_own(1, 1, 0)
    send_own(0, 1, 0)
    send_own(1, 0, 0)
    stage_a(2)
    relay_a(1)
    relay_a(3)
    stage_b(1)
    group = lax.broadcasted_iota(jnp.int32, (8, 128), 1) // 16
    for dy in range(8):
        pl.when(dy != r)(lambda dy=dy: await_copy(own_rows.at[dy], rso.at[dy]))
    for dy in range(8):
        lists = jnp.where(group == dy, own_rows[dy], lists)
    own_all[z, x] = lists
    own_x = [send(own_all.at[z, x], own_all.at[z, x], dev) for dev in along_x]
    relay_a(2)
    stage_b(3)
    for copy in own_x:
        copy.wait_recv()
    own_z = [send(own_all.at[z], own_all.at[z], dev) for dev in along_z]
    stage_b(2)
    l0.wait()
    sib_og.wait_recv()
    sib_hid.wait_recv()
    arrive(0, 0, 0)
    send_own(0, 0, 1)
    arrive(1, 1, 0)
    send_own(1, 1, 1)
    add_products(0, 0)
    add_products(0, 1)
    relay_b(1)
    arrive(0, 1, 0)
    send_own(0, 1, 1)
    arrive(1, 0, 0)
    send_own(1, 0, 1)
    for copy in own_z:
        copy.wait_recv()
    counts[...] = jnp.zeros_like(counts)
    plan_rules(own_all, hop_ref, trials, counts, (0, 1))
    relay_b(3)
    relayed(0, 0)
    relayed(1, 0)
    plan_rules(own_all, hop_ref, trials, counts, (2, 3))
    plan_choice(trials, counts, table_ref)
    arrive(0, 0, 1)
    arrive(1, 1, 1)
    relay_b(2)
    whole_og(1)
    whole(1, 0)
    add_products(1, 0)
    arrive(0, 1, 1)
    arrive(1, 0, 1)
    whole_og(3)
    whole(3, 0)
    add_products(3, 0)
    whole(1, 1)
    add_products(1, 1)
    whole(3, 1)
    add_products(3, 1)
    whole_og(2)
    whole(2, 0)
    add_products(2, 0)

    def pair(q, carry):
        def store(kind, at, value):
            packed_ref[2 * q + kind, at : at + value.shape[0], :] = value

        make_pair(lead[:, pl.ds(pl.multiple_of(q * BLK, BLK), BLK)], store)
        return carry

    lax.fori_loop(0, 1, pair, 0)
    relayed(0, 1)
    relayed(1, 1)
    lax.fori_loop(1, 2, pair, 0)
    whole(2, 1)
    add_products(2, 1)
    for copy in sent:
        copy.wait_send()


SENDS = 7 + 6 + 2 + 8 + 6 + 6 + 6 + 6 + 4 + 12 + 3 + 3


def gather(hid, og, own):
    return pl.pallas_call(
        gather_kernel,
        out_shape=(
            jax.ShapeDtypeStruct((4, ROWS, 128), jnp.bfloat16),
            jax.ShapeDtypeStruct((512, 1024), jnp.bfloat16),
            jax.ShapeDtypeStruct((TABLE, 128), jnp.int32),
        ),
        in_specs=[
            pl.BlockSpec(memory_space=pltpu.SMEM),
            pl.BlockSpec(memory_space=pl.ANY),
            pl.BlockSpec(memory_space=pl.ANY),
            pl.BlockSpec(memory_space=pltpu.VMEM),
        ],
        out_specs=(pl.BlockSpec(memory_space=pltpu.VMEM),) * 3,
        scratch_shapes=[
            pltpu.VMEM((4, 2, 2, 512, 512), jnp.bfloat16),
            pltpu.VMEM((4, 2, 4, 4, 32, 1024), jnp.bfloat16),
            pltpu.VMEM((8, 8, 128), jnp.int32),
            pltpu.VMEM((4, 4, 8, 128), jnp.int32),
            pltpu.VMEM((8, 128), jnp.int32),
            pltpu.VMEM((len(RULES), WHICH, 128), jnp.int32),
            pltpu.VMEM((16, 128), jnp.float32),
            pltpu.VMEM((512, 1024), jnp.bfloat16),
            pltpu.VMEM((1024, 1024), jnp.float32),
            pltpu.VMEM((512, 1024), jnp.bfloat16),
            pltpu.SemaphoreType.DMA((SENDS,)),
            pltpu.SemaphoreType.DMA((SENDS,)),
            pltpu.SemaphoreType.DMA((2,)),
            pltpu.SemaphoreType.DMA((4, 2)),
            pltpu.SemaphoreType.DMA((8,)),
        ],
        compiler_params=pltpu.CompilerParams(collective_id=0, has_side_effects=True, vmem_limit_bytes=LIMIT),
        name="gather",
    )(own, hid, og.reshape(4, 4, 32, 8192), jnp.asarray(hop_matrix(), jnp.bfloat16))


def dot(left, right, dims):
    return lax.dot_general(left, right, (dims, ((), ())), preferred_element_type=jnp.float32)


def patched(matrix, blocks):
    lines = []
    for i in range(4):
        cells = [matrix[128 * i : 128 * i + 128, 128 * j : 128 * j + 128] for j in range(4)]
        cells[i] = blocks[i]
        lines.append(jnp.concatenate(cells, axis=1))
    return jnp.concatenate(lines, axis=0)


def diagonals(matrix):
    return [matrix[128 * i : 128 * i + 128, 128 * i : 128 * i + 128] for i in range(4)]


def make_pair(g, store):
    rows = lax.broadcasted_iota(jnp.int32, (128, 128), 0)
    cols = lax.broadcasted_iota(jnp.int32, (128, 128), 1)
    diag = rows == cols
    unit = diag.astype(jnp.float32)
    plain = ((1,), (0,))
    both = (0, 1)
    quarter = jnp.asarray(-0.25, jnp.bfloat16)

    def narrow(value):
        return value.astype(jnp.bfloat16)

    stats = [narrow(dot(g, g, ((1 - kind,), (1 - kind,)))) for kind in both]
    coupled, first, scale = [None] * 2, [None] * 2, [None] * 2
    for kind in both:
        sym = stats[kind].astype(jnp.float32)
        trace = sum(jnp.where(diag, block, 0.0) for block in diagonals(sym))
        mean = jnp.sum(trace, keepdims=True) / BLK
        norm = jnp.sqrt(jnp.sum(sym * sym, keepdims=True) + (0.21 * BLK) * mean * mean + 1e-06)
        grow = 4.0 / norm
        spread = sym * grow
        ends = [block + unit * (0.1 * mean * grow) for block in diagonals(spread)]
        body_b = narrow(spread)
        coupled[kind] = patched(body_b, [narrow(block) for block in ends])
        first[kind] = patched(body_b * quarter, [narrow(1.25 * unit - 0.25 * block) for block in ends])
        scale[kind] = jnp.sqrt(jnp.sqrt(grow)) * jnp.sqrt(jnp.sqrt(1.1 * mean))
    two = [narrow(dot(first[kind], first[kind], plain)) for kind in both]
    four = [narrow(dot(two[kind], two[kind], plain)) for kind in both]
    second = []
    for kind in both:
        after = dot(four[kind], coupled[kind], plain) * -0.25
        second.append(patched(narrow(after), [narrow(1.25 * unit + block) for block in diagonals(after)]))
    for kind in both:
        top = dot(first[kind][:256], second[kind], plain) * scale[kind]
        low = dot(first[kind][256:], second[kind][:, 256:], plain) * scale[kind]

        def block(i, j):
            if i < 2:
                return top[128 * i : 128 * i + 128, 128 * j : 128 * j + 128]
            return low[128 * (i - 2) : 128 * (i - 1), 128 * (j - 2) : 128 * (j - 1)]

        for n, (i, j) in enumerate(OFF):
            store(kind, 128 * n, narrow(block(i, j)))
        spare = jnp.zeros((16, 128), jnp.float32)
        for n in (0, 1):
            lead, tail = block(2 * n, 2 * n), block(2 * n + 1, 2 * n + 1)
            store(kind, 128 * (6 + n), narrow(jnp.where(rows <= cols, lead, tail)))
            line = jnp.sum(jnp.where(diag, tail, 0.0), axis=0, keepdims=True)
            spare = jnp.where(rows[:16] == n, line, spare)
        store(kind, 1024, narrow(spare))


def roots_kernel(g_ref, out_ref):
    def store(kind, at, value):
        out_ref[kind, at : at + value.shape[0], :] = value

    make_pair(g_ref[...], store)


def roots(grad):
    return pl.pallas_call(
        roots_kernel,
        grid=(2,),
        out_shape=jax.ShapeDtypeStruct((4, ROWS, 128), jnp.bfloat16),
        in_specs=[pl.BlockSpec((BLK, BLK), lambda i: (0, i))],
        out_specs=pl.BlockSpec((2, ROWS, 128), lambda i: (i, 0, 0)),
        compiler_params=pltpu.CompilerParams(vmem_limit_bytes=LIMIT),
        name="roots",
    )(grad)


def hop_matrix():
    out = np.zeros((4, 128, 256), np.float32)
    for lane in range(128):
        g, n = lane // 16, lane % 16
        z, x = n // 4, n % 4
        targets = (z * 4 + (x + 1) % 4, z * 4 + (x + 3) % 4, (z + 1) % 4 * 4 + x, (z + 3) % 4 * 4 + x)
        for link, to in enumerate(targets):
            out[link, lane, g * 16 + to] = 1.0
            out[link, lane, 128 + g * 16 + to] = link
    return out.reshape(512, 256)


def plan_state(own_ref):
    lane = lax.broadcasted_iota(jnp.int32, (128, 128), 1)
    item = lax.broadcasted_iota(jnp.int32, (128, 128), 0)
    dest = jnp.concatenate([own_ref[c // 4, c % 4] for c in range(16)], axis=0)
    return lane, item, dest, lane & 15


def plan_rules(own_ref, hop_ref, trial_ref, count_ref, rules):
    lane, item, dest, node = plan_state(own_ref)
    home = dest == node
    homef = home.astype(jnp.float32)
    dx = (dest - node) & 3
    dz = ((dest >> 2) - (node >> 2)) & 3
    wants = ((dx == 1) | (dx == 2), dx >= 2, (dz == 1) | (dz == 2), dz >= 2)
    ways = sum(w.astype(jnp.int32) for w in wants)
    far = jnp.where(dx == 3, 1, dx) + jnp.where(dz == 3, 1, dz)
    origin = ((item >> 3) == node).astype(jnp.float32)
    late = (item & 7) >= 4
    below = (lane < item).astype(jnp.bfloat16)
    rank = dot(below, home.astype(jnp.bfloat16), ((1,), (0,)))
    hop = hop_ref[...]
    keys, here, slot = {}, {}, {}
    for v in rules:
        tie = (128 - item, item + 1, ((item * 37) & 127) + 1)[RULES[v][1]]
        key = ((4 - ways + far) * 1024 + tie).astype(jnp.float32)
        keys[v] = [jnp.where(w, key, 0.0) for w in wants]
        here[v] = jnp.where(late, 0.0, origin)
        slot[v] = (item & 7).astype(jnp.float32)
    for t in range(STEPS_MAX):
        for v in rules:
            if t == 1:
                here[v] = here[v] + jnp.where(late, origin, 0.0)
            moves = [None] * 4
            for link in RULES[v][0]:
                value = keys[v][link] * here[v]
                best = jnp.max(value, axis=0, keepdims=True)
                win = jnp.where((value == best) & (value > 0.0), 1.0, 0.0)
                here[v] = here[v] - win
                pick = jnp.sum(win * slot[v], axis=0, keepdims=True)
                trial_ref[v, 4 * t + link : 4 * t + link + 1, :] = pick.astype(jnp.int32)
                moves[link] = win.astype(jnp.bfloat16)
            landed = dot(jnp.concatenate(moves, axis=1), hop, ((1,), (0,)))
            new = landed[:, :128]
            here[v] = here[v] + new
            slot[v] = jnp.where(new > 0.5, landed[:, 128:] + (STATS + 4.0 * t), slot[v])
            if t + 1 in STEPS:
                row = len(STEPS) * v + STEPS.index(t + 1)
                count_ref[row : row + 1, :] = jnp.sum(here[v] * homef, axis=0, keepdims=True)
    for v in rules:
        for n in range(MOST):
            mine = jnp.where(home & (rank == float(n)), slot[v] + 1.0, 0.0)
            row = 4 * STEPS_MAX + n
            trial_ref[v, row : row + 1, :] = jnp.sum(mine, axis=0, keepdims=True).astype(jnp.int32) - 1


def plan_choice(trial_ref, count_ref, out_ref):
    left = lax.broadcasted_iota(jnp.int32, (128, 128), 0) // 16
    right = lax.broadcasted_iota(jnp.int32, (128, 128), 1) // 16
    same = (left == right).astype(jnp.bfloat16)
    done = (dot(count_ref[...].astype(jnp.bfloat16), same, ((1,), (0,))) == 128.0).astype(jnp.float32)
    score = [sum(done[len(STEPS) * v + n : len(STEPS) * v + n + 1] for n in range(len(STEPS))) for v in range(len(RULES))]
    best, table = score[0], trial_ref[0]
    for v in range(1, len(RULES)):
        better = score[v] > best
        table = jnp.where(better, trial_ref[v], table)
        best = jnp.maximum(best, score[v])
    out_ref[:WHICH, :] = table
    which = len(STEPS) - jnp.min(best, keepdims=True)
    out_ref[WHICH:, :] = jnp.broadcast_to(which, (8, 128)).astype(jnp.int32)


def deliver_kernel(steps, table, packed, grad, out, pool, recv, stage, ss, rs, ready, gone):
    r, c = lax.axis_index("dp"), lax.axis_index("mp")
    z, x = c // 4, c % 4
    me = r * 16 + c
    peers = (
        (r, z * 4 + (x + 1) % 4),
        (r, z * 4 + (x + 3) % 4),
        (r, (z + 1) % 4 * 4 + x),
        (r, (z + 3) % 4 * 4 + x),
    )

    def pair(q, carry):
        def store(kind, at, value):
            pool[4 + 2 * q + kind, at : at + value.shape[0], :] = value

        make_pair(grad[:, pl.ds(pl.multiple_of(q * BLK, BLK), BLK)], store)
        return carry

    def copy(t, link, half):
        return pltpu.make_async_remote_copy(
            src_ref=stage.at[t % 2, link, HALVES[half]],
            dst_ref=recv.at[t, link, HALVES[half]],
            send_sem=ss.at[t % 2, link, half],
            recv_sem=rs.at[t, link, half],
            device_id=peers[link],
            device_id_type=MESH,
        )

    def land(t, half):
        for link in range(4):
            copy(t, link, half).wait_recv()
            pool[STATS + 4 * t + link, HALVES[half], :] = recv[t, link, HALVES[half], :]

    def push(t, half):
        for link in range(4):
            stage[t % 2, link, HALVES[half], :] = pool[table[4 * t + link, me], HALVES[half], :]
            copy(t, link, half).start()

    def settle(t, half):
        for link in range(4):
            copy(t, link, half).wait_send()

    barrier = pltpu.get_barrier_semaphore()
    for dev in peers:
        pl.semaphore_signal(barrier, inc=1, device_id=dev, device_id_type=MESH)
    pool[:4] = packed[...]
    pl.semaphore_wait(barrier, 4)
    push(0, 0)
    push(0, 1)
    lax.fori_loop(0, 2, pair, 0)
    for half in (0, 1):
        land(0, half)
        push(1, half)

    def step(t, carry):
        for half in (0, 1):
            land(t - 1, half)
            settle(t - 2, half)
            push(t, half)
        return carry

    lax.fori_loop(2, steps, step, 0)
    for half in (0, 1):
        land(steps - 1, half)
    for t in (steps - 2, steps - 1):
        for half in (0, 1):
            settle(t, half)
    for n in range(MOST):
        at = table[4 * STEPS_MAX + n, me]
        block = pool[jnp.maximum(at, 0)]
        keep = (at >= 0).astype(jnp.bfloat16)
        ready[n] = block * keep
        pltpu.make_async_copy(ready.at[n], out.at[n], gone.at[n]).start()
    for n in range(MOST):
        pltpu.make_async_copy(ready.at[n], out.at[n], gone.at[n]).wait()


HALVES = (pl.ds(0, 528), pl.ds(528, 512))


def deliver(steps, table, packed, grad):
    return pl.pallas_call(
        functools.partial(deliver_kernel, steps),
        out_shape=jax.ShapeDtypeStruct((MOST, ROWS, 128), jnp.bfloat16),
        in_specs=[pl.BlockSpec(memory_space=pltpu.SMEM)] + [pl.BlockSpec(memory_space=pltpu.VMEM)] * 2,
        out_specs=pl.BlockSpec(memory_space=pl.ANY),
        scratch_shapes=[
            pltpu.VMEM((STATS + 4 * steps, ROWS, 128), jnp.bfloat16),
            pltpu.VMEM((steps, 4, ROWS, 128), jnp.bfloat16),
            pltpu.VMEM((2, 4, ROWS, 128), jnp.bfloat16),
            pltpu.SemaphoreType.DMA((2, 4, 2)),
            pltpu.SemaphoreType.DMA((steps, 4, 2)),
            pltpu.VMEM((MOST, ROWS, 128), jnp.bfloat16),
            pltpu.SemaphoreType.DMA((MOST,)),
        ],
        compiler_params=pltpu.CompilerParams(
            collective_id=steps, has_side_effects=True, vmem_limit_bytes=LIMIT
        ),
        name="deliver",
    )(table, packed, grad)


def deliver_any(owners, packed):
    myself = lax.axis_index("mp")
    lists = lax.all_gather(owners, "mp", axis=1, tiled=True)[0]
    mine = lists[myself]
    count = lists.shape[0]
    match = (mine[None, :] == jnp.arange(count, dtype=jnp.int32)[:, None]).astype(jnp.int32)
    rank = jnp.cumsum(match, axis=1) - match
    select = (match[:, None, :] > 0) & (rank[:, None, :] == jnp.arange(CAP, dtype=jnp.int32)[None, :, None])
    index = jnp.sum(select.astype(jnp.int32) * jnp.arange(STATS, dtype=jnp.int32), axis=2)
    outgoing = packed[index.reshape(-1)].reshape(count, CAP, ROWS, 128)
    received = lax.all_to_all(outgoing, "mp", split_axis=0, concat_axis=0, tiled=True)
    counts = jnp.sum((lists == myself).astype(jnp.int32), axis=1)
    valid = (jnp.arange(CAP, dtype=jnp.int32)[None, :] < counts[:, None]).reshape(-1).astype(jnp.int32)
    before = jnp.cumsum(valid) - valid
    chosen = (valid[None, :] > 0) & (before[None, :] == jnp.arange(MOST, dtype=jnp.int32)[:, None])
    index = jnp.sum(chosen.astype(jnp.int32) * jnp.arange(count * CAP, dtype=jnp.int32), axis=1)
    picked = received.reshape(count * CAP, ROWS, 128)[index]
    return jnp.where(jnp.any(chosen, axis=1)[:, None, None], picked, jnp.zeros_like(picked))


def unpack_kernel(src, dst, packed, whole, came, left):
    rows = lax.broadcasted_iota(jnp.int32, (128, 128), 0)
    cols = lax.broadcasted_iota(jnp.int32, (128, 128), 1)

    def fetch(m):
        return pltpu.make_async_copy(src.at[m], packed.at[m], came.at[m])

    def write(m):
        return pltpu.make_async_copy(whole.at[m], dst.at[m], left.at[m])

    def place(m, i, j, value):
        whole[m, 128 * i : 128 * i + 128, 128 * j : 128 * j + 128] = value

    for m in range(MOST):
        fetch(m).start()

    def one(m, carry):
        fetch(m).wait()
        flipped = packed[m, :1024, :].T
        for n, (i, j) in enumerate(OFF):
            place(m, i, j, packed[m, 128 * n : 128 * n + 128, :])
            place(m, j, i, flipped[:, 128 * n : 128 * n + 128])
        spare = packed[m, 1024:, :].astype(jnp.float32)
        for n in (0, 1):
            both = packed[m, 128 * (6 + n) : 128 * (7 + n), :].astype(jnp.float32)
            other = flipped[:, 128 * (6 + n) : 128 * (7 + n)].astype(jnp.float32)
            first = jnp.where(rows <= cols, both, other)
            second = jnp.where(rows > cols, both, other)
            second = jnp.where(rows == cols, spare[n : n + 1, :], second)
            place(m, 2 * n, 2 * n, first.astype(jnp.bfloat16))
            place(m, 2 * n + 1, 2 * n + 1, second.astype(jnp.bfloat16))
        write(m).start()
        return carry

    lax.fori_loop(0, MOST, one, 0)
    for m in range(MOST):
        write(m).wait()


def unpack(packed):
    return pl.pallas_call(
        unpack_kernel,
        out_shape=jax.ShapeDtypeStruct((MOST, BLK, BLK), jnp.bfloat16),
        in_specs=[pl.BlockSpec(memory_space=pl.ANY)],
        out_specs=pl.BlockSpec(memory_space=pl.ANY),
        scratch_shapes=[
            pltpu.VMEM((MOST, ROWS, 128), jnp.bfloat16),
            pltpu.VMEM((MOST, BLK, BLK), jnp.bfloat16),
            pltpu.SemaphoreType.DMA((MOST,)),
            pltpu.SemaphoreType.DMA((MOST,)),
        ],
        compiler_params=pltpu.CompilerParams(vmem_limit_bytes=LIMIT),
        name="unpack",
    )(packed)


def body(hidden_acts, out_grad, owners):
    packed, grad, table = gather(hidden_acts, out_grad, owners)
    ways = [functools.partial(deliver, steps, table, packed, grad) for steps in STEPS]
    ways.append(lambda: deliver_any(owners, jnp.concatenate([packed, roots(grad)])))
    arrived = lax.switch(table[WHICH, 0], ways)
    return unpack(arrived)[None, None]


def solution(mesh):
    placed = (P("dp", "mp"), P("dp", None), P("dp", "mp", None))
    return jax.shard_map(
        body, mesh=mesh, in_specs=placed, out_specs=P("dp", "mp", None, None, None), check_vma=False
    )
```
